32 devices in a mesh: narrow: 4 (over x, core), wide: 8 (over z, y).
Axes of the slice: x: 2, y: 2, z: 4, core: 2. Of those that a mesh axis runs over, the one named last changes fastest.
Arguments:
- tokens: bfloat16 [12288, 512], P(('narrow', 'wide')), may hold values from -6 to 6
- gain_one: float32 [512], replicated, may hold values from 0.5 to 1.5
- shift_one: float32 [512], replicated, may hold values from -1.25 to 1.25
- query_w: bfloat16 [512, 512], replicated, may hold values from -0.25 to 0.25
- key_w: bfloat16 [512, 512], replicated, may hold values from -0.25 to 0.25
- value_w: bfloat16 [512, 512], replicated, may hold values from -0.25 to 0.25
- out_w: bfloat16 [512, 512], replicated, may hold values from -1.5 to 1.5
- gain_two: float32 [512], replicated, may hold values from 0.5 to 1.5
- shift_two: float32 [512], replicated, may hold values from -1.25 to 1.25
- router_w: bfloat16 [512, 8], replicated, may hold values from -0.1875 to 0.1875
- up_w: bfloat16 [8, 512, 2048], P('wide'), may hold values from -0.25 to 0.25
- up_bias: float32 [8, 2048], P('wide'), may hold values from -0.625 to 0.625
- down_w: bfloat16 [8, 2048, 512], P('wide'), may hold values from -4 to 4
- down_bias: float32 [8, 512], P('wide'), may hold values from -12 to 12
- picks: int32 [12288, 2], P(('narrow', 'wide')), may hold values from 0 to 7, all different within a row
- ranks: int32 [12288, 2], P(('narrow', 'wide')), may hold values from 0 to 767, as said below
- out_grad: bfloat16 [12288, 512], P(('narrow', 'wide')), may hold values from -6 to 6
Outputs:
- block_out: bfloat16 [12288, 512], P(('narrow', 'wide'))
- tokens_grad: bfloat16 [12288, 512], P(('narrow', 'wide'))
- gain_one_grad: float32 [512], replicated
- shift_one_grad: float32 [512], replicated
- query_grad: float32 [512, 512], replicated
- key_grad: float32 [512, 512], replicated
- value_grad: float32 [512, 512], replicated
- out_w_grad: float32 [512, 512], replicated
- gain_two_grad: float32 [512], replicated
- shift_two_grad: float32 [512], replicated
- router_grad: float32 [512, 8], replicated
- up_grad: float32 [8, 512, 2048], P('wide')
- up_bias_grad: float32 [8, 2048], P('wide')
- down_grad: float32 [8, 2048, 512], P('wide')
- down_bias_grad: float32 [8, 512], P('wide')
- expert_counts: int32 [8, 2], replicated
The draws below stay inside these ranges and needn't reach their ends.
Inputs may be any that keep to these rules, and one draw needn't show every extreme that they name: `picks`: the two experts of a row differ. `ranks`: within the 384 tokens of each device block, the 768 entries are all different; a smaller rank takes its slot first.
All inputs are finite; a program needn't handle non-finite values.
Results may differ from the reference program's by a relative error of at most 0.017.
Values may be sent and summed in bfloat16 or wider, within the bound.
No kernel may reach another device: no remote copies, remote signals or barrier semaphores. Data moves between devices by JAX's collectives and lax.ppermute only.
A program may use at most 128 MiB of HBM per device.

```python
import math
import jax
import jax.numpy as jnp
from jax import lax

D = 512
HEADS = 8
HEAD_DIM = 64
FF = 2048
PATCHES = 48
TOK_DEV = 384
TOKENS = 12288
EXPERTS = 8
CAP = 104


def draw_ranks(key, part):
    key = jax.random.fold_in(key, 11)
    blocks = TOKENS // TOK_DEV
    block_keys = jax.random.split(key, blocks)
    orders = jax.vmap(lambda item: jax.random.permutation(item, 2 * TOK_DEV))(block_keys)
    return orders.reshape(TOKENS, 2).astype(jnp.int32)


def level_of(rng, shape, cuts, low, high):
    level, own = 1.0, jax.random.fold_in(rng, 6)
    for axis_at, blocks in cuts:
        draws = jnp.exp(jax.random.uniform(jax.random.fold_in(own, axis_at), (blocks,), jnp.float32, low / len(cuts), high / len(cuts)))
        level = level * jnp.repeat(draws, shape[axis_at] // blocks).reshape([-1 if axis == axis_at else 1 for axis in range(len(shape))])
    return level


def choose_distinct(stream_key, rows, number_of, top, lift):
    ranking = jax.random.permutation(jax.random.fold_in(stream_key, 1), number_of)
    pull = ranking
    for power in range(3):
        pull = pull * pull // number_of
    pull = pull * lift // number_of
    lots = jax.random.randint(jax.random.fold_in(stream_key, 2), (rows, number_of), 0, 4096) + pull
    fixed_rows = jax.random.permutation(jax.random.fold_in(stream_key, 3), rows)[jnp.arange(number_of) % rows]
    lots = jnp.where(jnp.arange(rows)[:, None] == fixed_rows[None, :], 1 << 14, lots)
    merit = lots * number_of + jnp.arange(number_of)
    return lax.top_k(merit.astype(jnp.int32), top)[1].astype(jnp.int32)


def centred(rng, shape, width, bound, cuts=(), held_as=jnp.bfloat16):
    entries = jax.random.normal(rng, shape, jnp.float32) * width
    if len(cuts) > 0:
        entries = level_of(rng, shape, cuts, -0.22, 0.18) * entries
    return jnp.clip(entries, min=-bound, max=bound).astype(held_as)


def setup_inputs(seed: int = 0) -> dict:
    splits = jax.random.split(jax.random.key(seed), 18)
    return {
        "tokens": centred(splits[0], (TOKENS, D), 1.0, 6.0, ((0, 32),)),
        "gain_one": jnp.clip(1.0 + 0.1 * jax.random.normal(splits[1], (D,), jnp.float32), 0.5, 1.5),
        "shift_one": centred(splits[2], (D,), 0.2, 1.25, (), jnp.float32),
        "query_w": centred(splits[3], (D, D), D ** -0.5, 0.25),
        "key_w": centred(splits[4], (D, D), D ** -0.5, 0.25),
        "value_w": centred(splits[5], (D, D), D ** -0.5, 0.25),
        "out_w": centred(splits[6], (D, D), (D // 32) ** -0.5, 1.5),
        "gain_two": jnp.clip(1.0 + 0.1 * jax.random.normal(splits[7], (D,), jnp.float32), 0.5, 1.5),
        "shift_two": centred(splits[8], (D,), 0.2, 1.25, (), jnp.float32),
        "router_w": centred(splits[9], (D, EXPERTS), (2 * D) ** -0.5, 0.1875),
        "up_w": centred(splits[10], (EXPERTS, D, FF), D ** -0.5, 0.25, ((0, 8),)),
        "up_bias": centred(splits[11], (EXPERTS, FF), 0.1, 0.625, ((0, 8),), jnp.float32),
        "down_w": centred(splits[12], (EXPERTS, FF, D), 2 ** -0.5, 4.0, ((0, 8),)),
        "down_bias": centred(splits[13], (EXPERTS, D), 2.0, 12.0, ((0, 8),), jnp.float32),
        "picks": choose_distinct(splits[14], TOKENS, EXPERTS, 2, 2048),
        "ranks": draw_ranks(jax.random.fold_in(splits[17], 71), 0),
        "out_grad": centred(splits[16], (TOKENS, D), 1.0, 6.0, ((0, 32),)),
    }


@jax.custom_vjp
def low(v):
    return lax.optimization_barrier(v.astype(jnp.bfloat16)).astype(jnp.float32)

@jax.custom_vjp
def low_back(v):
    return v

def low_keep(v):
    return (low(v), None)

def low_pass(kept, grad):
    return (grad,)

def back_keep(v):
    return (v, None)

def back_low(kept, grad):
    return (low(grad),)
low.defvjp(low_keep, low_pass)
low_back.defvjp(back_keep, back_low)
EPSILON = 1e-06
highest = lax.Precision.HIGHEST

def layer_norm(values, gain, shift):
    center = values - lax.optimization_barrier(jnp.mean(values, axis=-1, keepdims=True))
    spread = lax.optimization_barrier(jnp.mean(center * center, axis=-1, keepdims=True))
    return center * lax.rsqrt(spread + EPSILON) * gain + shift

def softmax_rows(scores):
    largest = lax.optimization_barrier(jnp.max(scores, axis=-1, keepdims=True))
    powers = jnp.exp(scores - largest)
    return powers / lax.optimization_barrier(jnp.sum(powers, axis=-1, keepdims=True))

def slot_tables(picks, ranks):
    expert_ids = picks.reshape(-1)
    order = ranks.reshape(-1)
    same = expert_ids[:, None] == expert_ids[None, :]
    earlier = order[None, :] < order[:, None]
    slots = lax.optimization_barrier(jnp.sum((same & earlier).astype(jnp.int32), axis=1, dtype=jnp.int32))
    kept = slots < CAP
    target = jnp.where(kept, expert_ids * CAP + slots, EXPERTS * CAP).astype(jnp.int32)
    return (target, kept)

def block_forward(inputs, picks, ranks, params):
    gain_one, shift_one, query_w, key_w, value_w, out_w, gain_two, shift_two, router_w, up_w, up_bias, down_w, down_bias = params
    count = inputs.shape[0]
    images = count // PATCHES
    scale = 1.0 / math.sqrt(HEAD_DIM)
    normed = low(layer_norm(inputs, gain_one, shift_one))

    def project(weight):
        made = low(low_back(jnp.dot(normed, weight, precision=highest)))
        return made.reshape(images, PATCHES, HEADS, HEAD_DIM)
    queries = project(query_w)
    keys = project(key_w)
    values = project(value_w)
    scores = low_back(jnp.einsum('iqhd,ikhd->ihqk', queries, keys, precision=highest) * scale)
    weights = low(softmax_rows(scores))
    mixed = jnp.einsum('ihqk,ikhd->iqhd', weights, values, precision=highest).reshape(count, D)
    mixed = low(low_back(mixed))
    branch = low_back(jnp.dot(mixed, out_w, precision=highest))
    resid = inputs + branch
    second = low(layer_norm(resid, gain_two, shift_two))
    logits = low_back(jnp.dot(second, router_w, precision=highest))
    gates = softmax_rows(logits)
    target, kept = slot_tables(picks, ranks)
    pair_token = jnp.arange(2 * count, dtype=jnp.int32) // 2
    table = jnp.full((EXPERTS * CAP + 1,), count, jnp.int32).at[target].set(pair_token)[:-1]
    padded = jnp.concatenate([second, jnp.zeros((1, D), jnp.float32)], axis=0)
    rows_in = low_back(padded[table].reshape(EXPERTS, CAP, D))
    inner = jnp.einsum('ecd,edf->ecf', rows_in, up_w, precision=highest) + up_bias[:, None, :]
    inner = low_back(inner)
    hidden = low(jax.nn.gelu(inner))
    produced = jnp.einsum('ecf,efd->ecd', hidden, down_w, precision=highest) + down_bias[:, None, :]
    produced = low(low_back(produced))
    flat = jnp.concatenate([produced.reshape(EXPERTS * CAP, D), jnp.zeros((1, D), jnp.float32)], axis=0)
    pair_out = flat[target].reshape(count, 2, D)
    pair_gate = jnp.take_along_axis(gates, picks, axis=1)
    return resid + lax.optimization_barrier(jnp.sum(pair_gate[:, :, None] * pair_out, axis=1))

def reference(tokens, gain_one, shift_one, query_w, key_w, value_w, out_w, gain_two, shift_two, router_w, up_w, up_bias, down_w, down_bias, picks, ranks, out_grad):
    blocks = TOKENS // TOK_DEV
    params = tuple((item.astype(jnp.float32) for item in (gain_one, shift_one, query_w, key_w, value_w, out_w, gain_two, shift_two, router_w, up_w, up_bias, down_w, down_bias)))
    inputs = tokens.astype(jnp.float32).reshape(blocks, TOK_DEV, D)
    pick_blocks = picks.reshape(blocks, TOK_DEV, 2)
    rank_blocks = ranks.reshape(blocks, TOK_DEV, 2)

    def forward(inputs, params):

        def one_block(items):
            return block_forward(items[0], items[1], items[2], params)
        return lax.map(jax.checkpoint(one_block), (inputs, pick_blocks, rank_blocks))
    outputs, pullback = jax.vjp(forward, inputs, params)
    input_grad, param_grads = pullback(out_grad.astype(jnp.float32).reshape(blocks, TOK_DEV, D))

    def tally(items):
        target, kept = slot_tables(items[0], items[1])
        expert_ids = items[0].reshape(-1)
        columns = jnp.arange(EXPERTS, dtype=jnp.int32)
        match = expert_ids[:, None] == columns[None, :]
        kept_count = lax.optimization_barrier(jnp.sum((match & kept[:, None]).astype(jnp.int32), axis=0, dtype=jnp.int32))
        dropped_count = lax.optimization_barrier(jnp.sum((match & ~kept[:, None]).astype(jnp.int32), axis=0, dtype=jnp.int32))
        return jnp.stack([kept_count, dropped_count], axis=1)
    counts = lax.optimization_barrier(jnp.sum(lax.map(tally, (pick_blocks, rank_blocks)), axis=0, dtype=jnp.int32))
    block_out = outputs.reshape(TOKENS, D).astype(jnp.bfloat16)
    tokens_grad = input_grad.reshape(TOKENS, D).astype(jnp.bfloat16)
    return (block_out, tokens_grad, param_grads[0], param_grads[1], param_grads[2], param_grads[3], param_grads[4], param_grads[5], param_grads[6], param_grads[7], param_grads[8], param_grads[9], param_grads[10], param_grads[11], param_grads[12], counts)
```

```python
import functools
import math

import jax
import jax.numpy as jnp
from jax import lax
from jax.experimental import pallas as pl
from jax.experimental.pallas import tpu as pltpu
from jax.sharding import PartitionSpec as P

HEADS = 8
PATCHES = 48
EPSILON = 1e-06
LANES = 128
MIB = 1 << 20
F32 = jnp.float32
BF16 = jnp.bfloat16

VMEM = functools.partial(pl.BlockSpec, memory_space=pltpu.VMEM)
SMEM = functools.partial(pl.BlockSpec, memory_space=pltpu.SMEM)


def shape(dims, dtype):
    return jax.ShapeDtypeStruct(dims, dtype)


def dot(a, b):
    return jnp.dot(a, b, preferred_element_type=F32)


def dot_nt(a, b):
    return lax.dot_general(a, b, (((1,), (1,)), ((), ())), preferred_element_type=F32)


def dot_tn(a, b):
    return lax.dot_general(a, b, (((0,), (0,)), ((), ())), preferred_element_type=F32)


def params(mib):
    return pltpu.CompilerParams(vmem_limit_bytes=mib * MIB)


def cost(us):
    return pl.CostEstimate(flops=int(us * 1.0e9), bytes_accessed=int(us * 1.0e6), transcendentals=0)


def norm_rows(values):
    center = values - jnp.mean(values, axis=-1, keepdims=True)
    spread = jnp.mean(center * center, axis=-1, keepdims=True)
    rate = lax.rsqrt(spread + EPSILON)
    return center * rate, rate


def norm_back(hat, rate, gain, grad):
    scaled = grad * gain
    mean_one = jnp.mean(scaled, axis=-1, keepdims=True)
    mean_two = jnp.mean(scaled * hat, axis=-1, keepdims=True)
    return rate * (scaled - mean_one - hat * mean_two)


def route_kernel(capacity, experts, picks_ref, ranks_ref, grad_ref, spread_ref, target_ref, count_ref, sent_ref):
    count = picks_ref.shape[1]
    slots_all = experts * capacity
    span = 1 << (2 * count - 1).bit_length()
    picks = picks_ref[...].astype(F32)
    base = picks * span
    order = base + ranks_ref[...].astype(F32)
    padded = jnp.concatenate([picks, order, jnp.zeros((4, count), F32)], axis=0)
    turned = jnp.transpose(padded)
    targets = []
    for j in range(2):
        row = order[j : j + 1]
        floor = base[j : j + 1]
        slot = jnp.zeros((1, count), F32)
        for other in range(2):
            column = turned[:, 2 + other : 3 + other]
            ahead = (column < row) & (column >= floor)
            slot = slot + jnp.sum(jnp.where(ahead, 1.0, 0.0), axis=0, keepdims=True)
        kept = slot < capacity
        targets.append(jnp.where(kept, picks[j : j + 1] * capacity + slot, float(slots_all)))
    target_turned = jnp.transpose(jnp.concatenate(targets + [jnp.zeros((6, count), F32)], axis=0))
    target_ref[...] = target_turned
    lane = lax.broadcasted_iota(jnp.int32, (count, LANES), 1).astype(F32)
    kept_count = jnp.zeros((1, LANES), F32)
    all_count = jnp.zeros((1, LANES), F32)
    for j in range(2):
        named = jnp.where(turned[:, j : j + 1] == lane, 1.0, 0.0)
        live = jnp.where(target_turned[:, j : j + 1] < slots_all, 1.0, 0.0)
        all_count = all_count + jnp.sum(named, axis=0, keepdims=True)
        kept_count = kept_count + jnp.sum(named * live, axis=0, keepdims=True)
    count_ref[...] = jnp.concatenate([kept_count, all_count - kept_count, jnp.zeros((6, LANES), F32)], axis=0)
    step = 64
    for start in range(0, slots_all, step):
        index = lax.broadcasted_iota(jnp.int32, (step, count), 0).astype(F32) + float(start)
        hit = (index == targets[0]) | (index == targets[1])
        spread_ref[start : start + step, :] = jnp.where(hit, 1.0, 0.0).astype(BF16)
    sent_ref[...] = dot(spread_ref[...], grad_ref[...]).astype(BF16)


def head_masks(width):
    lane = lax.broadcasted_iota(jnp.int32, (1, width), 1)
    return lane < width // 2


def stack_heads(pair, low):
    zero = jnp.zeros_like(pair)
    return jnp.concatenate([jnp.where(low, pair, zero), jnp.where(low, zero, pair)], axis=0)


def attention_kernel(
    tokens_ref,
    gain_one_ref,
    shift_one_ref,
    query_w_ref,
    key_w_ref,
    value_w_ref,
    out_w_ref,
    gain_two_ref,
    shift_two_ref,
    spread_ref,
    resid_ref,
    normed_ref,
    query_ref,
    key_ref,
    value_ref,
    weight_ref,
    mixed_ref,
    sent_ref,
):
    count, width = tokens_ref.shape
    inputs = tokens_ref[...].astype(F32)
    hat, _ = norm_rows(inputs)
    normed_ref[...] = (hat * gain_one_ref[...] + shift_one_ref[...]).astype(BF16)
    normed = normed_ref[...]
    query_ref[...] = (dot(normed, query_w_ref[...]).astype(BF16).astype(F32) * (1.0 / math.sqrt(width // HEADS))).astype(BF16)
    key_ref[...] = dot(normed, key_w_ref[...]).astype(BF16)
    value_ref[...] = dot(normed, value_w_ref[...]).astype(BF16)
    pairs = HEADS // 2
    wide = width // pairs
    block = 2 * PATCHES
    low = head_masks(wide)
    row_image = (lax.broadcasted_iota(jnp.int32, (2 * block, block), 0) % block) // PATCHES
    column_image = lax.broadcasted_iota(jnp.int32, (2 * block, block), 1) // PATCHES
    bias = jnp.where(row_image == column_image, 0.0, -1e30)
    for item in range(count // block):
        rows = slice(item * block, (item + 1) * block)
        for pair in range(pairs):
            lanes = slice(pair * wide, (pair + 1) * wide)
            stacked = stack_heads(query_ref[rows, lanes], low)
            scores = dot_nt(stacked, key_ref[rows, lanes]) + bias
            powers = jnp.exp(scores - jnp.max(scores, axis=-1, keepdims=True))
            weights = (powers / jnp.sum(powers, axis=-1, keepdims=True)).astype(BF16)
            weight_ref[item, pair] = weights
            mixed = dot(weights, value_ref[rows, lanes])
            mixed_ref[rows, lanes] = jnp.where(low, mixed[:block], mixed[block:]).astype(BF16)
    resid = inputs + dot(mixed_ref[...], out_w_ref[...])
    resid_ref[...] = resid
    hat, _ = norm_rows(resid)
    second = (hat * gain_two_ref[...] + shift_two_ref[...]).astype(BF16)
    sent_ref[...] = dot(spread_ref[...], second).astype(BF16)


def expert_kernel(
    experts,
    me_ref,
    rows_ref,
    grad_ref,
    up_ref,
    up_bias_ref,
    down_ref,
    down_bias_ref,
    router_ref,
    hidden_ref,
    inner_grad_ref,
    rows_grad_ref,
    gated_ref,
    gate_ref,
    router_grad_ref,
    inner_s,
    back_s,
    total_s,
    pair_s,
    gates_s,
):
    step = pl.program_id(0)
    total, width = rows_ref.shape
    tile = up_ref.shape[1]

    @pl.when(step == 0)
    def _():
        lane = lax.broadcasted_iota(jnp.int32, (total, LANES), 1)
        logits = dot_nt(rows_ref[...], router_ref[...])
        logits = jnp.where(lane < experts, logits, -1e30)
        powers = jnp.exp(logits - jnp.max(logits, axis=-1, keepdims=True))
        gates = powers / jnp.sum(powers, axis=-1, keepdims=True)
        gates_s[...] = gates
        gate = jnp.sum(jnp.where(lane == me_ref[0], gates, 0.0), axis=-1, keepdims=True)
        gate_ref[...] = jnp.broadcast_to(gate, (total, LANES))
        gated_ref[...] = (gate * grad_ref[...].astype(F32)).astype(BF16)
        total_s[...] = jnp.zeros_like(total_s)
        pair_s[...] = jnp.zeros_like(pair_s)

    inner_s[...] = dot(rows_ref[...], up_ref[...])
    back_s[...] = dot_nt(grad_ref[...], down_ref[...])
    chunk = 16
    root = math.sqrt(2.0 / math.pi)

    def some_rows(index, carry):
        at = pl.ds(pl.multiple_of(index * chunk, chunk), chunk)
        inner = inner_s[at, :] + up_bias_ref[...]
        back = back_s[at, :]
        square = inner * inner
        half = 0.5 + 0.5 * jnp.tanh(inner * (root + (root * 0.044715) * square))
        hidden = inner * half
        slope = half + (hidden - hidden * half) * (2.0 * root + (6.0 * root * 0.044715) * square)
        gate = gate_ref[at, :]
        gate = jnp.concatenate([gate] * (tile // LANES), axis=1)
        hidden_ref[at, :] = hidden.astype(BF16)
        inner_grad_ref[at, :] = (back * gate * slope).astype(BF16)
        product = hidden * back
        part = product[:, :LANES]
        for other in range(1, tile // LANES):
            part = part + product[:, other * LANES : (other + 1) * LANES]
        pair_s[at, :] = pair_s[at, :] + part
        return carry

    lax.fori_loop(0, total // chunk, some_rows, 0, unroll=2)
    total_s[...] += dot_nt(inner_grad_ref[...], up_ref[...])

    @pl.when(step == pl.num_programs(0) - 1)
    def _():
        lane = lax.broadcasted_iota(jnp.int32, (total, LANES), 1)
        pair_grad = jnp.sum(pair_s[...], axis=-1, keepdims=True)
        pair_grad = pair_grad + jnp.sum(grad_ref[...].astype(F32) * down_bias_ref[...], axis=-1, keepdims=True)
        own = jnp.where(lane == me_ref[0], 1.0, 0.0)
        logit_grad = (gates_s[...] * (own - gate_ref[...]) * pair_grad).astype(BF16)
        rows_grad_ref[...] = (total_s[...] + dot(logit_grad, router_ref[...])).astype(BF16)
        router_grad_ref[...] = dot_tn(logit_grad, rows_ref[...])


def weight_kernel(core_ref, rows_ref, gated_ref, hidden_ref, inner_grad_ref, keep_ref, send_ref):
    step = pl.program_id(0)
    width = rows_ref.shape[1]
    half = width // 2
    first = core_ref[0] == 0
    up = dot_tn(rows_ref[...], inner_grad_ref[...]).astype(BF16)
    keep_ref[0, :half, :] = jnp.where(first, up[:half], up[half:])
    send_ref[0, :half, :] = jnp.where(first, up[half:], up[:half])
    down = dot_tn(hidden_ref[...], gated_ref[...]).astype(BF16)
    keep_ref[0, half : 2 * half, :] = jnp.where(first, down[:half], down[half:])
    send_ref[0, half : 2 * half, :] = jnp.where(first, down[half:], down[:half])
    up_bias = jnp.sum(inner_grad_ref[...].astype(F32), axis=0, keepdims=True)
    down_bias = jnp.sum(gated_ref[...].astype(F32), axis=0, keepdims=True)
    small = jnp.concatenate([up_bias, down_bias, jnp.zeros((14, width), F32)], axis=0).astype(BF16)
    keep_ref[0, 2 * half :, :] = small
    send_ref[0, 2 * half :, :] = small


def produce_kernel(hidden_ref, down_ref, down_bias_ref, gate_ref, out_ref, total_s):
    step = pl.program_id(0)

    @pl.when(step == 0)
    def _():
        total_s[...] = jnp.zeros_like(total_s)

    total_s[...] += dot(hidden_ref[...], down_ref[...])

    @pl.when(step == pl.num_programs(0) - 1)
    def _():
        gate = gate_ref[...]
        gate = jnp.concatenate([gate] * (out_ref.shape[1] // LANES), axis=1)
        out_ref[...] = ((total_s[...] + down_bias_ref[...]) * gate).astype(BF16)


def add_kernel(one_ref, two_ref, out_ref):
    out_ref[...] = (one_ref[...].astype(F32) + two_ref[...].astype(F32)).astype(BF16)


def finish_experts_kernel(core_ref, own_ref, other_ref, up_ref, up_bias_ref, down_ref, down_bias_ref):
    half = up_ref.shape[0] // 2
    first = core_ref[0] == 0
    own = own_ref[0].astype(F32)
    other = other_ref[0].astype(F32)
    up_ref[:half, :] = jnp.where(first, own[:half], other[:half])
    up_ref[half:, :] = jnp.where(first, other[:half], own[:half])
    down_ref[:half, :] = jnp.where(first, own[half : 2 * half], other[half : 2 * half])
    down_ref[half:, :] = jnp.where(first, other[half : 2 * half], own[half : 2 * half])
    up_bias_ref[...] = own[2 * half : 2 * half + 1]
    down_bias_ref[...] = own[2 * half + 1 : 2 * half + 2]


def one_hot_rows(target_ref, slots_all):
    count = target_ref.shape[0]
    lane = lax.broadcasted_iota(jnp.int32, (64, slots_all), 1).astype(F32)
    pieces = []
    for start in range(0, count, 64):
        one = target_ref[start : start + 64, 0:1]
        two = target_ref[start : start + 64, 1:2]
        pieces.append(jnp.where((lane == one) | (lane == two), 1.0, 0.0).astype(BF16))
    return jnp.concatenate(pieces, axis=0)


def combine_kernel(target_ref, produced_ref, resid_ref, out_ref):
    picked = one_hot_rows(target_ref, produced_ref.shape[0])
    out_ref[...] = (resid_ref[...] + dot(picked, produced_ref[...])).astype(BF16)


def backward_kernel(
    experts,
    core_ref,
    target_ref,
    back_ref,
    resid_ref,
    grad_ref,
    gain_two_ref,
    tokens_ref,
    gain_one_ref,
    query_w_ref,
    key_w_ref,
    value_w_ref,
    out_w_ref,
    normed_ref,
    query_ref,
    key_ref,
    value_ref,
    weight_ref,
    mixed_ref,
    count_ref,
    router_grad_ref,
    keep_ref,
    send_ref,
    tokens_grad_ref,
    queries_s,
    keys_s,
    values_s,
    mixed_grad_s,
    resid_grad_s,
):
    count, width = tokens_ref.shape
    picked = one_hot_rows(target_ref, back_ref.shape[0])
    second_grad = dot(picked, back_ref[...])
    hat, rate = norm_rows(resid_ref[...])
    gain_two_grad = jnp.sum(second_grad * hat, axis=0, keepdims=True)
    shift_two_grad = jnp.sum(second_grad, axis=0, keepdims=True)
    resid_grad_s[...] = grad_ref[...].astype(F32) + norm_back(hat, rate, gain_two_ref[...], second_grad)
    branch = resid_grad_s[...].astype(BF16)
    half = width // 2
    first = core_ref[0] == 0

    def put(at, value):
        value = value.astype(BF16)
        keep_ref[at * half : (at + 1) * half, :] = jnp.where(first, value[:half], value[half:])
        send_ref[at * half : (at + 1) * half, :] = jnp.where(first, value[half:], value[:half])

    put(3, dot_tn(mixed_ref[...], branch))
    mixed_grad_s[...] = dot_nt(branch, out_w_ref[...]).astype(BF16)
    pairs = HEADS // 2
    wide = width // pairs
    block = 2 * PATCHES
    scale = 1.0 / math.sqrt(width // HEADS)
    low = head_masks(wide)
    for item in range(count // block):
        rows = slice(item * block, (item + 1) * block)
        for pair in range(pairs):
            lanes = slice(pair * wide, (pair + 1) * wide)
            mixed_stack = stack_heads(mixed_grad_s[rows, lanes], low)
            query_stack = stack_heads(query_ref[rows, lanes], low)
            weights = weight_ref[item, pair]
            weight_grad = dot_nt(mixed_stack, value_ref[rows, lanes])
            product = weights.astype(F32) * weight_grad
            score_grad = product - weights.astype(F32) * jnp.sum(product, axis=-1, keepdims=True)
            score_grad = score_grad.astype(BF16)
            values_s[rows, lanes] = dot_tn(weights, mixed_stack).astype(BF16)
            keys_s[rows, lanes] = dot_tn(score_grad, query_stack).astype(BF16)
            made = dot(score_grad, key_ref[rows, lanes]) * scale
            queries_s[rows, lanes] = jnp.where(low, made[:block], made[block:]).astype(BF16)
    normed = normed_ref[...]
    put(0, dot_tn(normed, queries_s[...]))
    put(1, dot_tn(normed, keys_s[...]))
    put(2, dot_tn(normed, values_s[...]))
    normed_grad = (
        dot_nt(queries_s[...], query_w_ref[...])
        + dot_nt(keys_s[...], key_w_ref[...])
        + dot_nt(values_s[...], value_w_ref[...])
    )
    hat, rate = norm_rows(tokens_ref[...].astype(F32))
    gain_one_grad = jnp.sum(normed_grad * hat, axis=0, keepdims=True)
    shift_one_grad = jnp.sum(normed_grad, axis=0, keepdims=True)
    tokens_grad_ref[...] = (resid_grad_s[...] + norm_back(hat, rate, gain_one_ref[...], normed_grad)).astype(BF16)
    digits = []
    for kind in range(2):
        value = count_ref[kind : kind + 1, :]
        high = jnp.floor(value * (1.0 / 128.0))
        digits.append(jnp.concatenate([value - 128.0 * high, high] + [jnp.zeros_like(value)] * (width // LANES - 2), axis=1))
    extra = keep_ref.shape[0] - 4 * half
    small = [gain_one_grad, shift_one_grad, gain_two_grad, shift_two_grad] + digits + [router_grad_ref[:experts, :]]
    small = jnp.concatenate(small + [jnp.zeros((extra - 6 - experts, width), F32)], axis=0).astype(BF16)
    keep_ref[4 * half :, :] = small
    send_ref[4 * half :, :] = small


def carry_digits(total):
    row = lax.broadcasted_iota(jnp.int32, (total.shape[0], LANES), 0)
    one, two, three = (total[:, at * LANES : (at + 1) * LANES] for at in range(3))
    over = jnp.floor(one * (1.0 / 128.0))
    two_full = two + over
    over_two = jnp.floor(two_full * (1.0 / 128.0))
    parts = [one - 128.0 * over, two_full - 128.0 * over_two, three + over_two]
    is_count = (row == 4) | (row == 5)
    parts = [jnp.where(is_count, part, total[:, at * LANES : (at + 1) * LANES]) for at, part in enumerate(parts)]
    return jnp.concatenate(parts + [total[:, 3 * LANES :]], axis=1)


def sum_in_tree(values):
    while len(values) > 1:
        values = [values[at] + values[at + 1] for at in range(0, len(values), 2)]
    return values[0]


def share_kernel(given, pieces, *refs):
    index_ref, arrived, made = refs[0], refs[1 : 1 + given], refs[1 + given :]
    small_rows = (pieces * made[0].shape[0] - arrived[0].shape[0]) // (pieces - 1)
    size = made[0].shape[0] - small_rows
    top = pieces * size
    small = carry_digits(sum_in_tree([ref[top:, :].astype(F32) for ref in arrived])).astype(BF16)
    for away in range(pieces):
        at = pl.ds(pl.multiple_of((index_ref[0] ^ away) * size, size), size)
        made[away][:size, :] = sum_in_tree([ref[at, :].astype(F32) for ref in arrived]).astype(BF16)
        made[away][size:, :] = small


def last_kernel(given, *refs):
    arrived, chunk_ref, small_ref = refs[:given], refs[given], refs[given + 1]
    size = chunk_ref.shape[0]
    chunk_ref[...] = sum_in_tree([ref[:size, :].astype(F32) for ref in arrived]).astype(BF16)
    small_ref[...] = carry_digits(sum_in_tree([ref[size:, :].astype(F32) for ref in arrived])).astype(BF16)


def finish_shared_kernel(experts, index_ref, own_ref, other_ref, small_ref, *outs):
    query_ref, key_ref, value_ref, out_ref, vector_refs, router_ref, count_ref = outs[:4] + (outs[4:8],) + outs[8:]
    core, place, inner_place = index_ref[0], index_ref[1], index_ref[2]
    width = query_ref.shape[1]
    half = width // 2
    size = half // 4
    for source, side in ((own_ref, core), (other_ref, 1 - core)):
        for at, out in enumerate((query_ref, key_ref, value_ref, out_ref)):
            for part in range(4):
                start = pl.multiple_of((place ^ at) * half + (inner_place ^ part) * size, size)
                row = pl.multiple_of(side * half + part * size, size)
                out[pl.ds(row, size), :] = source[pl.ds(start, size), :].astype(F32)
    small = small_ref[...].astype(F32)
    for at, ref in enumerate(vector_refs):
        ref[...] = small[at : at + 1, :]
    router_ref[...] = small[6 : 6 + experts, :]
    value = small[4:6, :LANES] + 128.0 * small[4:6, LANES : 2 * LANES] + 16384.0 * small[4:6, 2 * LANES : 3 * LANES]
    count_ref[...] = value[:, :experts].astype(jnp.int32)


def solution(mesh):
    narrow, wide = mesh.shape["narrow"], mesh.shape["wide"]

    def hop(value, narrow_bits, wide_bits):
        if wide_bits == 0:
            return lax.ppermute(value, "narrow", [(i, i ^ narrow_bits) for i in range(narrow)])
        if narrow_bits == 0:
            return lax.ppermute(value, "wide", [(i, i ^ wide_bits) for i in range(wide)])
        pairs = [
            (i * wide + j, (i ^ narrow_bits) * wide + (j ^ wide_bits)) for i in range(narrow) for j in range(wide)
        ]
        return lax.ppermute(value, ("narrow", "wide"), pairs)

    def body(
        tokens,
        gain_one,
        shift_one,
        query_w,
        key_w,
        value_w,
        out_w,
        gain_two,
        shift_two,
        router_w,
        up_w,
        up_bias,
        down_w,
        down_bias,
        picks,
        ranks,
        out_grad,
    ):
        count, width = tokens.shape
        experts = router_w.shape[1]
        capacity = ((21 * 2 * count + 20 * experts - 1) // (20 * experts) + 7) // 8 * 8
        slots_all = experts * capacity
        hidden_width = up_w.shape[2]
        half = width // 2
        pairs = HEADS // 2
        blocks = count // (2 * PATCHES)
        extra = (6 + experts + 15) // 16 * 16
        tile = width
        steps = hidden_width // tile
        narrow_at, wide_at = lax.axis_index("narrow"), lax.axis_index("wide")
        core = (narrow_at & 1)[None].astype(jnp.int32)
        place = (((narrow_at >> 1) & 1) * 2 + (wide_at & 1))[None].astype(jnp.int32)
        inner_place = ((wide_at >> 1) & 3)[None].astype(jnp.int32)
        gain_one, shift_one, gain_two, shift_two = (v[None, :] for v in (gain_one, shift_one, gain_two, shift_two))
        router_t = jnp.pad(router_w.T, ((0, LANES - experts), (0, 0)))
        up_w, down_w = up_w[0], down_w[0]

        def exchange(value):
            return lax.all_to_all(value, "wide", split_axis=0, concat_axis=0, tiled=True)

        spread, target, counts, grad_sent = pl.pallas_call(
            functools.partial(route_kernel, capacity, experts),
            out_shape=(
                shape((slots_all, count), BF16),
                shape((count, 8), F32),
                shape((8, LANES), F32),
                shape((slots_all, width), BF16),
            ),
            compiler_params=params(24),
            cost_estimate=cost(3),
            name="route",
        )(picks.T, ranks.T, out_grad)
        grad_rows = exchange(grad_sent)

        resid, normed, queries, keys, values, weights, mixed, sent = pl.pallas_call(
            attention_kernel,
            out_shape=(
                shape((count, width), F32),
                shape((count, width), BF16),
                shape((count, width), BF16),
                shape((count, width), BF16),
                shape((count, width), BF16),
                shape((blocks, pairs, 4 * PATCHES, 2 * PATCHES), BF16),
                shape((count, width), BF16),
                shape((slots_all, width), BF16),
            ),
            compiler_params=params(32),
            cost_estimate=cost(10),
            name="attention",
        )(tokens, gain_one, shift_one, query_w, key_w, value_w, out_w, gain_two, shift_two, spread)
        rows = exchange(sent)

        whole = pl.BlockSpec((slots_all, width), lambda f: (0, 0))
        lanes_whole = pl.BlockSpec((slots_all, LANES), lambda f: (0, 0))
        columns = pl.BlockSpec((slots_all, tile), lambda f: (0, f))
        up_spec = pl.BlockSpec((width, tile), lambda f: (0, f))
        down_spec = pl.BlockSpec((tile, width), lambda f: (f, 0))
        up_bias_spec = pl.BlockSpec((1, tile), lambda f: (0, f))
        down_bias_spec = pl.BlockSpec((1, width), lambda f: (0, 0))
        router_spec = pl.BlockSpec((LANES, width), lambda f: (0, 0))
        hidden, inner_grad, rows_grad, gated, gate, router_part = pl.pallas_call(
            functools.partial(expert_kernel, experts),
            grid=(steps,),
            in_specs=[SMEM(), whole, whole, up_spec, up_bias_spec, down_spec, down_bias_spec, router_spec],
            out_specs=(columns, columns, whole, whole, lanes_whole, router_spec),
            out_shape=(
                shape((slots_all, hidden_width), BF16),
                shape((slots_all, hidden_width), BF16),
                shape((slots_all, width), BF16),
                shape((slots_all, width), BF16),
                shape((slots_all, LANES), F32),
                shape((LANES, width), F32),
            ),
            scratch_shapes=[
                pltpu.VMEM((slots_all, tile), F32),
                pltpu.VMEM((slots_all, tile), F32),
                pltpu.VMEM((slots_all, width), F32),
                pltpu.VMEM((slots_all, LANES), F32),
                pltpu.VMEM((slots_all, LANES), F32),
            ],
            compiler_params=params(40),
            cost_estimate=cost(10),
            name="experts",
        )(wide_at[None].astype(jnp.int32), rows, grad_rows, up_w, up_bias, down_w, down_bias, router_t)
        back = exchange(rows_grad)

        payload = 2 * half + 16
        payload_spec = pl.BlockSpec((1, payload, width), lambda f: (f, 0, 0))
        keep, send = pl.pallas_call(
            weight_kernel,
            grid=(steps,),
            in_specs=[SMEM(), whole, whole, columns, columns],
            out_specs=(payload_spec, payload_spec),
            out_shape=(shape((steps, payload, width), BF16),) * 2,
            compiler_params=params(40),
            cost_estimate=cost(6),
            name="expert_weights",
        )(core, rows, gated, hidden, inner_grad)
        produced = pl.pallas_call(
            produce_kernel,
            grid=(steps,),
            in_specs=[columns, down_spec, down_bias_spec, lanes_whole],
            out_specs=whole,
            out_shape=shape((slots_all, width), BF16),
            scratch_shapes=[pltpu.VMEM((slots_all, width), F32)],
            compiler_params=params(32),
            cost_estimate=cost(4),
            name="produce",
        )(hidden, down_w, down_bias, gate)

        def add(one, two):
            return pl.pallas_call(
                add_kernel,
                grid=(steps,),
                in_specs=[payload_spec, payload_spec],
                out_specs=payload_spec,
                out_shape=shape((steps, payload, width), BF16),
                compiler_params=params(16),
                cost_estimate=cost(2),
                name="add_halves",
            )(one, two)

        expert_sum = add(keep, hop(send, 1, 0))
        bit = 2
        while bit < narrow:
            expert_sum = add(expert_sum, hop(expert_sum, bit, 0))
            bit *= 2
        up_grad, up_bias_grad, down_grad, down_bias_grad = pl.pallas_call(
            finish_experts_kernel,
            grid=(steps,),
            in_specs=[SMEM(), payload_spec, payload_spec],
            out_specs=(up_spec, up_bias_spec, down_spec, down_bias_spec),
            out_shape=(
                shape((width, hidden_width), F32),
                shape((1, hidden_width), F32),
                shape((hidden_width, width), F32),
                shape((1, width), F32),
            ),
            compiler_params=params(24),
            cost_estimate=cost(4),
            name="finish_experts",
        )(core, expert_sum, hop(expert_sum, 1, 0))

        produced_back = exchange(produced)
        block_out = pl.pallas_call(
            combine_kernel,
            out_shape=shape((count, width), BF16),
            compiler_params=params(16),
            cost_estimate=cost(2),
            name="combine",
        )(target, produced_back, resid)

        tall = 4 * half + extra
        keep, send, tokens_grad = pl.pallas_call(
            functools.partial(backward_kernel, experts),
            in_specs=[SMEM()] + [VMEM()] * 19,
            out_shape=(shape((tall, width), BF16), shape((tall, width), BF16), shape((count, width), BF16)),
            scratch_shapes=[pltpu.VMEM((count, width), BF16)] * 4 + [pltpu.VMEM((count, width), F32)],
            compiler_params=params(32),
            cost_estimate=cost(12),
            name="backward",
        )(
            core,
            target,
            back,
            resid,
            out_grad,
            gain_two,
            tokens,
            gain_one,
            query_w,
            key_w,
            value_w,
            out_w,
            normed,
            queries,
            keys,
            values,
            weights,
            mixed,
            counts,
            router_part,
        )

        def share(index, arrived):
            size = (arrived[0].shape[0] - extra) // 4
            return pl.pallas_call(
                functools.partial(share_kernel, len(arrived), 4),
                in_specs=[SMEM()] + [VMEM()] * len(arrived),
                out_shape=(shape((size + extra, width), BF16),) * 4,
                compiler_params=params(16),
                cost_estimate=cost(1),
                name="share",
            )(index, *arrived)

        places = ((0, 0), (0, 1), (2, 0), (2, 1))
        inner_places = ((0, 0), (0, 2), (0, 4), (0, 6))
        parts = share(place, [keep, hop(send, 1, 0)])
        parts = [parts[0]] + [hop(part, *bits) for part, bits in zip(parts[1:], places[1:])]
        parts = share(inner_place, parts)
        parts = [parts[0]] + [hop(part, *bits) for part, bits in zip(parts[1:], inner_places[1:])]

        def last(arrived):
            size = half // 4
            return pl.pallas_call(
                functools.partial(last_kernel, len(arrived)),
                out_shape=(shape((size, width), BF16), shape((extra, width), BF16)),
                compiler_params=params(16),
                cost_estimate=cost(1),
                name="last",
            )(*arrived)

        chunk, small = last(parts)
        others = [(bit, 0) for bit in (4, 8, 16, 32, 64) if bit < narrow]
        others += [(0, bit) for bit in (8, 16, 32, 64) if bit < wide]
        for bits in others:
            joined = jnp.concatenate([chunk, small], axis=0)
            chunk, small = last([joined, hop(joined, *bits)])
        chunk = jnp.concatenate([chunk] + [hop(chunk, *bits) for bits in inner_places[1:]], axis=0)
        chunk = jnp.concatenate([chunk] + [hop(chunk, *bits) for bits in places[1:]], axis=0)
        outs = pl.pallas_call(
            functools.partial(finish_shared_kernel, experts),
            in_specs=[SMEM()] + [VMEM()] * 3,
            out_shape=(shape((width, width), F32),) * 4
            + (shape((1, width), F32),) * 4
            + (shape((experts, width), F32), shape((2, experts), jnp.int32)),
            compiler_params=params(24),
            cost_estimate=cost(3),
            name="finish_shared",
        )(jnp.concatenate([core, place, inner_place]), chunk, hop(chunk, 1, 0), small)
        query_grad, key_grad, value_grad, out_w_grad, g_one, s_one, g_two, s_two, router_grad, tallies = outs
        return (
            block_out,
            tokens_grad,
            g_one[0],
            s_one[0],
            query_grad,
            key_grad,
            value_grad,
            out_w_grad,
            g_two[0],
            s_two[0],
            router_grad.T,
            up_grad[None],
            up_bias_grad,
            down_grad[None],
            down_bias_grad,
            tallies.T,
        )

    tokens_spec = P(("narrow", "wide"), None)
    in_specs = (
        (tokens_spec,)
        + (P(),) * 9
        + (P("wide", None, None), P("wide", None), P("wide", None, None), P("wide", None))
        + (tokens_spec,) * 3
    )
    out_specs = (
        (tokens_spec,) * 2
        + (P(),) * 9
        + (P("wide", None, None), P("wide", None), P("wide", None, None), P("wide", None))
        + (P(),)
    )
    return jax.shard_map(body, mesh=mesh, in_specs=in_specs, out_specs=out_specs, check_vma=False)
```

```python
import functools
import math

import jax
import jax.numpy as jnp
from jax import lax
from jax.experimental import pallas as pl
from jax.experimental.pallas import tpu as pltpu
from jax.sharding import PartitionSpec as P

HEADS = 8
PATCHES = 48
EPSILON = 1e-06
LANES = 128
MIB = 1 << 20
F32 = jnp.float32
BF16 = jnp.bfloat16

VMEM = functools.partial(pl.BlockSpec, memory_space=pltpu.VMEM)
SMEM = functools.partial(pl.BlockSpec, memory_space=pltpu.SMEM)


def shape(dims, dtype):
    return jax.ShapeDtypeStruct(dims, dtype)


def dot(a, b):
    return jnp.dot(a, b, preferred_element_type=F32)


def dot_nt(a, b):
    return lax.dot_general(a, b, (((1,), (1,)), ((), ())), preferred_element_type=F32)


def dot_tn(a, b):
    return lax.dot_general(a, b, (((0,), (0,)), ((), ())), preferred_element_type=F32)


def params(mib):
    return pltpu.CompilerParams(vmem_limit_bytes=mib * MIB)


def cost(us):
    return pl.CostEstimate(flops=int(us * 1.0e9), bytes_accessed=int(us * 1.0e5), transcendentals=0)


class Moved:
    def __init__(self, value):
        self.value = value
        self.shape, self.ndim = value.shape, value.ndim


def placed(value):
    if isinstance(value, Moved):
        return value.value
    return value if value.ndim == 1 else pltpu.with_memory_space_constraint(value, pltpu.HBM)


def loose(value):
    return pl.BlockSpec(memory_space=pl.ANY if isinstance(value, Moved) else pltpu.HBM)


def whole_spec(dims):
    return pl.BlockSpec(tuple(dims), lambda *_: (0,) * len(dims))


def run(kernel, args, outs, mib, us, name, scratch=(), after=(), grid=(1,), in_specs=None, out_specs=None, free=False, **more):
    given = len(args)
    if in_specs is None:
        in_specs = [SMEM() if a.ndim == 1 else whole_spec(a.shape) for a in args]
        out_specs = [whole_spec(o.shape) for o in outs]

    def body(*refs):
        kernel(*refs[:given], *refs[given + len(after) :])

    return pl.pallas_call(
        body,
        grid=grid,
        in_specs=list(in_specs) + [loose(value) for value in after],
        out_specs=tuple(out_specs),
        out_shape=tuple(o if free else pltpu.HBM(o.shape, o.dtype) for o in outs),
        scratch_shapes=list(scratch),
        compiler_params=params(mib),
        cost_estimate=cost(us),
        name=name,
        **more,
    )(*map(placed, args), *map(placed, after))


def norm_rows(values):
    center = values - jnp.mean(values, axis=-1, keepdims=True)
    spread = jnp.mean(center * center, axis=-1, keepdims=True)
    rate = lax.rsqrt(spread + EPSILON)
    return center * rate, rate


def norm_back(hat, rate, gain, grad):
    scaled = grad * gain
    mean_one = jnp.mean(scaled, axis=-1, keepdims=True)
    mean_two = jnp.mean(scaled * hat, axis=-1, keepdims=True)
    return rate * (scaled - mean_one - hat * mean_two)


def route_kernel(capacity, experts, picks_ref, ranks_ref, grad_ref, spread_ref, target_ref, count_ref, sent_ref):
    count = picks_ref.shape[1]
    slots_all = experts * capacity
    span = 1 << (2 * count - 1).bit_length()
    picks = picks_ref[...].astype(F32)
    base = picks * span
    order = base + ranks_ref[...].astype(F32)
    padded = jnp.concatenate([picks, order, jnp.zeros((4, count), F32)], axis=0)
    turned = jnp.transpose(padded)
    targets = []
    for j in range(2):
        row = order[j : j + 1]
        floor = base[j : j + 1]
        slot = jnp.zeros((1, count), F32)
        for other in range(2):
            column = turned[:, 2 + other : 3 + other]
            ahead = (column < row) & (column >= floor)
            slot = slot + jnp.sum(jnp.where(ahead, 1.0, 0.0), axis=0, keepdims=True)
        kept = slot < capacity
        targets.append(jnp.where(kept, picks[j : j + 1] * capacity + slot, float(slots_all)))
    target_turned = jnp.transpose(jnp.concatenate(targets + [jnp.zeros((6, count), F32)], axis=0))
    target_ref[...] = target_turned
    lane = lax.broadcasted_iota(jnp.int32, (count, LANES), 1).astype(F32)
    kept_count = jnp.zeros((1, LANES), F32)
    all_count = jnp.zeros((1, LANES), F32)
    for j in range(2):
        named = jnp.where(turned[:, j : j + 1] == lane, 1.0, 0.0)
        live = jnp.where(target_turned[:, j : j + 1] < slots_all, 1.0, 0.0)
        all_count = all_count + jnp.sum(named, axis=0, keepdims=True)
        kept_count = kept_count + jnp.sum(named * live, axis=0, keepdims=True)
    count_ref[...] = jnp.concatenate([kept_count, all_count - kept_count, jnp.zeros((6, LANES), F32)], axis=0)
    step = 64
    for start in range(0, slots_all, step):
        index = lax.broadcasted_iota(jnp.int32, (step, count), 0).astype(F32) + float(start)
        hit = (index == targets[0]) | (index == targets[1])
        spread_ref[start : start + step, :] = jnp.where(hit, 1.0, 0.0).astype(BF16)
    sent_ref[...] = dot(spread_ref[...], grad_ref[...]).astype(BF16)


def head_masks(width):
    lane = lax.broadcasted_iota(jnp.int32, (1, width), 1)
    return lane < width // 2


def stack_heads(pair, low):
    zero = jnp.zeros_like(pair)
    return jnp.concatenate([jnp.where(low, pair, zero), jnp.where(low, zero, pair)], axis=0)


def attention_kernel(
    tokens_ref,
    gain_one_ref,
    shift_one_ref,
    query_w_ref,
    key_w_ref,
    value_w_ref,
    out_w_ref,
    gain_two_ref,
    shift_two_ref,
    resid_ref,
    normed_ref,
    query_ref,
    key_ref,
    value_ref,
    weight_ref,
    mixed_ref,
    second_ref,
):
    count, width = tokens_ref.shape
    inputs = tokens_ref[...].astype(F32)
    hat, _ = norm_rows(inputs)
    normed_ref[...] = (hat * gain_one_ref[...] + shift_one_ref[...]).astype(BF16)
    normed = normed_ref[...]
    query_ref[...] = (dot(normed, query_w_ref[...]).astype(BF16).astype(F32) * (1.0 / math.sqrt(width // HEADS))).astype(BF16)
    key_ref[...] = dot(normed, key_w_ref[...]).astype(BF16)
    value_ref[...] = dot(normed, value_w_ref[...]).astype(BF16)
    pairs = HEADS // 2
    wide = width // pairs
    block = 2 * PATCHES
    low = head_masks(wide)
    row_image = (lax.broadcasted_iota(jnp.int32, (2 * block, block), 0) % block) // PATCHES
    column_image = lax.broadcasted_iota(jnp.int32, (2 * block, block), 1) // PATCHES
    bias = jnp.where(row_image == column_image, 0.0, -1e30)
    for item in range(count // block):
        rows = slice(item * block, (item + 1) * block)
        for pair in range(pairs):
            lanes = slice(pair * wide, (pair + 1) * wide)
            stacked = stack_heads(query_ref[rows, lanes], low)
            scores = dot_nt(stacked, key_ref[rows, lanes]) + bias
            powers = jnp.exp(scores - jnp.max(scores, axis=-1, keepdims=True))
            weights = (powers / jnp.sum(powers, axis=-1, keepdims=True)).astype(BF16)
            weight_ref[item, pair] = weights
            mixed = dot(weights, value_ref[rows, lanes])
            mixed_ref[rows, lanes] = jnp.where(low, mixed[:block], mixed[block:]).astype(BF16)
    resid = inputs + dot(mixed_ref[...], out_w_ref[...])
    resid_ref[...] = resid
    hat, _ = norm_rows(resid)
    second_ref[...] = (hat * gain_two_ref[...] + shift_two_ref[...]).astype(BF16)


def dispatch_kernel(spread_ref, second_ref, sent_ref):
    sent_ref[...] = dot(spread_ref[...], second_ref[...]).astype(BF16)


def expert_kernel(
    experts,
    me_ref,
    rows_ref,
    grad_ref,
    up_ref,
    up_bias_ref,
    down_ref,
    down_bias_ref,
    router_ref,
    hidden_ref,
    inner_grad_ref,
    rows_grad_ref,
    gated_ref,
    gate_ref,
    router_grad_ref,
    inner_s,
    back_s,
    total_s,
    pair_s,
    gates_s,
):
    step = pl.program_id(0)
    total, width = rows_ref.shape
    tile = up_ref.shape[1]

    @pl.when(step == 0)
    def _():
        lane = lax.broadcasted_iota(jnp.int32, (total, LANES), 1)
        logits = dot_nt(rows_ref[...], router_ref[...])
        logits = jnp.where(lane < experts, logits, -1e30)
        powers = jnp.exp(logits - jnp.max(logits, axis=-1, keepdims=True))
        gates = powers / jnp.sum(powers, axis=-1, keepdims=True)
        gates_s[...] = gates
        gate = jnp.sum(jnp.where(lane == me_ref[0], gates, 0.0), axis=-1, keepdims=True)
        gate_ref[...] = jnp.broadcast_to(gate, (total, LANES))
        gated_ref[...] = (gate * grad_ref[...].astype(F32)).astype(BF16)
        total_s[...] = jnp.zeros_like(total_s)
        pair_s[...] = jnp.zeros_like(pair_s)

    inner_s[...] = dot(rows_ref[...], up_ref[...])
    back_s[...] = dot_nt(grad_ref[...], down_ref[...])
    chunk = 16
    root = math.sqrt(2.0 / math.pi)

    def some_rows(index, carry):
        at = pl.ds(pl.multiple_of(index * chunk, chunk), chunk)
        inner = inner_s[at, :] + up_bias_ref[...]
        back = back_s[at, :]
        square = inner * inner
        half = 0.5 + 0.5 * jnp.tanh(inner * (root + (root * 0.044715) * square))
        hidden = inner * half
        slope = half + (hidden - hidden * half) * (2.0 * root + (6.0 * root * 0.044715) * square)
        gate = gate_ref[at, :]
        gate = jnp.concatenate([gate] * (tile // LANES), axis=1)
        hidden_ref[at, :] = hidden.astype(BF16)
        inner_grad_ref[at, :] = (back * gate * slope).astype(BF16)
        product = hidden * back
        part = product[:, :LANES]
        for other in range(1, tile // LANES):
            part = part + product[:, other * LANES : (other + 1) * LANES]
        pair_s[at, :] = pair_s[at, :] + part
        return carry

    lax.fori_loop(0, total // chunk, some_rows, 0, unroll=2)
    total_s[...] += dot_nt(inner_grad_ref[...], up_ref[...])

    @pl.when(step == pl.num_programs(0) - 1)
    def _():
        lane = lax.broadcasted_iota(jnp.int32, (total, LANES), 1)
        pair_grad = jnp.sum(pair_s[...], axis=-1, keepdims=True)
        pair_grad = pair_grad + jnp.sum(grad_ref[...].astype(F32) * down_bias_ref[...], axis=-1, keepdims=True)
        own = jnp.where(lane == me_ref[0], 1.0, 0.0)
        logit_grad = (gates_s[...] * (own - gate_ref[...]) * pair_grad).astype(BF16)
        rows_grad_ref[...] = (total_s[...] + dot(logit_grad, router_ref[...])).astype(BF16)
        router_grad_ref[...] = dot_tn(logit_grad, rows_ref[...])


def weight_kernel(core_ref, rows_ref, gated_ref, hidden_ref, inner_grad_ref, keep_ref, send_ref):
    step = pl.program_id(0)
    width = rows_ref.shape[1]
    half = width // 2
    first = core_ref[0] == 0
    up = dot_tn(rows_ref[...], inner_grad_ref[...]).astype(BF16)
    keep_ref[0, :half, :] = jnp.where(first, up[:half], up[half:])
    send_ref[0, :half, :] = jnp.where(first, up[half:], up[:half])
    down = dot_tn(hidden_ref[...], gated_ref[...]).astype(BF16)
    keep_ref[0, half : 2 * half, :] = jnp.where(first, down[:half], down[half:])
    send_ref[0, half : 2 * half, :] = jnp.where(first, down[half:], down[:half])
    up_bias = jnp.sum(inner_grad_ref[...].astype(F32), axis=0, keepdims=True)
    down_bias = jnp.sum(gated_ref[...].astype(F32), axis=0, keepdims=True)
    small = jnp.concatenate([up_bias, down_bias, jnp.zeros((14, width), F32)], axis=0).astype(BF16)
    keep_ref[0, 2 * half :, :] = small
    send_ref[0, 2 * half :, :] = small


def produce_kernel(hidden_ref, down_ref, down_bias_ref, gate_ref, out_ref, total_s):
    step = pl.program_id(0)

    @pl.when(step == 0)
    def _():
        total_s[...] = jnp.zeros_like(total_s)

    total_s[...] += dot(hidden_ref[...], down_ref[...])

    @pl.when(step == pl.num_programs(0) - 1)
    def _():
        gate = gate_ref[...]
        gate = jnp.concatenate([gate] * (out_ref.shape[1] // LANES), axis=1)
        out_ref[...] = ((total_s[...] + down_bias_ref[...]) * gate).astype(BF16)


def add_kernel(one_ref, two_ref, out_ref):
    out_ref[...] = (one_ref[...].astype(F32) + two_ref[...].astype(F32)).astype(BF16)


def finish_experts_kernel(core_ref, own_ref, other_ref, *refs):
    up_ref, up_bias_ref, down_ref, down_bias_ref = refs[-4:]
    half = up_ref.shape[0] // 2
    first = core_ref[0] == 0
    own = own_ref[0].astype(F32)
    other = other_ref[0].astype(F32)
    up_ref[:half, :] = jnp.where(first, own[:half], other[:half])
    up_ref[half:, :] = jnp.where(first, other[:half], own[:half])
    down_ref[:half, :] = jnp.where(first, own[half : 2 * half], other[half : 2 * half])
    down_ref[half:, :] = jnp.where(first, other[half : 2 * half], own[half : 2 * half])
    up_bias_ref[...] = own[2 * half : 2 * half + 1]
    down_bias_ref[...] = own[2 * half + 1 : 2 * half + 2]


def one_hot_rows(target_ref, slots_all):
    count = target_ref.shape[0]
    lane = lax.broadcasted_iota(jnp.int32, (64, slots_all), 1).astype(F32)
    pieces = []
    for start in range(0, count, 64):
        one = target_ref[start : start + 64, 0:1]
        two = target_ref[start : start + 64, 1:2]
        pieces.append(jnp.where((lane == one) | (lane == two), 1.0, 0.0).astype(BF16))
    return jnp.concatenate(pieces, axis=0)


def combine_kernel(target_ref, produced_ref, resid_ref, out_ref):
    picked = one_hot_rows(target_ref, produced_ref.shape[0])
    out_ref[...] = (resid_ref[...] + dot(picked, produced_ref[...])).astype(BF16)


def backward_kernel(
    experts,
    core_ref,
    target_ref,
    back_ref,
    resid_ref,
    grad_ref,
    gain_two_ref,
    tokens_ref,
    gain_one_ref,
    query_w_ref,
    key_w_ref,
    value_w_ref,
    out_w_ref,
    normed_ref,
    query_ref,
    key_ref,
    value_ref,
    weight_ref,
    mixed_ref,
    count_ref,
    router_grad_ref,
    keep_ref,
    send_ref,
    tokens_grad_ref,
    queries_s,
    keys_s,
    values_s,
    mixed_grad_s,
    resid_grad_s,
):
    count, width = tokens_ref.shape
    picked = one_hot_rows(target_ref, back_ref.shape[0])
    second_grad = dot(picked, back_ref[...])
    hat, rate = norm_rows(resid_ref[...])
    gain_two_grad = jnp.sum(second_grad * hat, axis=0, keepdims=True)
    shift_two_grad = jnp.sum(second_grad, axis=0, keepdims=True)
    resid_grad_s[...] = grad_ref[...].astype(F32) + norm_back(hat, rate, gain_two_ref[...], second_grad)
    branch = resid_grad_s[...].astype(BF16)
    half = width // 2
    first = core_ref[0] == 0

    def put(at, value):
        value = value.astype(BF16)
        keep_ref[at * half : (at + 1) * half, :] = jnp.where(first, value[:half], value[half:])
        send_ref[at * half : (at + 1) * half, :] = jnp.where(first, value[half:], value[:half])

    put(3, dot_tn(mixed_ref[...], branch))
    mixed_grad_s[...] = dot_nt(branch, out_w_ref[...]).astype(BF16)
    pairs = HEADS // 2
    wide = width // pairs
    block = 2 * PATCHES
    scale = 1.0 / math.sqrt(width // HEADS)
    low = head_masks(wide)
    for item in range(count // block):
        rows = slice(item * block, (item + 1) * block)
        for pair in range(pairs):
            lanes = slice(pair * wide, (pair + 1) * wide)
            mixed_stack = stack_heads(mixed_grad_s[rows, lanes], low)
            query_stack = stack_heads(query_ref[rows, lanes], low)
            weights = weight_ref[item, pair]
            weight_grad = dot_nt(mixed_stack, value_ref[rows, lanes])
            product = weights.astype(F32) * weight_grad
            score_grad = product - weights.astype(F32) * jnp.sum(product, axis=-1, keepdims=True)
            score_grad = score_grad.astype(BF16)
            values_s[rows, lanes] = dot_tn(weights, mixed_stack).astype(BF16)
            keys_s[rows, lanes] = dot_tn(score_grad, query_stack).astype(BF16)
            made = dot(score_grad, key_ref[rows, lanes]) * scale
            queries_s[rows, lanes] = jnp.where(low, made[:block], made[block:]).astype(BF16)
    normed = normed_ref[...]
    put(0, dot_tn(normed, queries_s[...]))
    put(1, dot_tn(normed, keys_s[...]))
    put(2, dot_tn(normed, values_s[...]))
    normed_grad = (
        dot_nt(queries_s[...], query_w_ref[...])
        + dot_nt(keys_s[...], key_w_ref[...])
        + dot_nt(values_s[...], value_w_ref[...])
    )
    hat, rate = norm_rows(tokens_ref[...].astype(F32))
    gain_one_grad = jnp.sum(normed_grad * hat, axis=0, keepdims=True)
    shift_one_grad = jnp.sum(normed_grad, axis=0, keepdims=True)
    tokens_grad_ref[...] = (resid_grad_s[...] + norm_back(hat, rate, gain_one_ref[...], normed_grad)).astype(BF16)
    digits = []
    for kind in range(2):
        value = count_ref[kind : kind + 1, :]
        high = jnp.floor(value * (1.0 / 128.0))
        digits.append(jnp.concatenate([value - 128.0 * high, high] + [jnp.zeros_like(value)] * (width // LANES - 2), axis=1))
    extra = keep_ref.shape[0] - 4 * half
    small = [gain_one_grad, shift_one_grad, gain_two_grad, shift_two_grad] + digits + [router_grad_ref[:experts, :]]
    small = jnp.concatenate(small + [jnp.zeros((extra - 6 - experts, width), F32)], axis=0).astype(BF16)
    keep_ref[4 * half :, :] = small
    send_ref[4 * half :, :] = small


def carry_digits(total):
    row = lax.broadcasted_iota(jnp.int32, (total.shape[0], LANES), 0)
    one, two, three = (total[:, at * LANES : (at + 1) * LANES] for at in range(3))
    over = jnp.floor(one * (1.0 / 128.0))
    two_full = two + over
    over_two = jnp.floor(two_full * (1.0 / 128.0))
    parts = [one - 128.0 * over, two_full - 128.0 * over_two, three + over_two]
    is_count = (row == 4) | (row == 5)
    parts = [jnp.where(is_count, part, total[:, at * LANES : (at + 1) * LANES]) for at, part in enumerate(parts)]
    return jnp.concatenate(parts + [total[:, 3 * LANES :]], axis=1)


def sum_in_tree(values):
    while len(values) > 1:
        values = [values[at] + values[at + 1] for at in range(0, len(values), 2)]
    return values[0]


def share_kernel(given, pieces, *refs):
    index_ref, arrived, made = refs[0], refs[1 : 1 + given], refs[1 + given :]
    small_rows = (pieces * made[0].shape[0] - arrived[0].shape[0]) // (pieces - 1)
    size = made[0].shape[0] - small_rows
    top = pieces * size
    small = carry_digits(sum_in_tree([ref[top:, :].astype(F32) for ref in arrived])).astype(BF16)
    for away in range(pieces):
        at = pl.ds(pl.multiple_of((index_ref[0] ^ away) * size, size), size)
        made[away][:size, :] = sum_in_tree([ref[at, :].astype(F32) for ref in arrived]).astype(BF16)
        made[away][size:, :] = small


def gather_kernel(*refs):
    arrived, out_ref = refs[:-1], refs[-1]
    size = arrived[0].shape[0]
    for at, ref in enumerate(arrived):
        out_ref[at * size : (at + 1) * size, :] = ref[...]


def last_kernel(given, *refs):
    arrived, chunk_ref, small_ref = refs[:given], refs[given], refs[given + 1]
    size = chunk_ref.shape[0]
    chunk_ref[...] = sum_in_tree([ref[:size, :].astype(F32) for ref in arrived]).astype(BF16)
    small_ref[...] = carry_digits(sum_in_tree([ref[size:, :].astype(F32) for ref in arrived])).astype(BF16)


def finish_shared_kernel(experts, index_ref, own_ref, other_ref, small_ref, *outs):
    query_ref, key_ref, value_ref, out_ref, vector_refs, router_ref, count_ref = outs[:4] + (outs[4:8],) + outs[8:]
    core, place, inner_place = index_ref[0], index_ref[1], index_ref[2]
    width = query_ref.shape[1]
    half = width // 2
    size = half // 4
    for source, side in ((own_ref, core), (other_ref, 1 - core)):
        for at, out in enumerate((query_ref, key_ref, value_ref, out_ref)):
            for part in range(4):
                start = pl.multiple_of((place ^ at) * half + (inner_place ^ part) * size, size)
                row = pl.multiple_of(side * half + part * size, size)
                out[pl.ds(row, size), :] = source[pl.ds(start, size), :].astype(F32)
    small = small_ref[...].astype(F32)
    for at, ref in enumerate(vector_refs):
        ref[...] = small[at : at + 1, :]
    router_ref[...] = small[6 : 6 + experts, :]
    value = small[4:6, :LANES] + 128.0 * small[4:6, LANES : 2 * LANES] + 16384.0 * small[4:6, 2 * LANES : 3 * LANES]
    count_ref[...] = value[:, :experts].astype(jnp.int32)


def solution(mesh):
    narrow, wide = mesh.shape["narrow"], mesh.shape["wide"]

    def hop(value, narrow_bits, wide_bits):
        if wide_bits == 0:
            return lax.ppermute(value, "narrow", [(i, i ^ narrow_bits) for i in range(narrow)])
        if narrow_bits == 0:
            return lax.ppermute(value, "wide", [(i, i ^ wide_bits) for i in range(wide)])
        pairs = [
            (i * wide + j, (i ^ narrow_bits) * wide + (j ^ wide_bits)) for i in range(narrow) for j in range(wide)
        ]
        return lax.ppermute(value, ("narrow", "wide"), pairs)

    def body(
        tokens,
        gain_one,
        shift_one,
        query_w,
        key_w,
        value_w,
        out_w,
        gain_two,
        shift_two,
        router_w,
        up_w,
        up_bias,
        down_w,
        down_bias,
        picks,
        ranks,
        out_grad,
    ):
        count, width = tokens.shape
        experts = router_w.shape[1]
        capacity = ((21 * 2 * count + 20 * experts - 1) // (20 * experts) + 7) // 8 * 8
        slots_all = experts * capacity
        hidden_width = up_w.shape[2]
        half = width // 2
        pairs = HEADS // 2
        blocks = count // (2 * PATCHES)
        extra = (6 + experts + 15) // 16 * 16
        tile = width
        steps = hidden_width // tile
        narrow_at, wide_at = lax.axis_index("narrow"), lax.axis_index("wide")
        core = (narrow_at & 1)[None].astype(jnp.int32)
        place = (((narrow_at >> 1) & 1) * 2 + (wide_at & 1))[None].astype(jnp.int32)
        inner_place = ((wide_at >> 1) & 3)[None].astype(jnp.int32)
        gain_one, shift_one, gain_two, shift_two = (v[None, :] for v in (gain_one, shift_one, gain_two, shift_two))
        router_t = jnp.pad(router_w.T, ((0, LANES - experts), (0, 0)))
        up_w, down_w = up_w[0], down_w[0]

        def exchange(value):
            return lax.all_to_all(value, "wide", split_axis=0, concat_axis=0, tiled=True)

        spread, target, counts, grad_sent = run(
            functools.partial(route_kernel, capacity, experts),
            (picks.T, ranks.T, out_grad),
            (
                shape((slots_all, count), BF16),
                shape((count, 8), F32),
                shape((8, LANES), F32),
                shape((slots_all, width), BF16),
            ),
            24,
            3,
            "route",
        )
        grad_rows = exchange(grad_sent)
        token_rows = shape((count, width), BF16)
        resid, normed, queries, keys, values, weights, mixed, second = run(
            attention_kernel,
            (tokens, gain_one, shift_one, query_w, key_w, value_w, out_w, gain_two, shift_two),
            (shape((count, width), F32),)
            + (token_rows,) * 4
            + (shape((blocks, pairs, 4 * PATCHES, 2 * PATCHES), BF16), token_rows, token_rows),
            40,
            10,
            "attention",
        )
        rows_shape = shape((slots_all, width), BF16)
        (sent,) = run(dispatch_kernel, (spread, second), (rows_shape,), 16, 1, "dispatch", after=(Moved(grad_rows),))
        rows = exchange(sent)

        whole = pl.BlockSpec((slots_all, width), lambda f: (0, 0))
        lanes_whole = pl.BlockSpec((slots_all, LANES), lambda f: (0, 0))
        columns = pl.BlockSpec((slots_all, tile), lambda f: (0, f))
        up_spec = pl.BlockSpec((width, tile), lambda f: (0, f))
        down_spec = pl.BlockSpec((tile, width), lambda f: (f, 0))
        up_bias_spec = pl.BlockSpec((1, tile), lambda f: (0, f))
        down_bias_spec = pl.BlockSpec((1, width), lambda f: (0, 0))
        router_spec = pl.BlockSpec((LANES, width), lambda f: (0, 0))
        payload = 2 * half + 16
        hidden_shape = shape((slots_all, hidden_width), BF16)
        hidden, inner_grad, rows_grad, gated, gate, router_part = run(
            functools.partial(expert_kernel, experts),
            (
                wide_at[None].astype(jnp.int32),
                Moved(rows),
                Moved(grad_rows),
                up_w,
                up_bias,
                down_w,
                down_bias,
                router_t,
            ),
            (hidden_shape, hidden_shape, rows_shape, rows_shape, shape((slots_all, LANES), F32), shape((LANES, width), F32)),
            48,
            10,
            "experts",
            (
                pltpu.VMEM((slots_all, tile), F32),
                pltpu.VMEM((slots_all, tile), F32),
                pltpu.VMEM((slots_all, width), F32),
                pltpu.VMEM((slots_all, LANES), F32),
                pltpu.VMEM((slots_all, LANES), F32),
            ),
            grid=(steps,),
            in_specs=(SMEM(), whole, whole, up_spec, up_bias_spec, down_spec, down_bias_spec, router_spec),
            out_specs=(columns, columns, whole, whole, lanes_whole, router_spec),
        )
        back = exchange(rows_grad)

        halves = 2
        per_half = steps // halves
        payload_shape = shape((per_half, payload, width), BF16)
        payload_spec = pl.BlockSpec((1, payload, width), lambda f: (f, 0, 0))
        expert_sums = []
        for side in range(halves):
            some = pl.BlockSpec((slots_all, tile), lambda f, side=side: (0, side * per_half + f))
            expert_sums.append(
                run(
                    weight_kernel,
                    (core, Moved(rows), gated, hidden, inner_grad),
                    (payload_shape,) * 2,
                    40,
                    0.5,
                    "expert_weights",
                    grid=(per_half,),
                    in_specs=(SMEM(), whole, whole, some, some),
                    out_specs=(payload_spec,) * 2,
                    after=[pair[0] for pair in expert_sums],
                )
            )

        def add(one, two, after=()):
            return run(
                add_kernel,
                (one, Moved(two)),
                (payload_shape,),
                16,
                1,
                "add_halves",
                grid=(per_half,),
                in_specs=(payload_spec,) * 2,
                out_specs=(payload_spec,),
                after=after,
            )[0]

        sum_one = add(expert_sums[0][0], hop(expert_sums[0][1], 1, 0))
        two_keep, two_arrived = expert_sums[1][0], hop(expert_sums[1][1], 1, 0)
        (produced,) = run(
            produce_kernel,
            (hidden, down_w, down_bias, gate),
            (rows_shape,),
            32,
            1,
            "produce",
            (pltpu.VMEM((slots_all, width), F32),),
            grid=(steps,),
            in_specs=(columns, down_spec, down_bias_spec, lanes_whole),
            out_specs=(whole,),
            after=(sum_one,),
        )

        def over_chips(value, bit=2, after=()):
            while bit < narrow:
                value = add(value, hop(value, bit, 0), after)
                bit *= 2
            return value

        def finish_experts(side, total, arrived, earlier):
            spec = lambda dims, at: pl.BlockSpec(dims, lambda f: at(side * per_half + f))
            outs = (
                shape((width, hidden_width), F32),
                shape((1, hidden_width), F32),
                shape((hidden_width, width), F32),
                shape((1, width), F32),
            )
            return run(
                finish_experts_kernel,
                (core, total, Moved(arrived), *earlier),
                outs,
                24,
                0.5,
                "finish_experts",
                grid=(per_half,),
                in_specs=[SMEM(), payload_spec, payload_spec] + [pl.BlockSpec(memory_space=pltpu.HBM)] * len(earlier),
                out_specs=(
                    spec((width, tile), lambda f: (0, f)),
                    spec((1, tile), lambda f: (0, f)),
                    spec((tile, width), lambda f: (f, 0)),
                    down_bias_spec,
                ),
                input_output_aliases={3 + at: at for at in range(len(earlier))},
            )

        produced_back = exchange(produced)

        tall = 4 * half + extra
        keep, send, tokens_grad = run(
            functools.partial(backward_kernel, experts),
            (
                core,
                target,
                Moved(back),
                resid,
                out_grad,
                gain_two,
                tokens,
                gain_one,
                query_w,
                key_w,
                value_w,
                out_w,
                normed,
                queries,
                keys,
                values,
                weights,
                mixed,
                counts,
                router_part,
            ),
            (shape((tall, width), BF16), shape((tall, width), BF16), token_rows),
            48,
            2,
            "backward",
            [pltpu.VMEM((count, width), BF16)] * 4 + [pltpu.VMEM((count, width), F32)],
            after=(sum_one, produced, Moved(two_arrived)),
        )

        def share(index, arrived, after=()):
            size = (arrived[0].shape[0] - extra) // 4
            return run(
                functools.partial(share_kernel, len(arrived), 4),
                (index, arrived[0] if size == half else Moved(arrived[0]), *map(Moved, arrived[1:])),
                (shape((size + extra, width), BF16),) * 4,
                16,
                0.05,
                "share",
                after=after,
                free=True,
            )

        def last(arrived, after=()):
            return run(
                functools.partial(last_kernel, len(arrived)),
                tuple(map(Moved, arrived)),
                (shape((half // 4, width), BF16), shape((extra, width), BF16)),
                16,
                0.05,
                "last",
                after=after,
                free=True,
            )

        def gather(arrived, after=()):
            rows_in = sum(value.shape[0] for value in arrived)
            return run(
                gather_kernel,
                tuple(map(Moved, arrived)),
                (shape((rows_in, width), BF16),),
                16,
                0.05,
                "gather",
                after=after,
                free=True,
            )[0]

        def spread_out(parts, bits):
            return [parts[0]] + [hop(part, *bit) for part, bit in zip(parts[1:], bits[1:])]

        places = ((0, 0), (0, 1), (2, 0), (2, 1))
        inner_places = ((0, 0), (0, 2), (0, 4), (0, 6))
        one_arrived = hop(sum_one, 2, 0)
        parts = share(place, [keep, hop(send, 1, 0)], (Moved(one_arrived),))
        sum_one = over_chips(add(sum_one, one_arrived, (Moved(parts[0]),)), 4)
        parts = share(inner_place, spread_out(parts, places), (sum_one,))
        sum_two = add(two_keep, two_arrived, (Moved(parts[0]),))
        parts = spread_out(parts, inner_places)
        (block_out,) = run(combine_kernel, (target, Moved(produced_back), resid), (token_rows,), 16, 0.1, "combine")
        chunk, small = last(parts, (block_out, sum_two))
        others = [(bit, 0) for bit in (4, 8, 16, 32, 64) if bit < narrow]
        others += [(0, bit) for bit in (8, 16, 32, 64) if bit < wide]
        for bits in others:
            joined = jnp.concatenate([chunk, small], axis=0)
            chunk, small = last([joined, hop(joined, *bits)])
        finished = finish_experts(0, sum_one, hop(sum_one, 1, 0), ())
        chunk = gather(spread_out([chunk] * 4, inner_places), finished[:1])
        sum_two = over_chips(sum_two, after=(Moved(chunk),))
        finished = finish_experts(1, sum_two, hop(sum_two, 1, 0), finished)
        chunk = gather(spread_out([chunk] * 4, places), finished[:1])
        up_grad, up_bias_grad, down_grad, down_bias_grad = finished
        outs = run(
            functools.partial(finish_shared_kernel, experts),
            (jnp.concatenate([core, place, inner_place]), Moved(chunk), Moved(hop(chunk, 1, 0)), small),
            (shape((width, width), F32),) * 4
            + (shape((1, width), F32),) * 4
            + (shape((experts, width), F32), shape((2, experts), jnp.int32)),
            32,
            3,
            "finish_shared",
        )
        query_grad, key_grad, value_grad, out_w_grad, g_one, s_one, g_two, s_two, router_grad, tallies = outs
        return (
            block_out,
            tokens_grad,
            g_one[0],
            s_one[0],
            query_grad,
            key_grad,
            value_grad,
            out_w_grad,
            g_two[0],
            s_two[0],
            router_grad.T,
            up_grad[None],
            up_bias_grad,
            down_grad[None],
            down_bias_grad,
            tallies.T,
        )

    tokens_spec = P(("narrow", "wide"), None)
    in_specs = (
        (tokens_spec,)
        + (P(),) * 9
        + (P("wide", None, None), P("wide", None), P("wide", None, None), P("wide", None))
        + (tokens_spec,) * 3
    )
    out_specs = (
        (tokens_spec,) * 2
        + (P(),) * 9
        + (P("wide", None, None), P("wide", None), P("wide", None, None), P("wide", None))
        + (P(),)
    )
    return jax.shard_map(body, mesh=mesh, in_specs=in_specs, out_specs=out_specs, check_vma=False)
```

```python
import functools
import math

import jax
import jax.numpy as jnp
from jax import lax
from jax.experimental import pallas as pl
from jax.experimental.pallas import tpu as pltpu
from jax.sharding import PartitionSpec as P

HEADS = 8
PATCHES = 48
EPSILON = 1e-06
LANES = 128
MIB = 1 << 20
F32 = jnp.float32
BF16 = jnp.bfloat16

VMEM = functools.partial(pl.BlockSpec, memory_space=pltpu.VMEM)
SMEM = functools.partial(pl.BlockSpec, memory_space=pltpu.SMEM)


def shape(dims, dtype):
    return jax.ShapeDtypeStruct(dims, dtype)


def dot(a, b):
    return jnp.dot(a, b, preferred_element_type=F32)


def dot_nt(a, b):
    return lax.dot_general(a, b, (((1,), (1,)), ((), ())), preferred_element_type=F32)


def dot_tn(a, b):
    return lax.dot_general(a, b, (((0,), (0,)), ((), ())), preferred_element_type=F32)


def params(mib):
    return pltpu.CompilerParams(vmem_limit_bytes=mib * MIB)


def cost(us):
    return pl.CostEstimate(flops=int(us * 1.0e9), bytes_accessed=int(us * 1.0e5), transcendentals=0)


class Held:
    def __init__(self, value):
        self.value = value
        self.shape, self.dtype, self.ndim = value.shape, value.dtype, value.ndim


def placed(value):
    if isinstance(value, Held):
        return value.value
    if isinstance(value, Part):
        value = value.value
    return value if value.ndim == 1 else pltpu.with_memory_space_constraint(value, pltpu.HBM)


def whole_spec(dims):
    return pl.BlockSpec(tuple(dims), lambda *_: (0,) * len(dims))


def held(dims, dtype):
    return pltpu.VMEM(tuple(dims), dtype)


def far(dims, dtype):
    return pltpu.HBM(tuple(dims), dtype)


def loose(value):
    return pl.BlockSpec(memory_space=pl.ANY if isinstance(value, Held) else pltpu.HBM)


def run(kernel, args, outs, mib, us, name, scratch=(), after=(), grid=(1,), in_specs=None, out_specs=None, free=False, **more):
    given = len(args)
    if in_specs is None:
        in_specs = [SMEM() if a.ndim == 1 else whole_spec(a.shape) for a in args]
    if out_specs is None:
        out_specs = [whole_spec(o.shape) for o in outs]

    def body(*refs):
        kernel(*refs[:given], *refs[given + len(after) :])

    return pl.pallas_call(
        body,
        grid=grid,
        in_specs=list(in_specs) + [loose(value) for value in after],
        out_specs=tuple(out_specs),
        out_shape=tuple(shape(o.shape, o.dtype) if free else far(o.shape, o.dtype) for o in outs),
        scratch_shapes=list(scratch),
        compiler_params=params(mib),
        cost_estimate=cost(us),
        name=name,
        **more,
    )(*map(placed, args), *map(placed, after))


class Part:
    def __init__(self, value, tile, at, rows=False):
        some, all_of = slice(at * tile, (at + 1) * tile), slice(None)
        self.value, self.index = value, (some, all_of) if rows else (all_of, some)
        self.shape = (tile, value.shape[1]) if rows else (value.shape[0], tile)
        self.dtype, self.ndim = value.dtype, 2


class Arriving:
    def __init__(self, source, target, semaphore):
        self.target, self.shape = target, target.shape
        self.copy = pltpu.make_async_copy(source, target, semaphore)
        self.copy.start()
        self.here = False

    def wait(self):
        if not self.here:
            self.copy.wait()
            self.here = True

    def __getitem__(self, index):
        self.wait()
        return self.target[index]


class Leaving:
    def __init__(self, source, target, semaphores):
        self.source, self.target, self.semaphores = source, target, semaphores
        self.shape = source.shape
        self.copies = []

    def __getitem__(self, index):
        return self.source[index]

    def __setitem__(self, index, value):
        self.source[index] = value

    def flush(self, *index):
        one, two = (self.source.at[index], self.target.at[index]) if index else (self.source, self.target)
        self.copies.append(pltpu.make_async_copy(one, two, self.semaphores.at[len(self.copies)]))
        self.copies[-1].start()

    def wait(self):
        for copy in self.copies:
            copy.wait()


def fuse(kernel, args, outs, mib, us, name, scratch=(), after=()):
    is_far = [not isinstance(a, Held) and a.ndim > 1 for a in args]
    out_far = [o.memory_space == pltpu.HBM for o in outs]
    given, made = len(args), len(outs)

    def body(*refs):
        ins, refs = list(refs[:given]), refs[given + len(after) :]
        results, refs = list(refs[:made]), list(refs[made:])
        arrivals, departures = refs.pop(), refs.pop()
        coming, going = [], []
        for at in range(given):
            if is_far[at]:
                source = ins[at].at[args[at].index] if isinstance(args[at], Part) else ins[at]
                ins[at] = Arriving(source, refs.pop(0), arrivals.at[len(coming)])
                coming.append(ins[at])
        for at in range(made):
            if out_far[at]:
                results[at] = Leaving(refs.pop(0), results[at], departures.at[len(going)])
                going.append(results[at])
        kernel(*ins, *results, *refs)
        for item in coming + going:
            item.wait()

    def spec(value):
        if isinstance(value, Held):
            return VMEM()
        return SMEM() if value.ndim == 1 else pl.BlockSpec(memory_space=pltpu.HBM)

    return pl.pallas_call(
        body,
        in_specs=[spec(a) for a in args] + [loose(value) for value in after],
        out_specs=tuple(pl.BlockSpec(memory_space=o.memory_space) for o in outs),
        out_shape=tuple(outs),
        scratch_shapes=[pltpu.VMEM(a.shape, a.dtype) for a, there in zip(args, is_far) if there]
        + [pltpu.VMEM(o.shape, o.dtype) for o, there in zip(outs, out_far) if there]
        + list(scratch)
        + [pltpu.SemaphoreType.DMA((max(sum(out_far), 1), 8)), pltpu.SemaphoreType.DMA((max(sum(is_far), 1),))],
        compiler_params=params(mib),
        cost_estimate=cost(us),
        name=name,
    )(*map(placed, args), *map(placed, after))


def norm_rows(values):
    center = values - jnp.mean(values, axis=-1, keepdims=True)
    spread = jnp.mean(center * center, axis=-1, keepdims=True)
    rate = lax.rsqrt(spread + EPSILON)
    return center * rate, rate


def norm_back(hat, rate, gain, grad):
    scaled = grad * gain
    mean_one = jnp.mean(scaled, axis=-1, keepdims=True)
    mean_two = jnp.mean(scaled * hat, axis=-1, keepdims=True)
    return rate * (scaled - mean_one - hat * mean_two)


def route_kernel(capacity, experts, picks_ref, ranks_ref, spread_ref, target_ref, count_ref):
    count = picks_ref.shape[1]
    slots_all = experts * capacity
    span = 1 << (2 * count - 1).bit_length()
    picks = picks_ref[...].astype(F32)
    base = picks * span
    order = base + ranks_ref[...].astype(F32)
    padded = jnp.concatenate([picks, order, jnp.zeros((4, count), F32)], axis=0)
    turned = jnp.transpose(padded)
    targets = []
    for j in range(2):
        row = order[j : j + 1]
        floor = base[j : j + 1]
        slot = jnp.zeros((1, count), F32)
        for other in range(2):
            column = turned[:, 2 + other : 3 + other]
            ahead = (column < row) & (column >= floor)
            slot = slot + jnp.sum(jnp.where(ahead, 1.0, 0.0), axis=0, keepdims=True)
        kept = slot < capacity
        targets.append(jnp.where(kept, picks[j : j + 1] * capacity + slot, float(slots_all)))
    target_turned = jnp.transpose(jnp.concatenate(targets + [jnp.zeros((6, count), F32)], axis=0))
    target_ref[...] = target_turned
    lane = lax.broadcasted_iota(jnp.int32, (count, LANES), 1).astype(F32)
    kept_count = jnp.zeros((1, LANES), F32)
    all_count = jnp.zeros((1, LANES), F32)
    for j in range(2):
        named = jnp.where(turned[:, j : j + 1] == lane, 1.0, 0.0)
        live = jnp.where(target_turned[:, j : j + 1] < slots_all, 1.0, 0.0)
        all_count = all_count + jnp.sum(named, axis=0, keepdims=True)
        kept_count = kept_count + jnp.sum(named * live, axis=0, keepdims=True)
    count_ref[...] = jnp.concatenate([kept_count, all_count - kept_count, jnp.zeros((6, LANES), F32)], axis=0)
    step = 64
    for start in range(0, slots_all, step):
        index = lax.broadcasted_iota(jnp.int32, (step, count), 0).astype(F32) + float(start)
        hit = (index == targets[0]) | (index == targets[1])
        spread_ref[start : start + step, :] = jnp.where(hit, 1.0, 0.0).astype(BF16)


def head_masks(width):
    lane = lax.broadcasted_iota(jnp.int32, (1, width), 1)
    return lane < width // 2


def stack_heads(pair, low):
    zero = jnp.zeros_like(pair)
    return jnp.concatenate([jnp.where(low, pair, zero), jnp.where(low, zero, pair)], axis=0)


def attention_kernel(
    tokens_ref,
    gain_one_ref,
    shift_one_ref,
    query_w_ref,
    key_w_ref,
    value_w_ref,
    out_w_ref,
    gain_two_ref,
    shift_two_ref,
    spread_ref,
    resid_ref,
    normed_ref,
    query_ref,
    key_ref,
    value_ref,
    weight_ref,
    mixed_ref,
    sent_ref,
):
    count, width = tokens_ref.shape
    inputs = tokens_ref[...].astype(F32)
    hat, _ = norm_rows(inputs)
    normed_ref[...] = (hat * gain_one_ref[...] + shift_one_ref[...]).astype(BF16)
    normed = normed_ref[...]
    query_ref[...] = (dot(normed, query_w_ref[...]).astype(BF16).astype(F32) * (1.0 / math.sqrt(width // HEADS))).astype(BF16)
    key_ref[...] = dot(normed, key_w_ref[...]).astype(BF16)
    value_ref[...] = dot(normed, value_w_ref[...]).astype(BF16)
    pairs = HEADS // 2
    wide = width // pairs
    block = 2 * PATCHES
    low = head_masks(wide)
    row_image = (lax.broadcasted_iota(jnp.int32, (2 * block, block), 0) % block) // PATCHES
    column_image = lax.broadcasted_iota(jnp.int32, (2 * block, block), 1) // PATCHES
    bias = jnp.where(row_image == column_image, 0.0, -1e30)
    for item in range(count // block):
        rows = slice(item * block, (item + 1) * block)
        for pair in range(pairs):
            lanes = slice(pair * wide, (pair + 1) * wide)
            stacked = stack_heads(query_ref[rows, lanes], low)
            scores = dot_nt(stacked, key_ref[rows, lanes]) + bias
            powers = jnp.exp(scores - jnp.max(scores, axis=-1, keepdims=True))
            weights = (powers / jnp.sum(powers, axis=-1, keepdims=True)).astype(BF16)
            weight_ref[item, pair] = weights
            mixed = dot(weights, value_ref[rows, lanes])
            mixed_ref[rows, lanes] = jnp.where(low, mixed[:block], mixed[block:]).astype(BF16)
    resid = inputs + dot(mixed_ref[...], out_w_ref[...])
    resid_ref[...] = resid
    hat, _ = norm_rows(resid)
    second = (hat * gain_two_ref[...] + shift_two_ref[...]).astype(BF16)
    sent_ref[...] = dot(spread_ref[...], second).astype(BF16)


def dispatch_kernel(spread_ref, second_ref, sent_ref):
    sent_ref[...] = dot(spread_ref[...], second_ref[...]).astype(BF16)


def forward_kernel(experts, tile, me_ref, rows_ref, router_ref, up_bias_ref, *refs):
    ups = refs[:-5]
    hidden_ref, slope_ref, gate_ref, gates_ref, inner_s = refs[-5:]
    total = rows_ref.shape[0]
    chunk = 16
    root = math.sqrt(2.0 / math.pi)

    def project(step):
        inner_s[step % 2] = dot(rows_ref[...], ups[step][...])

    lane = lax.broadcasted_iota(jnp.int32, (total, LANES), 1)
    logits = dot_nt(rows_ref[...], router_ref[...])
    project(0)
    logits = jnp.where(lane < experts, logits, -1e30)
    powers = jnp.exp(logits - jnp.max(logits, axis=-1, keepdims=True))
    gates = powers / jnp.sum(powers, axis=-1, keepdims=True)
    gates_ref[...] = gates
    gates_ref.flush()
    gate = jnp.sum(jnp.where(lane == me_ref[0], gates, 0.0), axis=-1, keepdims=True)
    gate_ref[...] = jnp.broadcast_to(gate, (total, LANES))
    gate_ref.flush()
    for step in range(len(ups)):
        if step + 1 < len(ups):
            project(step + 1)
        lanes = slice(step * tile, (step + 1) * tile)
        bias = up_bias_ref[:, lanes]
        for start in range(0, total, chunk):
            at = slice(start, start + chunk)
            inner = inner_s[step % 2, at, :] + bias
            square = inner * inner
            half = 0.5 + 0.5 * jnp.tanh(inner * (root + (root * 0.044715) * square))
            hidden = inner * half
            slope = half + (hidden - hidden * half) * (2.0 * root + (6.0 * root * 0.044715) * square)
            hidden_ref[at, lanes] = hidden.astype(BF16)
            slope_ref[at, lanes] = slope.astype(BF16)
        hidden_ref.flush(slice(None), lanes)
        slope_ref.flush(slice(None), lanes)


def produce_kernel(hidden_ref, down_ref, down_bias_ref, gate_ref, out_ref, *refs):
    parts, total_s = refs[:-1], refs[-1]
    step = pl.program_id(0)
    made = dot(hidden_ref[...], down_ref[...])

    @pl.when(step == 0)
    def _():
        total_s[...] = made

    @pl.when(step > 0)
    def _():
        total_s[...] += made

    @pl.when(step == pl.num_programs(0) - 1)
    def _():
        produced = (total_s[...] + down_bias_ref[...]).astype(BF16)
        out_ref[...] = produced
        size = parts[0].shape[1]
        gate = jnp.concatenate([gate_ref[...]] * (size // LANES), axis=1)
        for at, ref in enumerate(parts):
            ref[...] = (produced[:, at * size : (at + 1) * size].astype(F32) * gate).astype(BF16)


def expert_kernel(experts, tile, me_ref, grad_ref, gate_ref, *refs):
    steps = (len(refs) - 8) // 3
    downs, slopes, ups = [refs[0], *refs[6 : 3 * steps + 3 : 3]], [refs[1], *refs[7 : 3 * steps + 3 : 3]], [refs[2], *refs[8 : 3 * steps + 3 : 3]]
    produced_ref, gates_ref, router_ref = refs[3:6]
    inner_grad_ref, rows_grad_ref, logit_grad_ref, back_s, total_s = refs[3 * steps + 3 :]
    total, width = grad_ref.shape
    chunk = 16

    def project(step):
        back_s[step % 2] = dot_nt(grad_ref[...], downs[step][...])

    project(0)
    for step in range(steps):
        if step + 1 < steps:
            project(step + 1)
        lanes = slice(step * tile, (step + 1) * tile)
        for start in range(0, total, chunk):
            at = slice(start, start + chunk)
            gate = jnp.concatenate([gate_ref[at, :]] * (tile // LANES), axis=1)
            made = back_s[step % 2, at, :] * gate * slopes[step][at, :].astype(F32)
            inner_grad_ref[at, lanes] = made.astype(BF16)
        inner_grad_ref.flush(slice(None), lanes)
        made = dot_nt(inner_grad_ref[:, lanes], ups[step][...])
        total_s[...] = made if step == 0 else total_s[...] + made
        if step == 0:
            lane = lax.broadcasted_iota(jnp.int32, (total, LANES), 1)
            product = grad_ref[...].astype(F32) * produced_ref[...].astype(F32)
            pair_grad = jnp.sum(product, axis=-1, keepdims=True)
            own = jnp.where(lane == me_ref[0], 1.0, 0.0)
            logit_grad = (gates_ref[...] * (own - gate_ref[...]) * pair_grad).astype(BF16)
            logit_grad_ref[...] = logit_grad
            logit_grad_ref.flush()
            total_s[...] += dot(logit_grad, router_ref[...])
    rows_grad_ref[...] = total_s[...].astype(BF16)


def weight_kernel(sets, again, *refs):
    groups, refs = [refs[at * 5 : at * 5 + 5] for at in range(sets)], refs[5 * sets :]
    extra_ref, out_ref, refs = refs[0], refs[1], refs[2:]
    router_refs, gated_s, inner_grad_s, back_s = refs[:-3], refs[-3], refs[-2], refs[-1]
    total, width = groups[0][0].shape
    chunk = 16

    @pl.when(pl.program_id(0) == 0)
    def _():
        for at, some in enumerate(groups):
            gate = jnp.concatenate([some[2][...]] * (width // LANES), axis=1)
            gated_s[at] = (gate * some[1][...].astype(F32)).astype(BF16)
        if router_refs:
            router_refs[0][...] = dot_tn(extra_ref[...], groups[0][0][...])[: router_refs[0].shape[0]]

    ones = jnp.ones((16, total), BF16)
    ups, downs, up_biases, down_biases = [], [], [], []
    for at, (rows_ref, grad_ref, gate_ref, hidden_ref, inner_grad_ref) in enumerate(groups):
        if again:
            slope_ref, inner_grad_ref = inner_grad_ref, inner_grad_s
            back_s[...] = dot_nt(grad_ref[...], extra_ref[...])
            for start in range(0, total, chunk):
                here = slice(start, start + chunk)
                gate = jnp.concatenate([gate_ref[here, :]] * (width // LANES), axis=1)
                made = back_s[here, :] * gate * slope_ref[here, :].astype(F32)
                inner_grad_s[here, :] = made.astype(BF16)
        inner_grad = inner_grad_ref[...]
        ups.append(dot_tn(rows_ref[...], inner_grad))
        downs.append(dot_tn(hidden_ref[...], gated_s[at]))
        up_biases.append(dot(ones, inner_grad))
        down_biases.append(dot(ones, gated_s[at]))
    out_ref[0, :width, :] = sum(ups[1:], ups[0]).astype(BF16)
    out_ref[0, width : 2 * width, :] = sum(downs[1:], downs[0]).astype(BF16)
    row = lax.broadcasted_iota(jnp.int32, (16, width), 0)
    small = jnp.where(row == 0, sum(up_biases[1:], up_biases[0]), sum(down_biases[1:], down_biases[0]))
    out_ref[0, 2 * width :, :] = small.astype(BF16)


def finish_experts_kernel(*refs):
    parts, (up_ref, up_bias_ref, down_ref, down_bias_ref) = refs[:4], refs[-4:]
    tall = up_ref.shape[0]

    def total(some):
        return sum_in_tree([ref[0, some, :].astype(F32) for ref in parts])

    up_ref[...] = total(slice(0, tall))
    down_ref[...] = total(slice(tall, 2 * tall))
    small = total(slice(2 * tall, None))
    up_bias_ref[...] = small[0:1]
    down_bias_ref[...] = small[1:2]


def one_hot_rows(target_ref, slots_all):
    count = target_ref.shape[0]
    lane = lax.broadcasted_iota(jnp.int32, (64, slots_all), 1).astype(F32)
    pieces = []
    for start in range(0, count, 64):
        one = target_ref[start : start + 64, 0:1]
        two = target_ref[start : start + 64, 1:2]
        pieces.append(jnp.where((lane == one) | (lane == two), 1.0, 0.0).astype(BF16))
    return jnp.concatenate(pieces, axis=0)


def combine_kernel(target_ref, resid_ref, *refs):
    parts, out_ref = refs[:-1], refs[-1]
    picked = one_hot_rows(target_ref, parts[0].shape[0])
    size = parts[0].shape[1]
    for at, ref in enumerate(parts):
        lanes = slice(at * size, (at + 1) * size)
        out_ref[:, lanes] = (resid_ref[:, lanes] + dot(picked, ref[...])).astype(BF16)


def backward_kernel(
    experts,
    core_ref,
    target_ref,
    back_ref,
    resid_ref,
    grad_ref,
    gain_two_ref,
    tokens_ref,
    gain_one_ref,
    query_w_ref,
    key_w_ref,
    value_w_ref,
    out_w_ref,
    normed_ref,
    query_ref,
    key_ref,
    value_ref,
    weight_ref,
    mixed_ref,
    count_ref,
    router_grad_ref,
    keep_ref,
    send_ref,
    tokens_grad_ref,
    queries_s,
    keys_s,
    values_s,
    mixed_grad_s,
    resid_grad_s,
):
    count, width = tokens_ref.shape
    picked = one_hot_rows(target_ref, back_ref.shape[0])
    second_grad = dot(picked, back_ref[...])
    hat, rate = norm_rows(resid_ref[...])
    gain_two_grad = jnp.sum(second_grad * hat, axis=0, keepdims=True)
    shift_two_grad = jnp.sum(second_grad, axis=0, keepdims=True)
    resid_grad_s[...] = grad_ref[...].astype(F32) + norm_back(hat, rate, gain_two_ref[...], second_grad)
    branch = resid_grad_s[...].astype(BF16)
    half = width // 2
    first = core_ref[0] == 0

    def put(at, value):
        value = value.astype(BF16)
        keep_ref[at * half : (at + 1) * half, :] = jnp.where(first, value[:half], value[half:])
        send_ref[at * half : (at + 1) * half, :] = jnp.where(first, value[half:], value[:half])
        keep_ref.flush(slice(at * half, (at + 1) * half))

    put(3, dot_tn(mixed_ref[...], branch))
    mixed_grad_s[...] = dot_nt(branch, out_w_ref[...]).astype(BF16)
    pairs = HEADS // 2
    wide = width // pairs
    block = 2 * PATCHES
    scale = 1.0 / math.sqrt(width // HEADS)
    low = head_masks(wide)
    for item in range(count // block):
        rows = slice(item * block, (item + 1) * block)
        for pair in range(pairs):
            lanes = slice(pair * wide, (pair + 1) * wide)
            mixed_stack = stack_heads(mixed_grad_s[rows, lanes], low)
            query_stack = stack_heads(query_ref[rows, lanes], low)
            weights = weight_ref[item, pair]
            weight_grad = dot_nt(mixed_stack, value_ref[rows, lanes])
            product = weights.astype(F32) * weight_grad
            score_grad = product - weights.astype(F32) * jnp.sum(product, axis=-1, keepdims=True)
            score_grad = score_grad.astype(BF16)
            values_s[rows, lanes] = dot_tn(weights, mixed_stack).astype(BF16)
            keys_s[rows, lanes] = dot_tn(score_grad, query_stack).astype(BF16)
            made = dot(score_grad, key_ref[rows, lanes]) * scale
            queries_s[rows, lanes] = jnp.where(low, made[:block], made[block:]).astype(BF16)
    normed = normed_ref[...]
    put(0, dot_tn(normed, queries_s[...]))
    put(1, dot_tn(normed, keys_s[...]))
    put(2, dot_tn(normed, values_s[...]))
    normed_grad = (
        dot_nt(queries_s[...], query_w_ref[...])
        + dot_nt(keys_s[...], key_w_ref[...])
        + dot_nt(values_s[...], value_w_ref[...])
    )
    hat, rate = norm_rows(tokens_ref[...].astype(F32))
    gain_one_grad = jnp.sum(normed_grad * hat, axis=0, keepdims=True)
    shift_one_grad = jnp.sum(normed_grad, axis=0, keepdims=True)
    tokens_grad_ref[...] = (resid_grad_s[...] + norm_back(hat, rate, gain_one_ref[...], normed_grad)).astype(BF16)
    tokens_grad_ref.flush()
    digits = []
    for kind in range(2):
        value = count_ref[kind : kind + 1, :]
        high = jnp.floor(value * (1.0 / 128.0))
        digits.append(jnp.concatenate([value - 128.0 * high, high] + [jnp.zeros_like(value)] * (width // LANES - 2), axis=1))
    extra = keep_ref.shape[0] - 4 * half
    small = [gain_one_grad, shift_one_grad, gain_two_grad, shift_two_grad] + digits + [router_grad_ref[:experts, :]]
    small = jnp.concatenate(small + [jnp.zeros((extra - 6 - experts, width), F32)], axis=0).astype(BF16)
    keep_ref[4 * half :, :] = small
    send_ref[4 * half :, :] = small
    keep_ref.flush(slice(4 * half, None))


def carry_digits(total):
    row = lax.broadcasted_iota(jnp.int32, (total.shape[0], LANES), 0)
    one, two, three = (total[:, at * LANES : (at + 1) * LANES] for at in range(3))
    over = jnp.floor(one * (1.0 / 128.0))
    two_full = two + over
    over_two = jnp.floor(two_full * (1.0 / 128.0))
    parts = [one - 128.0 * over, two_full - 128.0 * over_two, three + over_two]
    is_count = (row == 4) | (row == 5)
    parts = [jnp.where(is_count, part, total[:, at * LANES : (at + 1) * LANES]) for at, part in enumerate(parts)]
    return jnp.concatenate(parts + [total[:, 3 * LANES :]], axis=1)


def sum_in_tree(values):
    while len(values) > 1:
        values = [values[at] + values[at + 1] for at in range(0, len(values), 2)]
    return values[0]


def share_kernel(given, pieces, *refs):
    index_ref, arrived, made = refs[0], refs[1 : 1 + given], refs[1 + given :]
    small_rows = (pieces * made[0].shape[0] - arrived[0].shape[0]) // (pieces - 1)
    size = made[0].shape[0] - small_rows
    top = pieces * size
    small = carry_digits(sum_in_tree([ref[top:, :].astype(F32) for ref in arrived])).astype(BF16)
    for away in range(pieces):
        at = pl.ds(pl.multiple_of((index_ref[0] ^ away) * size, size), size)
        made[away][:size, :] = sum_in_tree([ref[at, :].astype(F32) for ref in arrived]).astype(BF16)
        made[away][size:, :] = small


def copy_kernel(given_ref, made_ref, arrival):
    copy = pltpu.make_async_copy(given_ref, made_ref, arrival)
    copy.start()
    copy.wait()


def pass_kernel(given_ref, same_ref):
    pass


def gather_kernel(*refs):
    arrived, out_ref = refs[:-1], refs[-1]
    size = arrived[0].shape[0]
    for at, ref in enumerate(arrived):
        out_ref[at * size : (at + 1) * size, :] = ref[...]


def last_kernel(given, *refs):
    arrived, chunk_ref, small_ref = refs[:given], refs[given], refs[given + 1]
    size = chunk_ref.shape[0]
    chunk_ref[...] = sum_in_tree([ref[:size, :].astype(F32) for ref in arrived]).astype(BF16)
    small_ref[...] = carry_digits(sum_in_tree([ref[size:, :].astype(F32) for ref in arrived])).astype(BF16)


def finish_shared_kernel(experts, index_ref, *refs):
    own, others, small_ref, outs = refs[:4], refs[4:8], refs[8], refs[9:]
    vector_refs, router_ref, count_ref = outs[4:8], outs[8], outs[9]
    core, place, inner_place = index_ref[0], index_ref[1], index_ref[2]
    half = outs[0].shape[1] // 2
    size = half // 4
    for pieces, side in ((own, core), (others, 1 - core)):
        for away, piece in enumerate(pieces):
            for at in range(4):

                @pl.when((place ^ away) == at)
                def _(piece=piece, side=side, out=outs[at]):
                    for part in range(4):
                        start = pl.multiple_of((inner_place ^ part) * size, size)
                        row = pl.multiple_of(side * half + part * size, size)
                        out[pl.ds(row, size), :] = piece[pl.ds(start, size), :].astype(F32)

    small = small_ref[...].astype(F32)
    for at, ref in enumerate(vector_refs):
        ref[...] = small[at : at + 1, :]
    router_ref[...] = small[6 : 6 + experts, :]
    value = small[4:6, :LANES] + 128.0 * small[4:6, LANES : 2 * LANES] + 16384.0 * small[4:6, 2 * LANES : 3 * LANES]
    count_ref[...] = value[:, :experts].astype(jnp.int32)


def solution(mesh):
    narrow, wide = mesh.shape["narrow"], mesh.shape["wide"]

    def hop(value, narrow_bits, wide_bits):
        if wide_bits == 0:
            return lax.ppermute(value, "narrow", [(i, i ^ narrow_bits) for i in range(narrow)])
        if narrow_bits == 0:
            return lax.ppermute(value, "wide", [(i, i ^ wide_bits) for i in range(wide)])
        pairs = [
            (i * wide + j, (i ^ narrow_bits) * wide + (j ^ wide_bits)) for i in range(narrow) for j in range(wide)
        ]
        return lax.ppermute(value, ("narrow", "wide"), pairs)

    def body(
        tokens,
        gain_one,
        shift_one,
        query_w,
        key_w,
        value_w,
        out_w,
        gain_two,
        shift_two,
        router_w,
        up_w,
        up_bias,
        down_w,
        down_bias,
        picks,
        ranks,
        out_grad,
    ):
        count, width = tokens.shape
        experts = router_w.shape[1]
        capacity = ((21 * 2 * count + 20 * experts - 1) // (20 * experts) + 7) // 8 * 8
        slots_all = experts * capacity
        hidden_width = up_w.shape[2]
        half = width // 2
        pairs = HEADS // 2
        blocks = count // (2 * PATCHES)
        extra = (6 + experts + 15) // 16 * 16
        tile = width
        steps = hidden_width // tile
        narrow_at, wide_at = lax.axis_index("narrow"), lax.axis_index("wide")
        core = (narrow_at & 1)[None].astype(jnp.int32)
        place = (((narrow_at >> 1) & 1) * 2 + (wide_at & 1))[None].astype(jnp.int32)
        inner_place = ((wide_at >> 1) & 3)[None].astype(jnp.int32)
        gain_one, shift_one, gain_two, shift_two = (v[None, :] for v in (gain_one, shift_one, gain_two, shift_two))
        router_t = jnp.pad(router_w.T, ((0, LANES - experts), (0, 0)))
        up_w, down_w = up_w[0], down_w[0]

        def exchange(value):
            return lax.all_to_all(value, "wide", split_axis=0, concat_axis=0, tiled=True)

        token_rows = shape((count, width), BF16)
        rows_shape = shape((slots_all, width), BF16)
        lanes_shape = shape((slots_all, LANES), F32)
        spread, target, counts = run(
            functools.partial(route_kernel, capacity, experts),
            (picks.T, ranks.T),
            (shape((slots_all, count), BF16), shape((count, 8), F32), shape((8, LANES), F32)),
            24,
            3,
            "route",
        )
        resid, normed, queries, keys, values, weights, mixed, sent = run(
            attention_kernel,
            (tokens, gain_one, shift_one, query_w, key_w, value_w, out_w, gain_two, shift_two, spread),
            (shape((count, width), F32),)
            + (token_rows,) * 4
            + (shape((blocks, pairs, 4 * PATCHES, 2 * PATCHES), BF16), token_rows, rows_shape),
            40,
            10,
            "attention",
        )
        rows = exchange(sent)
        (grad_sent,) = run(dispatch_kernel, (spread, out_grad), (rows_shape,), 16, 1, "dispatch", after=(sent,))
        grad_rows = exchange(grad_sent)

        whole = pl.BlockSpec((slots_all, width), lambda f: (0, 0))
        lanes_whole = pl.BlockSpec((slots_all, LANES), lambda f: (0, 0))
        columns = pl.BlockSpec((slots_all, tile), lambda f: (0, f))
        down_spec = pl.BlockSpec((tile, width), lambda f: (f, 0))
        down_bias_spec = pl.BlockSpec((1, width), lambda f: (0, 0))
        payload = 2 * width + 16
        me = wide_at[None].astype(jnp.int32)
        rows = Held(rows)

        def forward(rows, us, after=()):
            return fuse(
                functools.partial(forward_kernel, experts, tile),
                (me, rows, router_t, up_bias) + tuple(Part(up_w, tile, at) for at in range(steps)),
                (far((slots_all, hidden_width), BF16),) * 2 + (far((slots_all, LANES), F32),) * 2,
                32,
                us,
                "forward",
                (pltpu.VMEM((2, slots_all, tile), F32),),
                after=after,
            )

        hidden, slope, gate, gates = forward(rows, 0.01)
        produced, gated = run(
            produce_kernel,
            (hidden, down_w, down_bias, gate),
            (rows_shape,) * 2,
            32,
            0.01,
            "produce",
            (pltpu.VMEM((slots_all, width), F32),),
            grid=(steps,),
            in_specs=(columns, down_spec, down_bias_spec, lanes_whole),
            out_specs=(whole,) * 2,
        )
        grad_rows = Held(grad_rows)

        def triple(at):
            return Part(down_w, tile, at, rows=True), Part(slope, tile, at), Part(up_w, tile, at)

        rows_others = [hop(rows.value, bits, 0) for bits in range(2, narrow, 2)]
        inner_grad, rows_grad, logit_grad = fuse(
            functools.partial(expert_kernel, experts, tile),
            (me, grad_rows, gate, *triple(0), produced, gates, router_t, *(part for at in range(1, steps) for part in triple(at))),
            (far((slots_all, hidden_width), BF16), held((slots_all, width), BF16), far((slots_all, LANES), BF16)),
            32,
            0.01,
            "experts",
            (pltpu.VMEM((2, slots_all, tile), F32), pltpu.VMEM((slots_all, width), F32)),
            after=[Held(one) for one in rows_others],
        )
        back = exchange(rows_grad)

        def payload_of(number):
            return shape((number, payload, width), BF16)

        payload_spec = pl.BlockSpec((1, payload, width), lambda f: (f, 0, 0))
        router_spec = pl.BlockSpec((experts, width), lambda f: (0, 0))
        (grad_later,) = run(
            copy_kernel,
            (grad_rows,),
            (rows_shape,),
            4,
            0.01,
            "copy_rows",
            (pltpu.SemaphoreType.DMA,),
            in_specs=(pl.BlockSpec(memory_space=pl.ANY),),
            out_specs=(pl.BlockSpec(memory_space=pltpu.HBM),),
            after=(produced,),
        )

        def held_back(value, after, space=pltpu.HBM):
            return run(
                pass_kernel,
                (value if space == pltpu.HBM else Held(value),),
                (value,),
                1,
                0.01,
                "pass",
                in_specs=(pl.BlockSpec(memory_space=space),),
                out_specs=(pl.BlockSpec(memory_space=space),),
                after=after,
                free=space != pltpu.HBM,
                input_output_aliases={0: 0},
            )[0]

        sets = []
        for bits, rows_of in zip(range(2, narrow, 2), rows_others):
            grad_of = hop(grad_later, bits, 0)
            hidden_of, slope_of, gate_of, _ = forward(rows_of, 0.01, (logit_grad,))
            sets.append((rows_of, grad_of, gate_of, hidden_of, slope_of))

        def weight_part(again, sets, extra, extra_spec, after=()):
            return run(
                functools.partial(weight_kernel, len(sets), again),
                (*(item for one in sets for item in one), extra),
                (payload_of(steps),) + (shape((experts, width), F32),) * (not again),
                48,
                0.01,
                "expert_weights",
                (
                    pltpu.VMEM((len(sets), slots_all, width), BF16),
                    pltpu.VMEM((slots_all, tile), BF16),
                    pltpu.VMEM((slots_all, tile), F32),
                ),
                grid=(steps,),
                in_specs=(*(spec for _ in sets for spec in (whole, whole, lanes_whole, columns, columns)), extra_spec),
                out_specs=(payload_spec,) + (router_spec,) * (not again),
                after=after,
            )

        def finish_experts(start, number, parts, earlier, after=()):
            spec = lambda dims, index: pl.BlockSpec(dims, lambda f: index(start + f))
            return run(
                finish_experts_kernel,
                (*parts, *earlier),
                (
                    shape((width, hidden_width), F32),
                    shape((1, hidden_width), F32),
                    shape((hidden_width, width), F32),
                    shape((1, width), F32),
                ),
                32,
                0.01,
                "finish_experts",
                grid=(number,),
                in_specs=[pl.BlockSpec((1, payload, width), lambda f: (start + f, 0, 0))] * 4
                + [pl.BlockSpec(memory_space=pltpu.HBM)] * len(earlier),
                out_specs=(
                    spec((width, tile), lambda f: (0, f)),
                    spec((1, tile), lambda f: (0, f)),
                    spec((tile, width), lambda f: (f, 0)),
                    down_bias_spec,
                ),
                after=after,
                input_output_aliases={4 + at: at for at in range(len(earlier))},
            )

        own_sum, router_part = weight_part(
            False, [(rows, grad_rows, gate, hidden, inner_grad)], logit_grad, lanes_whole, [one[4] for one in sets]
        )
        produced_back = exchange(held_back(gated, (own_sum,)))

        tall = 4 * half + extra
        keep, send, tokens_grad = fuse(
            functools.partial(backward_kernel, experts),
            (
                core,
                target,
                Held(back),
                resid,
                out_grad,
                gain_two,
                tokens,
                gain_one,
                query_w,
                key_w,
                value_w,
                out_w,
                normed,
                queries,
                keys,
                values,
                weights,
                mixed,
                counts,
                router_part,
            ),
            (far((tall, width), BF16), held((tall, width), BF16), far((count, width), BF16)),
            32,
            0.01,
            "backward",
            [pltpu.VMEM((count, width), BF16)] * 4 + [pltpu.VMEM((count, width), F32)],
            after=[own_sum] + [one[1] for one in sets],
        )

        def share(index, arrived, after=()):
            size = (arrived[0].shape[0] - extra) // 4
            return run(
                functools.partial(share_kernel, len(arrived), 4),
                (index, arrived[0] if size == half else Held(arrived[0]), *map(Held, arrived[1:])),
                (shape((size + extra, width), BF16),) * 4,
                16,
                0.05,
                "share",
                after=after,
                free=True,
            )

        def last(arrived, after=()):
            return run(
                functools.partial(last_kernel, len(arrived)),
                tuple(map(Held, arrived)),
                (shape((half // 4, width), BF16), shape((extra, width), BF16)),
                16,
                0.05,
                "last",
                after=after,
                free=True,
            )

        def gather(arrived, after=()):
            rows_in = sum(value.shape[0] for value in arrived)
            return run(
                gather_kernel,
                tuple(map(Held, arrived)),
                (shape((rows_in, width), BF16),),
                16,
                0.05,
                "gather",
                after=after,
                free=True,
            )[0]

        def spread_out(parts, bits):
            return [parts[0]] + [hop(part, *bit) for part, bit in zip(parts[1:], bits[1:])]

        places = ((0, 0), (0, 1), (2, 0), (2, 1))
        inner_places = ((0, 0), (0, 2), (0, 4), (0, 6))
        parts = share(place, [keep, hop(send, 1, 0)])
        (far_sum,) = weight_part(True, sets, down_w, down_spec, (Held(parts[0]),))
        parts = share(inner_place, spread_out(parts, places), (far_sum, Held(produced_back)))
        far_sum = held_back(far_sum, (Held(parts[0]),))
        parts = spread_out(parts, inner_places)
        (block_out,) = run(
            combine_kernel, (target, resid, Held(produced_back)), (token_rows,), 16, 0.01, "combine"
        )
        chunk, small = last(parts, (block_out,))
        others = [(bit, 0) for bit in (4, 8, 16, 32, 64) if bit < narrow]
        others += [(0, bit) for bit in (8, 16, 32, 64) if bit < wide]
        for bits in others:
            joined = jnp.concatenate([chunk, small], axis=0)
            chunk, small = last([joined, hop(joined, *bits)])
        sums = (own_sum, far_sum, Held(hop(own_sum, 1, 0)), Held(hop(far_sum, 1, 0)))
        finished = finish_experts(0, steps // 2, sums, (), (Held(chunk),))
        chunk = gather(spread_out([chunk] * 4, inner_places), (finished[0],))
        pieces = spread_out([chunk] * 4, places)
        finished = finish_experts(steps // 2, steps - steps // 2, sums, finished, (Held(chunk),))
        pieces[3] = held_back(pieces[3], finished[:1], pl.ANY)
        up_grad, up_bias_grad, down_grad, down_bias_grad = finished
        outs = run(
            functools.partial(finish_shared_kernel, experts),
            (
                jnp.concatenate([core, place, inner_place]),
                *map(Held, pieces),
                *(Held(hop(piece, 1, 0)) for piece in pieces),
                Held(small),
            ),
            (shape((width, width), F32),) * 4
            + (shape((1, width), F32),) * 4
            + (shape((experts, width), F32), shape((2, experts), jnp.int32)),
            32,
            3,
            "finish_shared",
        )
        query_grad, key_grad, value_grad, out_w_grad, g_one, s_one, g_two, s_two, router_grad, tallies = outs
        return (
            block_out,
            tokens_grad,
            g_one[0],
            s_one[0],
            query_grad,
            key_grad,
            value_grad,
            out_w_grad,
            g_two[0],
            s_two[0],
            router_grad.T,
            up_grad[None],
            up_bias_grad,
            down_grad[None],
            down_bias_grad,
            tallies.T,
        )

    tokens_spec = P(("narrow", "wide"), None)
    in_specs = (
        (tokens_spec,)
        + (P(),) * 9
        + (P("wide", None, None), P("wide", None), P("wide", None, None), P("wide", None))
        + (tokens_spec,) * 3
    )
    out_specs = (
        (tokens_spec,) * 2
        + (P(),) * 9
        + (P("wide", None, None), P("wide", None), P("wide", None, None), P("wide", None))
        + (P(),)
    )
    return jax.shard_map(body, mesh=mesh, in_specs=in_specs, out_specs=out_specs, check_vma=False)
```

```python
import functools
import math

import jax
import jax.numpy as jnp
from jax import lax
from jax.experimental import pallas as pl
from jax.experimental.pallas import tpu as pltpu
from jax.sharding import PartitionSpec as P

HEADS = 8
PATCHES = 48
EPSILON = 1e-06
LANES = 128
MIB = 1 << 20
F32 = jnp.float32
BF16 = jnp.bfloat16

VMEM = functools.partial(pl.BlockSpec, memory_space=pltpu.VMEM)
SMEM = functools.partial(pl.BlockSpec, memory_space=pltpu.SMEM)


def shape(dims, dtype):
    return jax.ShapeDtypeStruct(dims, dtype)


def dot(a, b):
    return jnp.dot(a, b, preferred_element_type=F32)


def dot_nt(a, b):
    return lax.dot_general(a, b, (((1,), (1,)), ((), ())), preferred_element_type=F32)


def dot_tn(a, b):
    return lax.dot_general(a, b, (((0,), (0,)), ((), ())), preferred_element_type=F32)


def params(mib):
    return pltpu.CompilerParams(vmem_limit_bytes=mib * MIB)


def cost(us):
    return pl.CostEstimate(flops=int(us * 1.0e9), bytes_accessed=int(us * 1.0e5), transcendentals=0)


class Held:
    def __init__(self, value):
        self.value = value
        self.shape, self.dtype, self.ndim = value.shape, value.dtype, value.ndim


def placed(value):
    if isinstance(value, Held):
        return value.value
    if isinstance(value, Part):
        value = value.value
    return value if value.ndim == 1 else pltpu.with_memory_space_constraint(value, pltpu.HBM)


def whole_spec(dims):
    return pl.BlockSpec(tuple(dims), lambda *_: (0,) * len(dims))


def held(dims, dtype):
    return pltpu.VMEM(tuple(dims), dtype)


def far(dims, dtype):
    return pltpu.HBM(tuple(dims), dtype)


def loose(value):
    return pl.BlockSpec(memory_space=pl.ANY if isinstance(value, Held) else pltpu.HBM)


def run(kernel, args, outs, mib, us, name, scratch=(), after=(), grid=(1,), in_specs=None, out_specs=None, free=False, **more):
    given = len(args)
    if in_specs is None:
        in_specs = [SMEM() if a.ndim == 1 else whole_spec(a.shape) for a in args]
    if out_specs is None:
        out_specs = [whole_spec(o.shape) for o in outs]

    def body(*refs):
        kernel(*refs[:given], *refs[given + len(after) :])

    return pl.pallas_call(
        body,
        grid=grid,
        in_specs=list(in_specs) + [loose(value) for value in after],
        out_specs=tuple(out_specs),
        out_shape=tuple(shape(o.shape, o.dtype) if free else far(o.shape, o.dtype) for o in outs),
        scratch_shapes=list(scratch),
        compiler_params=params(mib),
        cost_estimate=cost(us),
        name=name,
        **more,
    )(*map(placed, args), *map(placed, after))


class Part:
    def __init__(self, value, tile, at, rows=False):
        some, all_of = slice(at * tile, (at + 1) * tile), slice(None)
        self.value, self.index = value, (some, all_of) if rows else (all_of, some)
        self.shape = (tile, value.shape[1]) if rows else (value.shape[0], tile)
        self.dtype, self.ndim = value.dtype, 2


class Arriving:
    def __init__(self, source, target, semaphore):
        self.target, self.shape = target, target.shape
        self.copy = pltpu.make_async_copy(source, target, semaphore)
        self.copy.start()
        self.here = False

    def wait(self):
        if not self.here:
            self.copy.wait()
            self.here = True

    def __getitem__(self, index):
        self.wait()
        return self.target[index]


class Leaving:
    def __init__(self, source, target, semaphores):
        self.source, self.target, self.semaphores = source, target, semaphores
        self.shape = source.shape
        self.copies = []

    def __getitem__(self, index):
        return self.source[index]

    def __setitem__(self, index, value):
        self.source[index] = value

    def flush(self, *index):
        one, two = (self.source.at[index], self.target.at[index]) if index else (self.source, self.target)
        self.copies.append(pltpu.make_async_copy(one, two, self.semaphores.at[len(self.copies)]))
        self.copies[-1].start()

    def wait(self):
        for copy in self.copies:
            copy.wait()


def fuse(kernel, args, outs, mib, us, name, scratch=(), after=()):
    is_far = [not isinstance(a, Held) and a.ndim > 1 for a in args]
    out_far = [o.memory_space == pltpu.HBM for o in outs]
    given, made = len(args), len(outs)

    def body(*refs):
        ins, refs = list(refs[:given]), refs[given + len(after) :]
        results, refs = list(refs[:made]), list(refs[made:])
        arrivals, departures = refs.pop(), refs.pop()
        coming, going = [], []
        for at in range(given):
            if is_far[at]:
                source = ins[at].at[args[at].index] if isinstance(args[at], Part) else ins[at]
                ins[at] = Arriving(source, refs.pop(0), arrivals.at[len(coming)])
                coming.append(ins[at])
        for at in range(made):
            if out_far[at]:
                results[at] = Leaving(refs.pop(0), results[at], departures.at[len(going)])
                going.append(results[at])
        kernel(*ins, *results, *refs)
        for item in coming + going:
            item.wait()

    def spec(value):
        if isinstance(value, Held):
            return VMEM()
        return SMEM() if value.ndim == 1 else pl.BlockSpec(memory_space=pltpu.HBM)

    return pl.pallas_call(
        body,
        in_specs=[spec(a) for a in args] + [loose(value) for value in after],
        out_specs=tuple(pl.BlockSpec(memory_space=o.memory_space) for o in outs),
        out_shape=tuple(outs),
        scratch_shapes=[pltpu.VMEM(a.shape, a.dtype) for a, there in zip(args, is_far) if there]
        + [pltpu.VMEM(o.shape, o.dtype) for o, there in zip(outs, out_far) if there]
        + list(scratch)
        + [pltpu.SemaphoreType.DMA((max(sum(out_far), 1), 8)), pltpu.SemaphoreType.DMA((max(sum(is_far), 1),))],
        compiler_params=params(mib),
        cost_estimate=cost(us),
        name=name,
    )(*map(placed, args), *map(placed, after))


def norm_rows(values):
    center = values - jnp.mean(values, axis=-1, keepdims=True)
    spread = jnp.mean(center * center, axis=-1, keepdims=True)
    rate = lax.rsqrt(spread + EPSILON)
    return center * rate, rate


def norm_back(hat, rate, gain, grad):
    scaled = grad * gain
    mean_one = jnp.mean(scaled, axis=-1, keepdims=True)
    mean_two = jnp.mean(scaled * hat, axis=-1, keepdims=True)
    return rate * (scaled - mean_one - hat * mean_two)


def route(capacity, experts, picks_ref, ranks_ref, spread_ref, target_ref, count_ref):
    count = picks_ref.shape[1]
    slots_all = experts * capacity
    span = 1 << (2 * count - 1).bit_length()
    picks = picks_ref[...].astype(F32)
    base = picks * span
    order = base + ranks_ref[...].astype(F32)
    padded = jnp.concatenate([picks, order, jnp.zeros((4, count), F32)], axis=0)
    turned = jnp.transpose(padded)
    targets = []
    for j in range(2):
        row = order[j : j + 1]
        floor = base[j : j + 1]
        slot = jnp.zeros((1, count), F32)
        for other in range(2):
            column = turned[:, 2 + other : 3 + other]
            ahead = (column < row) & (column >= floor)
            slot = slot + jnp.sum(jnp.where(ahead, 1.0, 0.0), axis=0, keepdims=True)
        kept = slot < capacity
        targets.append(jnp.where(kept, picks[j : j + 1] * capacity + slot, float(slots_all)))
    target_turned = jnp.transpose(jnp.concatenate(targets + [jnp.zeros((6, count), F32)], axis=0))
    target_ref[...] = target_turned
    lane = lax.broadcasted_iota(jnp.int32, (count, LANES), 1).astype(F32)
    kept_count = jnp.zeros((1, LANES), F32)
    all_count = jnp.zeros((1, LANES), F32)
    for j in range(2):
        named = jnp.where(turned[:, j : j + 1] == lane, 1.0, 0.0)
        live = jnp.where(target_turned[:, j : j + 1] < slots_all, 1.0, 0.0)
        all_count = all_count + jnp.sum(named, axis=0, keepdims=True)
        kept_count = kept_count + jnp.sum(named * live, axis=0, keepdims=True)
    count_ref[...] = jnp.concatenate([kept_count, all_count - kept_count, jnp.zeros((6, LANES), F32)], axis=0)
    step = 64
    for start in range(0, slots_all, step):
        index = lax.broadcasted_iota(jnp.int32, (step, count), 0).astype(F32) + float(start)
        hit = (index == targets[0]) | (index == targets[1])
        spread_ref[start : start + step, :] = jnp.where(hit, 1.0, 0.0).astype(BF16)


def head_masks(width):
    lane = lax.broadcasted_iota(jnp.int32, (1, width), 1)
    return lane < width // 2


def stack_heads(pair, low):
    zero = jnp.zeros_like(pair)
    return jnp.concatenate([jnp.where(low, pair, zero), jnp.where(low, zero, pair)], axis=0)


def attention_kernel(
    capacity,
    experts,
    tokens_ref,
    gain_one_ref,
    shift_one_ref,
    picks_ref,
    ranks_ref,
    query_w_ref,
    key_w_ref,
    value_w_ref,
    out_w_ref,
    gain_two_ref,
    shift_two_ref,
    spread_ref,
    target_ref,
    count_ref,
    resid_ref,
    normed_ref,
    query_ref,
    key_ref,
    value_ref,
    weight_ref,
    mixed_ref,
    sent_ref,
):
    count, width = tokens_ref.shape
    inputs = tokens_ref[...].astype(F32)
    hat, _ = norm_rows(inputs)
    normed_ref[...] = (hat * gain_one_ref[...] + shift_one_ref[...]).astype(BF16)
    normed_ref.flush()
    route(capacity, experts, picks_ref, ranks_ref, spread_ref, target_ref, count_ref)
    spread_ref.flush()
    target_ref.flush()
    count_ref.flush()
    normed = normed_ref[...]
    scale = 1.0 / math.sqrt(width // HEADS)
    query_ref[...] = (dot(normed, query_w_ref[...]).astype(BF16).astype(F32) * scale).astype(BF16)
    query_ref.flush()
    key_ref[...] = dot(normed, key_w_ref[...]).astype(BF16)
    key_ref.flush()
    value_ref[...] = dot(normed, value_w_ref[...]).astype(BF16)
    value_ref.flush()
    pairs = HEADS // 2
    wide = width // pairs
    block = 2 * PATCHES
    low = head_masks(wide)
    row_image = (lax.broadcasted_iota(jnp.int32, (2 * block, block), 0) % block) // PATCHES
    column_image = lax.broadcasted_iota(jnp.int32, (2 * block, block), 1) // PATCHES
    bias = jnp.where(row_image == column_image, 0.0, -1e30)
    together = 8
    cells = [(item, pair) for item in range(count // block) for pair in range(pairs)]
    for start in range(0, len(cells), together):
        work = []
        for item, pair in cells[start : start + together]:
            rows = slice(item * block, (item + 1) * block)
            lanes = slice(pair * wide, (pair + 1) * wide)
            scores = dot_nt(stack_heads(query_ref[rows, lanes], low), key_ref[rows, lanes]) + bias
            work.append((rows, lanes, scores))
        tops = [jnp.max(scores, axis=-1, keepdims=True) for _, _, scores in work]
        powers = [jnp.exp(scores - top) for (_, _, scores), top in zip(work, tops)]
        totals = [jnp.sum(power, axis=-1, keepdims=True) for power in powers]
        lows = [(power / total).astype(BF16) for power, total in zip(powers, totals)]
        for (item, pair), weights in zip(cells[start : start + together], lows):
            weight_ref[item, pair] = weights
        for (rows, lanes, _), weights in zip(work, lows):
            mixed = dot(weights, value_ref[rows, lanes])
            mixed_ref[rows, lanes] = jnp.where(low, mixed[:block], mixed[block:]).astype(BF16)
    weight_ref.flush()
    mixed_ref.flush()
    resid = inputs + dot(mixed_ref[...], out_w_ref[...])
    resid_ref[...] = resid
    resid_ref.flush()
    hat, _ = norm_rows(resid)
    second = (hat * gain_two_ref[...] + shift_two_ref[...]).astype(BF16)
    sent_ref[...] = dot(spread_ref[...], second).astype(BF16)


def dispatch_kernel(spread_ref, second_ref, sent_ref):
    sent_ref[...] = dot(spread_ref[...], second_ref[...]).astype(BF16)


def forward_kernel(experts, tile, me_ref, rows_ref, router_ref, up_bias_ref, *refs):
    ups = refs[:-5]
    hidden_ref, slope_ref, gate_ref, gates_ref, inner_s = refs[-5:]
    total = rows_ref.shape[0]
    chunk = 16
    root = math.sqrt(2.0 / math.pi)

    def project(step):
        inner_s[step % 2] = dot(rows_ref[...], ups[step][...])

    lane = lax.broadcasted_iota(jnp.int32, (total, LANES), 1)
    logits = dot_nt(rows_ref[...], router_ref[...])
    project(0)
    logits = jnp.where(lane < experts, logits, -1e30)
    powers = jnp.exp(logits - jnp.max(logits, axis=-1, keepdims=True))
    gates = powers / jnp.sum(powers, axis=-1, keepdims=True)
    gates_ref[...] = gates
    gates_ref.flush()
    gate = jnp.sum(jnp.where(lane == me_ref[0], gates, 0.0), axis=-1, keepdims=True)
    gate_ref[...] = jnp.broadcast_to(gate, (total, LANES))
    gate_ref.flush()
    for step in range(len(ups)):
        if step + 1 < len(ups):
            project(step + 1)
        lanes = slice(step * tile, (step + 1) * tile)
        bias = up_bias_ref[:, lanes]
        for start in range(0, total, chunk):
            at = slice(start, start + chunk)
            inner = inner_s[step % 2, at, :] + bias
            square = inner * inner
            half = 0.5 + 0.5 * jnp.tanh(inner * (root + (root * 0.044715) * square))
            hidden = inner * half
            slope = half + (hidden - hidden * half) * (2.0 * root + (6.0 * root * 0.044715) * square)
            hidden_ref[at, lanes] = hidden.astype(BF16)
            slope_ref[at, lanes] = slope.astype(BF16)
        hidden_ref.flush(slice(None), lanes)
        slope_ref.flush(slice(None), lanes)


def produce_kernel(hidden_ref, down_ref, down_bias_ref, gate_ref, out_ref, *refs):
    parts, total_s = refs[:-1], refs[-1]
    step = pl.program_id(0)
    made = dot(hidden_ref[...], down_ref[...])

    @pl.when(step == 0)
    def _():
        total_s[...] = made

    @pl.when(step > 0)
    def _():
        total_s[...] += made

    @pl.when(step == pl.num_programs(0) - 1)
    def _():
        produced = (total_s[...] + down_bias_ref[...]).astype(BF16)
        out_ref[...] = produced
        size = parts[0].shape[1]
        gate = jnp.concatenate([gate_ref[...]] * (size // LANES), axis=1)
        for at, ref in enumerate(parts):
            ref[...] = (produced[:, at * size : (at + 1) * size].astype(F32) * gate).astype(BF16)


def expert_kernel(experts, tile, me_ref, grad_ref, gate_ref, *refs):
    steps = (len(refs) - 8) // 3
    downs, slopes, ups = [refs[0], *refs[6 : 3 * steps + 3 : 3]], [refs[1], *refs[7 : 3 * steps + 3 : 3]], [refs[2], *refs[8 : 3 * steps + 3 : 3]]
    produced_ref, gates_ref, router_ref = refs[3:6]
    inner_grad_ref, rows_grad_ref, logit_grad_ref, back_s, total_s = refs[3 * steps + 3 :]
    total, width = grad_ref.shape
    chunk = 16

    def project(step):
        back_s[step % 2] = dot_nt(grad_ref[...], downs[step][...])

    project(0)
    for step in range(steps):
        if step + 1 < steps:
            project(step + 1)
        lanes = slice(step * tile, (step + 1) * tile)
        for start in range(0, total, chunk):
            at = slice(start, start + chunk)
            gate = jnp.concatenate([gate_ref[at, :]] * (tile // LANES), axis=1)
            made = back_s[step % 2, at, :] * gate * slopes[step][at, :].astype(F32)
            inner_grad_ref[at, lanes] = made.astype(BF16)
        inner_grad_ref.flush(slice(None), lanes)
        made = dot_nt(inner_grad_ref[:, lanes], ups[step][...])
        total_s[...] = made if step == 0 else total_s[...] + made
        if step == 0:
            lane = lax.broadcasted_iota(jnp.int32, (total, LANES), 1)
            product = grad_ref[...].astype(F32) * produced_ref[...].astype(F32)
            pair_grad = jnp.sum(product, axis=-1, keepdims=True)
            own = jnp.where(lane == me_ref[0], 1.0, 0.0)
            logit_grad = (gates_ref[...] * (own - gate_ref[...]) * pair_grad).astype(BF16)
            logit_grad_ref[...] = logit_grad
            logit_grad_ref.flush()
            total_s[...] += dot(logit_grad, router_ref[...])
    rows_grad_ref[...] = total_s[...].astype(BF16)


def weight_kernel(sets, again, *refs):
    groups, refs = [refs[at * 5 : at * 5 + 5] for at in range(sets)], refs[5 * sets :]
    extra_ref, out_ref, refs = refs[0], refs[1], refs[2:]
    router_refs, gated_s, inner_grad_s, back_s = refs[:-3], refs[-3], refs[-2], refs[-1]
    total, width = groups[0][0].shape
    chunk = 16

    @pl.when(pl.program_id(0) == 0)
    def _():
        for at, some in enumerate(groups):
            gate = jnp.concatenate([some[2][...]] * (width // LANES), axis=1)
            gated_s[at] = (gate * some[1][...].astype(F32)).astype(BF16)
        if router_refs:
            router_refs[0][...] = dot_tn(extra_ref[...], groups[0][0][...])[: router_refs[0].shape[0]]

    ones = jnp.ones((16, total), BF16)
    ups, downs, up_biases, down_biases = [], [], [], []
    for at, (rows_ref, grad_ref, gate_ref, hidden_ref, inner_grad_ref) in enumerate(groups):
        if again:
            slope_ref, inner_grad_ref = inner_grad_ref, inner_grad_s
            back_s[...] = dot_nt(grad_ref[...], extra_ref[...])
            for start in range(0, total, chunk):
                here = slice(start, start + chunk)
                gate = jnp.concatenate([gate_ref[here, :]] * (width // LANES), axis=1)
                made = back_s[here, :] * gate * slope_ref[here, :].astype(F32)
                inner_grad_s[here, :] = made.astype(BF16)
        inner_grad = inner_grad_ref[...]
        ups.append(dot_tn(rows_ref[...], inner_grad))
        downs.append(dot_tn(hidden_ref[...], gated_s[at]))
        up_biases.append(dot(ones, inner_grad))
        down_biases.append(dot(ones, gated_s[at]))
    out_ref[0, :width, :] = sum(ups[1:], ups[0]).astype(BF16)
    out_ref[0, width : 2 * width, :] = sum(downs[1:], downs[0]).astype(BF16)
    row = lax.broadcasted_iota(jnp.int32, (16, width), 0)
    small = jnp.where(row == 0, sum(up_biases[1:], up_biases[0]), sum(down_biases[1:], down_biases[0]))
    out_ref[0, 2 * width :, :] = small.astype(BF16)


def finish_experts_kernel(*refs):
    parts, (up_ref, up_bias_ref, down_ref, down_bias_ref) = refs[:4], refs[-4:]
    tall = up_ref.shape[0]

    def total(some):
        return sum_in_tree([ref[0, some, :].astype(F32) for ref in parts])

    up_ref[...] = total(slice(0, tall))
    down_ref[...] = total(slice(tall, 2 * tall))
    small = total(slice(2 * tall, None))
    up_bias_ref[...] = small[0:1]
    down_bias_ref[...] = small[1:2]


def one_hot_rows(target_ref, slots_all):
    count = target_ref.shape[0]
    lane = lax.broadcasted_iota(jnp.int32, (64, slots_all), 1).astype(F32)
    pieces = []
    for start in range(0, count, 64):
        one = target_ref[start : start + 64, 0:1]
        two = target_ref[start : start + 64, 1:2]
        pieces.append(jnp.where((lane == one) | (lane == two), 1.0, 0.0).astype(BF16))
    return jnp.concatenate(pieces, axis=0)


def combine_kernel(target_ref, resid_ref, *refs):
    parts, out_ref = refs[:-1], refs[-1]
    picked = one_hot_rows(target_ref, parts[0].shape[0])
    size = parts[0].shape[1]
    for at, ref in enumerate(parts):
        lanes = slice(at * size, (at + 1) * size)
        out_ref[:, lanes] = (resid_ref[:, lanes] + dot(picked, ref[...])).astype(BF16)


def backward_kernel(
    experts,
    core_ref,
    back_ref,
    target_ref,
    resid_ref,
    gain_two_ref,
    grad_ref,
    mixed_ref,
    out_w_ref,
    value_ref,
    query_ref,
    weight_ref,
    key_ref,
    normed_ref,
    query_w_ref,
    key_w_ref,
    value_w_ref,
    tokens_ref,
    gain_one_ref,
    count_ref,
    router_grad_ref,
    keep_ref,
    send_ref,
    tokens_grad_ref,
    queries_s,
    keys_s,
    values_s,
    mixed_grad_s,
    resid_grad_s,
):
    count, width = grad_ref.shape
    picked = one_hot_rows(target_ref, back_ref.shape[0])
    second_grad = dot(picked, back_ref[...])
    hat, rate = norm_rows(resid_ref[...])
    gain_two_grad = jnp.sum(second_grad * hat, axis=0, keepdims=True)
    shift_two_grad = jnp.sum(second_grad, axis=0, keepdims=True)
    resid_grad_s[...] = grad_ref[...].astype(F32) + norm_back(hat, rate, gain_two_ref[...], second_grad)
    branch = resid_grad_s[...].astype(BF16)
    half = width // 2
    first = core_ref[0] == 0

    def put(at, value):
        value = value.astype(BF16)
        keep_ref[at * half : (at + 1) * half, :] = jnp.where(first, value[:half], value[half:])
        send_ref[at * half : (at + 1) * half, :] = jnp.where(first, value[half:], value[:half])
        keep_ref.flush(slice(at * half, (at + 1) * half))

    put(3, dot_tn(mixed_ref[...], branch))
    mixed_grad_s[...] = dot_nt(branch, out_w_ref[...]).astype(BF16)
    pairs = HEADS // 2
    wide = width // pairs
    block = 2 * PATCHES
    scale = 1.0 / math.sqrt(width // HEADS)
    low = head_masks(wide)
    together = 8
    cells = [(item, pair) for item in range(count // block) for pair in range(pairs)]
    for start in range(0, len(cells), together):
        work = []
        for item, pair in cells[start : start + together]:
            rows = slice(item * block, (item + 1) * block)
            lanes = slice(pair * wide, (pair + 1) * wide)
            mixed_stack = stack_heads(mixed_grad_s[rows, lanes], low)
            weights = weight_ref[item, pair]
            work.append((rows, lanes, mixed_stack, weights, dot_nt(mixed_stack, value_ref[rows, lanes])))
        score_grads = []
        for rows, lanes, mixed_stack, weights, weight_grad in work:
            product = weights.astype(F32) * weight_grad
            score_grad = product - weights.astype(F32) * jnp.sum(product, axis=-1, keepdims=True)
            score_grads.append(score_grad.astype(BF16))
        for rows, lanes, mixed_stack, weights, _ in work:
            values_s[rows, lanes] = dot_tn(weights, mixed_stack).astype(BF16)
        for (rows, lanes, *_), score_grad in zip(work, score_grads):
            made = dot(score_grad, key_ref[rows, lanes]) * scale
            queries_s[rows, lanes] = jnp.where(low, made[:block], made[block:]).astype(BF16)
        for (rows, lanes, *_), score_grad in zip(work, score_grads):
            keys_s[rows, lanes] = dot_tn(score_grad, stack_heads(query_ref[rows, lanes], low)).astype(BF16)
    normed = normed_ref[...]
    put(0, dot_tn(normed, queries_s[...]))
    put(1, dot_tn(normed, keys_s[...]))
    put(2, dot_tn(normed, values_s[...]))
    normed_grad = (
        dot_nt(queries_s[...], query_w_ref[...])
        + dot_nt(keys_s[...], key_w_ref[...])
        + dot_nt(values_s[...], value_w_ref[...])
    )
    hat, rate = norm_rows(tokens_ref[...].astype(F32))
    gain_one_grad = jnp.sum(normed_grad * hat, axis=0, keepdims=True)
    shift_one_grad = jnp.sum(normed_grad, axis=0, keepdims=True)
    tokens_grad_ref[...] = (resid_grad_s[...] + norm_back(hat, rate, gain_one_ref[...], normed_grad)).astype(BF16)
    tokens_grad_ref.flush()
    digits = []
    for kind in range(2):
        value = count_ref[kind : kind + 1, :]
        high = jnp.floor(value * (1.0 / 128.0))
        digits.append(jnp.concatenate([value - 128.0 * high, high] + [jnp.zeros_like(value)] * (width // LANES - 2), axis=1))
    extra = keep_ref.shape[0] - 4 * half
    small = [gain_one_grad, shift_one_grad, gain_two_grad, shift_two_grad] + digits + [router_grad_ref[:experts, :]]
    small = jnp.concatenate(small + [jnp.zeros((extra - 6 - experts, width), F32)], axis=0).astype(BF16)
    keep_ref[4 * half :, :] = small
    send_ref[4 * half :, :] = small
    keep_ref.flush(slice(4 * half, None))


def carry_digits(total):
    row = lax.broadcasted_iota(jnp.int32, (total.shape[0], LANES), 0)
    one, two, three = (total[:, at * LANES : (at + 1) * LANES] for at in range(3))
    over = jnp.floor(one * (1.0 / 128.0))
    two_full = two + over
    over_two = jnp.floor(two_full * (1.0 / 128.0))
    parts = [one - 128.0 * over, two_full - 128.0 * over_two, three + over_two]
    is_count = (row == 4) | (row == 5)
    parts = [jnp.where(is_count, part, total[:, at * LANES : (at + 1) * LANES]) for at, part in enumerate(parts)]
    return jnp.concatenate(parts + [total[:, 3 * LANES :]], axis=1)


def sum_in_tree(values):
    while len(values) > 1:
        values = [values[at] + values[at + 1] for at in range(0, len(values), 2)]
    return values[0]


def share_kernel(given, pieces, *refs):
    index_ref, arrived, made = refs[0], refs[1 : 1 + given], refs[1 + given :]
    small_rows = (pieces * made[0].shape[0] - arrived[0].shape[0]) // (pieces - 1)
    size = made[0].shape[0] - small_rows
    top = pieces * size
    small = carry_digits(sum_in_tree([ref[top:, :].astype(F32) for ref in arrived])).astype(BF16)
    for away in range(pieces):
        at = pl.ds(pl.multiple_of((index_ref[0] ^ away) * size, size), size)
        made[away][:size, :] = sum_in_tree([ref[at, :].astype(F32) for ref in arrived]).astype(BF16)
        made[away][size:, :] = small


def copy_kernel(given_ref, made_ref, arrival):
    copy = pltpu.make_async_copy(given_ref, made_ref, arrival)
    copy.start()
    copy.wait()


def pass_kernel(given_ref, same_ref):
    pass


def gather_kernel(*refs):
    arrived, out_ref = refs[:-1], refs[-1]
    size = arrived[0].shape[0]
    for at, ref in enumerate(arrived):
        out_ref[at * size : (at + 1) * size, :] = ref[...]


def last_kernel(given, *refs):
    arrived, chunk_ref, small_ref = refs[:given], refs[given], refs[given + 1]
    size = chunk_ref.shape[0]
    chunk_ref[...] = sum_in_tree([ref[:size, :].astype(F32) for ref in arrived]).astype(BF16)
    small_ref[...] = carry_digits(sum_in_tree([ref[size:, :].astype(F32) for ref in arrived])).astype(BF16)


def finish_shared_kernel(experts, index_ref, *refs):
    own, others, small_ref, outs = refs[:4], refs[4:8], refs[8], refs[9:]
    vector_refs, router_ref, count_ref = outs[4:8], outs[8], outs[9]
    core, place, inner_place = index_ref[0], index_ref[1], index_ref[2]
    half = outs[0].shape[1] // 2
    size = half // 4
    for pieces, side in ((own, core), (others, 1 - core)):
        for away, piece in enumerate(pieces):
            for at in range(4):

                @pl.when((place ^ away) == at)
                def _(piece=piece, side=side, out=outs[at]):
                    for part in range(4):
                        start = pl.multiple_of((inner_place ^ part) * size, size)
                        row = pl.multiple_of(side * half + part * size, size)
                        out[pl.ds(row, size), :] = piece[pl.ds(start, size), :].astype(F32)

    small = small_ref[...].astype(F32)
    for at, ref in enumerate(vector_refs):
        ref[...] = small[at : at + 1, :]
    router_ref[...] = small[6 : 6 + experts, :]
    value = small[4:6, :LANES] + 128.0 * small[4:6, LANES : 2 * LANES] + 16384.0 * small[4:6, 2 * LANES : 3 * LANES]
    count_ref[...] = value[:, :experts].astype(jnp.int32)


def solution(mesh):
    narrow, wide = mesh.shape["narrow"], mesh.shape["wide"]

    def hop(value, narrow_bits, wide_bits):
        if wide_bits == 0:
            return lax.ppermute(value, "narrow", [(i, i ^ narrow_bits) for i in range(narrow)])
        if narrow_bits == 0:
            return lax.ppermute(value, "wide", [(i, i ^ wide_bits) for i in range(wide)])
        pairs = [
            (i * wide + j, (i ^ narrow_bits) * wide + (j ^ wide_bits)) for i in range(narrow) for j in range(wide)
        ]
        return lax.ppermute(value, ("narrow", "wide"), pairs)

    def body(
        tokens,
        gain_one,
        shift_one,
        query_w,
        key_w,
        value_w,
        out_w,
        gain_two,
        shift_two,
        router_w,
        up_w,
        up_bias,
        down_w,
        down_bias,
        picks,
        ranks,
        out_grad,
    ):
        count, width = tokens.shape
        experts = router_w.shape[1]
        capacity = ((21 * 2 * count + 20 * experts - 1) // (20 * experts) + 7) // 8 * 8
        slots_all = experts * capacity
        hidden_width = up_w.shape[2]
        half = width // 2
        pairs = HEADS // 2
        blocks = count // (2 * PATCHES)
        extra = (6 + experts + 15) // 16 * 16
        tile = width
        steps = hidden_width // tile
        narrow_at, wide_at = lax.axis_index("narrow"), lax.axis_index("wide")
        core = (narrow_at & 1)[None].astype(jnp.int32)
        place = (((narrow_at >> 1) & 1) * 2 + (wide_at & 1))[None].astype(jnp.int32)
        inner_place = ((wide_at >> 1) & 3)[None].astype(jnp.int32)
        gain_one, shift_one, gain_two, shift_two = (v[None, :] for v in (gain_one, shift_one, gain_two, shift_two))
        router_t = jnp.pad(router_w.T, ((0, LANES - experts), (0, 0)))
        up_w, down_w = up_w[0], down_w[0]

        def exchange(value):
            return lax.all_to_all(value, "wide", split_axis=0, concat_axis=0, tiled=True)

        token_rows = shape((count, width), BF16)
        rows_shape = shape((slots_all, width), BF16)
        lanes_shape = shape((slots_all, LANES), F32)
        narrow_far = far((count, width), BF16)
        spread, target, counts, resid, normed, queries, keys, values, weights, mixed, sent = fuse(
            functools.partial(attention_kernel, capacity, experts),
            (tokens, gain_one, shift_one, picks.T, ranks.T, query_w, key_w, value_w, out_w, gain_two, shift_two),
            (
                far((slots_all, count), BF16),
                far((count, 8), F32),
                far((8, LANES), F32),
                far((count, width), F32),
                narrow_far,
                narrow_far,
                narrow_far,
                narrow_far,
                far((blocks, pairs, 4 * PATCHES, 2 * PATCHES), BF16),
                narrow_far,
                held((slots_all, width), BF16),
            ),
            32,
            10,
            "attention",
        )
        rows = exchange(sent)
        (grad_sent,) = run(dispatch_kernel, (spread, out_grad), (rows_shape,), 16, 1, "dispatch", after=(Held(sent),))
        grad_rows = exchange(grad_sent)

        whole = pl.BlockSpec((slots_all, width), lambda f: (0, 0))
        lanes_whole = pl.BlockSpec((slots_all, LANES), lambda f: (0, 0))
        columns = pl.BlockSpec((slots_all, tile), lambda f: (0, f))
        down_spec = pl.BlockSpec((tile, width), lambda f: (f, 0))
        down_bias_spec = pl.BlockSpec((1, width), lambda f: (0, 0))
        payload = 2 * width + 16
        me = wide_at[None].astype(jnp.int32)
        rows = Held(rows)

        def forward(rows, us, after=()):
            return fuse(
                functools.partial(forward_kernel, experts, tile),
                (me, rows, router_t, up_bias) + tuple(Part(up_w, tile, at) for at in range(steps)),
                (far((slots_all, hidden_width), BF16),) * 2 + (far((slots_all, LANES), F32),) * 2,
                32,
                us,
                "forward",
                (pltpu.VMEM((2, slots_all, tile), F32),),
                after=after,
            )

        hidden, slope, gate, gates = forward(rows, 0.01)
        produced, gated = run(
            produce_kernel,
            (hidden, down_w, down_bias, gate),
            (rows_shape,) * 2,
            32,
            0.01,
            "produce",
            (pltpu.VMEM((slots_all, width), F32),),
            grid=(steps,),
            in_specs=(columns, down_spec, down_bias_spec, lanes_whole),
            out_specs=(whole,) * 2,
        )
        grad_rows = Held(grad_rows)

        def triple(at):
            return Part(down_w, tile, at, rows=True), Part(slope, tile, at), Part(up_w, tile, at)

        rows_others = [hop(rows.value, bits, 0) for bits in range(2, narrow, 2)]
        inner_grad, rows_grad, logit_grad = fuse(
            functools.partial(expert_kernel, experts, tile),
            (me, grad_rows, gate, *triple(0), produced, gates, router_t, *(part for at in range(1, steps) for part in triple(at))),
            (far((slots_all, hidden_width), BF16), held((slots_all, width), BF16), far((slots_all, LANES), BF16)),
            32,
            0.01,
            "experts",
            (pltpu.VMEM((2, slots_all, tile), F32), pltpu.VMEM((slots_all, width), F32)),
            after=[Held(one) for one in rows_others],
        )
        back = exchange(rows_grad)

        def payload_of(number):
            return shape((number, payload, width), BF16)

        payload_spec = pl.BlockSpec((1, payload, width), lambda f: (f, 0, 0))
        router_spec = pl.BlockSpec((experts, width), lambda f: (0, 0))
        (grad_later,) = run(
            copy_kernel,
            (grad_rows,),
            (rows_shape,),
            4,
            0.01,
            "copy_rows",
            (pltpu.SemaphoreType.DMA,),
            in_specs=(pl.BlockSpec(memory_space=pl.ANY),),
            out_specs=(pl.BlockSpec(memory_space=pltpu.HBM),),
            after=(produced,),
        )

        def held_back(value, after, space=pltpu.HBM):
            return run(
                pass_kernel,
                (value if space == pltpu.HBM else Held(value),),
                (value,),
                1,
                0.01,
                "pass",
                in_specs=(pl.BlockSpec(memory_space=space),),
                out_specs=(pl.BlockSpec(memory_space=space),),
                after=after,
                free=space != pltpu.HBM,
                input_output_aliases={0: 0},
            )[0]

        sets = []
        for bits, rows_of in zip(range(2, narrow, 2), rows_others):
            grad_of = hop(grad_later, bits, 0)
            hidden_of, slope_of, gate_of, _ = forward(rows_of, 0.01, (logit_grad,))
            sets.append((rows_of, grad_of, gate_of, hidden_of, slope_of))

        def weight_part(again, sets, extra, extra_spec, after=()):
            return run(
                functools.partial(weight_kernel, len(sets), again),
                (*(item for one in sets for item in one), extra),
                (payload_of(steps),) + (shape((experts, width), F32),) * (not again),
                48,
                0.01,
                "expert_weights",
                (
                    pltpu.VMEM((len(sets), slots_all, width), BF16),
                    pltpu.VMEM((slots_all, tile), BF16),
                    pltpu.VMEM((slots_all, tile), F32),
                ),
                grid=(steps,),
                in_specs=(*(spec for _ in sets for spec in (whole, whole, lanes_whole, columns, columns)), extra_spec),
                out_specs=(payload_spec,) + (router_spec,) * (not again),
                after=after,
            )

        def finish_experts(start, number, parts, earlier, after=()):
            spec = lambda dims, index: pl.BlockSpec(dims, lambda f: index(start + f))
            return run(
                finish_experts_kernel,
                (*parts, *earlier),
                (
                    shape((width, hidden_width), F32),
                    shape((1, hidden_width), F32),
                    shape((hidden_width, width), F32),
                    shape((1, width), F32),
                ),
                32,
                0.01,
                "finish_experts",
                grid=(number,),
                in_specs=[pl.BlockSpec((1, payload, width), lambda f: (start + f, 0, 0))] * 4
                + [pl.BlockSpec(memory_space=pltpu.HBM)] * len(earlier),
                out_specs=(
                    spec((width, tile), lambda f: (0, f)),
                    spec((1, tile), lambda f: (0, f)),
                    spec((tile, width), lambda f: (f, 0)),
                    down_bias_spec,
                ),
                after=after,
                input_output_aliases={4 + at: at for at in range(len(earlier))},
            )

        own_sum, router_part = weight_part(
            False, [(rows, grad_rows, gate, hidden, inner_grad)], logit_grad, lanes_whole, [one[4] for one in sets]
        )
        produced_back = exchange(held_back(gated, (own_sum,)))

        tall = 4 * half + extra
        keep, send, tokens_grad = fuse(
            functools.partial(backward_kernel, experts),
            (
                core,
                Held(back),
                target,
                resid,
                gain_two,
                out_grad,
                mixed,
                out_w,
                values,
                queries,
                weights,
                keys,
                normed,
                query_w,
                key_w,
                value_w,
                tokens,
                gain_one,
                counts,
                router_part,
            ),
            (far((tall, width), BF16), held((tall, width), BF16), far((count, width), BF16)),
            32,
            0.01,
            "backward",
            [pltpu.VMEM((count, width), BF16)] * 4 + [pltpu.VMEM((count, width), F32)],
            after=[own_sum] + [one[1] for one in sets],
        )

        def share(index, arrived, after=()):
            size = (arrived[0].shape[0] - extra) // 4
            return run(
                functools.partial(share_kernel, len(arrived), 4),
                (index, arrived[0] if size == half else Held(arrived[0]), *map(Held, arrived[1:])),
                (shape((size + extra, width), BF16),) * 4,
                16,
                0.05,
                "share",
                after=after,
                free=True,
            )

        def last(arrived, after=()):
            return run(
                functools.partial(last_kernel, len(arrived)),
                tuple(map(Held, arrived)),
                (shape((half // 4, width), BF16), shape((extra, width), BF16)),
                16,
                0.05,
                "last",
                after=after,
                free=True,
            )

        def gather(arrived, after=()):
            rows_in = sum(value.shape[0] for value in arrived)
            return run(
                gather_kernel,
                tuple(map(Held, arrived)),
                (shape((rows_in, width), BF16),),
                16,
                0.05,
                "gather",
                after=after,
                free=True,
            )[0]

        def spread_out(parts, bits):
            return [parts[0]] + [hop(part, *bit) for part, bit in zip(parts[1:], bits[1:])]

        places = ((0, 0), (0, 1), (2, 0), (2, 1))
        inner_places = ((0, 0), (0, 2), (0, 4), (0, 6))
        parts = share(place, [keep, hop(send, 1, 0)])
        (far_sum,) = weight_part(True, sets, down_w, down_spec, (Held(parts[0]),))
        parts = share(inner_place, spread_out(parts, places), (far_sum, Held(produced_back)))
        far_sum = held_back(far_sum, (Held(parts[0]),))
        parts = spread_out(parts, inner_places)
        (block_out,) = run(
            combine_kernel, (target, resid, Held(produced_back)), (token_rows,), 16, 0.01, "combine"
        )
        chunk, small = last(parts, (block_out,))
        others = [(bit, 0) for bit in (4, 8, 16, 32, 64) if bit < narrow]
        others += [(0, bit) for bit in (8, 16, 32, 64) if bit < wide]
        for bits in others:
            joined = jnp.concatenate([chunk, small], axis=0)
            chunk, small = last([joined, hop(joined, *bits)])
        sums = (own_sum, far_sum, Held(hop(own_sum, 1, 0)), Held(hop(far_sum, 1, 0)))
        finished = finish_experts(0, steps // 2, sums, (), (Held(chunk),))
        chunk = gather(spread_out([chunk] * 4, inner_places), (finished[0],))
        pieces = spread_out([chunk] * 4, places)
        finished = finish_experts(steps // 2, steps - steps // 2, sums, finished, (Held(chunk),))
        pieces[3] = held_back(pieces[3], finished[:1], pl.ANY)
        up_grad, up_bias_grad, down_grad, down_bias_grad = finished
        outs = run(
            functools.partial(finish_shared_kernel, experts),
            (
                jnp.concatenate([core, place, inner_place]),
                *map(Held, pieces),
                *(Held(hop(piece, 1, 0)) for piece in pieces),
                Held(small),
            ),
            (shape((width, width), F32),) * 4
            + (shape((1, width), F32),) * 4
            + (shape((experts, width), F32), shape((2, experts), jnp.int32)),
            32,
            3,
            "finish_shared",
        )
        query_grad, key_grad, value_grad, out_w_grad, g_one, s_one, g_two, s_two, router_grad, tallies = outs
        return (
            block_out,
            tokens_grad,
            g_one[0],
            s_one[0],
            query_grad,
            key_grad,
            value_grad,
            out_w_grad,
            g_two[0],
            s_two[0],
            router_grad.T,
            up_grad[None],
            up_bias_grad,
            down_grad[None],
            down_bias_grad,
            tallies.T,
        )

    tokens_spec = P(("narrow", "wide"), None)
    in_specs = (
        (tokens_spec,)
        + (P(),) * 9
        + (P("wide", None, None), P("wide", None), P("wide", None, None), P("wide", None))
        + (tokens_spec,) * 3
    )
    out_specs = (
        (tokens_spec,) * 2
        + (P(),) * 9
        + (P("wide", None, None), P("wide", None), P("wide", None, None), P("wide", None))
        + (P(),)
    )
    return jax.shard_map(body, mesh=mesh, in_specs=in_specs, out_specs=out_specs, check_vma=False)
```

```python
import functools
import math

import jax
import jax.numpy as jnp
from jax import lax
from jax.experimental import pallas as pl
from jax.experimental.pallas import tpu as pltpu
from jax.sharding import PartitionSpec as P

HEADS = 8
PATCHES = 48
EPSILON = 1e-06
LANES = 128
MIB = 1 << 20
F32 = jnp.float32
BF16 = jnp.bfloat16

VMEM = functools.partial(pl.BlockSpec, memory_space=pltpu.VMEM)
SMEM = functools.partial(pl.BlockSpec, memory_space=pltpu.SMEM)


def shape(dims, dtype):
    return jax.ShapeDtypeStruct(dims, dtype)


def dot(a, b):
    return jnp.dot(a, b, preferred_element_type=F32)


def dot_nt(a, b):
    return lax.dot_general(a, b, (((1,), (1,)), ((), ())), preferred_element_type=F32)


def dot_tn(a, b):
    return lax.dot_general(a, b, (((0,), (0,)), ((), ())), preferred_element_type=F32)


def params(mib):
    return pltpu.CompilerParams(vmem_limit_bytes=mib * MIB)


def cost(us):
    return pl.CostEstimate(flops=int(us * 1.0e9), bytes_accessed=int(us * 1.0e5), transcendentals=0)


class Held:
    def __init__(self, value):
        self.value = value
        self.shape, self.dtype, self.ndim = value.shape, value.dtype, value.ndim


def placed(value):
    if isinstance(value, Held):
        return value.value
    if isinstance(value, Part):
        value = value.value
    return value if value.ndim == 1 else pltpu.with_memory_space_constraint(value, pltpu.HBM)


def whole_spec(dims):
    return pl.BlockSpec(tuple(dims), lambda *_: (0,) * len(dims))


def held(dims, dtype):
    return pltpu.VMEM(tuple(dims), dtype)


def far(dims, dtype):
    return pltpu.HBM(tuple(dims), dtype)


def loose(value):
    return pl.BlockSpec(memory_space=pl.ANY if isinstance(value, Held) else pltpu.HBM)


def run(kernel, args, outs, mib, us, name, scratch=(), after=(), grid=(1,), in_specs=None, out_specs=None, free=False, **more):
    given = len(args)
    if in_specs is None:
        in_specs = [SMEM() if a.ndim == 1 else whole_spec(a.shape) for a in args]
    if out_specs is None:
        out_specs = [whole_spec(o.shape) for o in outs]

    def body(*refs):
        kernel(*refs[:given], *refs[given + len(after) :])

    return pl.pallas_call(
        body,
        grid=grid,
        in_specs=list(in_specs) + [loose(value) for value in after],
        out_specs=tuple(out_specs),
        out_shape=tuple(shape(o.shape, o.dtype) if free else far(o.shape, o.dtype) for o in outs),
        scratch_shapes=list(scratch),
        compiler_params=params(mib),
        cost_estimate=cost(us),
        name=name,
        **more,
    )(*map(placed, args), *map(placed, after))


class Part:
    def __init__(self, value, tile, at, rows=False):
        some, all_of = slice(at * tile, (at + 1) * tile), slice(None)
        self.value, self.index = value, (some, all_of) if rows else (all_of, some)
        self.shape = (tile, value.shape[1]) if rows else (value.shape[0], tile)
        self.dtype, self.ndim = value.dtype, 2


class Arriving:
    def __init__(self, source, target, semaphore):
        self.target, self.shape = target, target.shape
        self.copy = pltpu.make_async_copy(source, target, semaphore)
        self.copy.start()
        self.here = False

    def wait(self):
        if not self.here:
            self.copy.wait()
            self.here = True

    def __getitem__(self, index):
        self.wait()
        return self.target[index]


class Leaving:
    def __init__(self, source, target, semaphores):
        self.source, self.target, self.semaphores = source, target, semaphores
        self.shape = source.shape
        self.copies = []

    def __getitem__(self, index):
        return self.source[index]

    def __setitem__(self, index, value):
        self.source[index] = value

    def flush(self, *index):
        one, two = (self.source.at[index], self.target.at[index]) if index else (self.source, self.target)
        self.copies.append(pltpu.make_async_copy(one, two, self.semaphores.at[len(self.copies)]))
        self.copies[-1].start()

    def wait(self):
        for copy in self.copies:
            copy.wait()


def fuse(kernel, args, outs, mib, us, name, scratch=(), after=()):
    is_far = [not isinstance(a, Held) and a.ndim > 1 for a in args]
    out_far = [o.memory_space == pltpu.HBM for o in outs]
    given, made = len(args), len(outs)

    def body(*refs):
        ins, refs = list(refs[:given]), refs[given + len(after) :]
        results, refs = list(refs[:made]), list(refs[made:])
        arrivals, departures = refs.pop(), refs.pop()
        coming, going = [], []
        for at in range(given):
            if is_far[at]:
                source = ins[at].at[args[at].index] if isinstance(args[at], Part) else ins[at]
                ins[at] = Arriving(source, refs.pop(0), arrivals.at[len(coming)])
                coming.append(ins[at])
        for at in range(made):
            if out_far[at]:
                results[at] = Leaving(refs.pop(0), results[at], departures.at[len(going)])
                going.append(results[at])
        kernel(*ins, *results, *refs)
        for item in coming + going:
            item.wait()

    def spec(value):
        if isinstance(value, Held):
            return VMEM()
        return SMEM() if value.ndim == 1 else pl.BlockSpec(memory_space=pltpu.HBM)

    return pl.pallas_call(
        body,
        in_specs=[spec(a) for a in args] + [loose(value) for value in after],
        out_specs=tuple(pl.BlockSpec(memory_space=o.memory_space) for o in outs),
        out_shape=tuple(outs),
        scratch_shapes=[pltpu.VMEM(a.shape, a.dtype) for a, there in zip(args, is_far) if there]
        + [pltpu.VMEM(o.shape, o.dtype) for o, there in zip(outs, out_far) if there]
        + list(scratch)
        + [pltpu.SemaphoreType.DMA((max(sum(out_far), 1), 8)), pltpu.SemaphoreType.DMA((max(sum(is_far), 1),))],
        compiler_params=params(mib),
        cost_estimate=cost(us),
        name=name,
    )(*map(placed, args), *map(placed, after))


def norm_rows(values):
    center = values - jnp.mean(values, axis=-1, keepdims=True)
    spread = jnp.mean(center * center, axis=-1, keepdims=True)
    rate = lax.rsqrt(spread + EPSILON)
    return center * rate, rate


def norm_back(hat, rate, gain, grad):
    scaled = grad * gain
    mean_one = jnp.mean(scaled, axis=-1, keepdims=True)
    mean_two = jnp.mean(scaled * hat, axis=-1, keepdims=True)
    return rate * (scaled - mean_one - hat * mean_two)


def route(capacity, experts, picks_ref, ranks_ref, spread_ref, target_ref, count_ref):
    count = picks_ref.shape[1]
    slots_all = experts * capacity
    span = 1 << (2 * count - 1).bit_length()
    picks = picks_ref[...].astype(F32)
    base = picks * span
    order = base + ranks_ref[...].astype(F32)
    padded = jnp.concatenate([picks, order, jnp.zeros((4, count), F32)], axis=0)
    turned = jnp.transpose(padded)
    targets = []
    for j in range(2):
        row = order[j : j + 1]
        floor = base[j : j + 1]
        slot = jnp.zeros((1, count), F32)
        for other in range(2):
            column = turned[:, 2 + other : 3 + other]
            ahead = (column < row) & (column >= floor)
            slot = slot + jnp.sum(jnp.where(ahead, 1.0, 0.0), axis=0, keepdims=True)
        kept = slot < capacity
        targets.append(jnp.where(kept, picks[j : j + 1] * capacity + slot, float(slots_all)))
    target_turned = jnp.transpose(jnp.concatenate(targets + [jnp.zeros((6, count), F32)], axis=0))
    target_ref[...] = target_turned
    lane = lax.broadcasted_iota(jnp.int32, (count, LANES), 1).astype(F32)
    kept_count = jnp.zeros((1, LANES), F32)
    all_count = jnp.zeros((1, LANES), F32)
    for j in range(2):
        named = jnp.where(turned[:, j : j + 1] == lane, 1.0, 0.0)
        live = jnp.where(target_turned[:, j : j + 1] < slots_all, 1.0, 0.0)
        all_count = all_count + jnp.sum(named, axis=0, keepdims=True)
        kept_count = kept_count + jnp.sum(named * live, axis=0, keepdims=True)
    count_ref[...] = jnp.concatenate([kept_count, all_count - kept_count, jnp.zeros((6, LANES), F32)], axis=0)
    step = 64
    for start in range(0, slots_all, step):
        index = lax.broadcasted_iota(jnp.int32, (step, count), 0).astype(F32) + float(start)
        hit = (index == targets[0]) | (index == targets[1])
        spread_ref[start : start + step, :] = jnp.where(hit, 1.0, 0.0).astype(BF16)


def head_masks(width):
    lane = lax.broadcasted_iota(jnp.int32, (1, width), 1)
    return lane < width // 2


def stack_heads(pair, low):
    zero = jnp.zeros_like(pair)
    return jnp.concatenate([jnp.where(low, pair, zero), jnp.where(low, zero, pair)], axis=0)


def attention_kernel(
    capacity,
    experts,
    tokens_ref,
    gain_one_ref,
    shift_one_ref,
    picks_ref,
    ranks_ref,
    query_w_ref,
    key_w_ref,
    value_w_ref,
    out_w_ref,
    gain_two_ref,
    shift_two_ref,
    spread_ref,
    target_ref,
    count_ref,
    resid_ref,
    normed_ref,
    query_ref,
    key_ref,
    value_ref,
    weight_ref,
    mixed_ref,
    sent_ref,
):
    count, width = tokens_ref.shape
    inputs = tokens_ref[...].astype(F32)
    hat, _ = norm_rows(inputs)
    normed_ref[...] = (hat * gain_one_ref[...] + shift_one_ref[...]).astype(BF16)
    normed_ref.flush()
    route(capacity, experts, picks_ref, ranks_ref, spread_ref, target_ref, count_ref)
    spread_ref.flush()
    target_ref.flush()
    count_ref.flush()
    normed = normed_ref[...]
    scale = 1.0 / math.sqrt(width // HEADS)
    query_ref[...] = (dot(normed, query_w_ref[...]).astype(BF16).astype(F32) * scale).astype(BF16)
    query_ref.flush()
    key_ref[...] = dot(normed, key_w_ref[...]).astype(BF16)
    key_ref.flush()
    value_ref[...] = dot(normed, value_w_ref[...]).astype(BF16)
    value_ref.flush()
    pairs = HEADS // 2
    wide = width // pairs
    block = 2 * PATCHES
    low = head_masks(wide)
    row_image = (lax.broadcasted_iota(jnp.int32, (2 * block, block), 0) % block) // PATCHES
    column_image = lax.broadcasted_iota(jnp.int32, (2 * block, block), 1) // PATCHES
    bias = jnp.where(row_image == column_image, 0.0, -1e30)
    together = 8
    cells = [(item, pair) for item in range(count // block) for pair in range(pairs)]
    for start in range(0, len(cells), together):
        work = []
        for item, pair in cells[start : start + together]:
            rows = slice(item * block, (item + 1) * block)
            lanes = slice(pair * wide, (pair + 1) * wide)
            scores = dot_nt(stack_heads(query_ref[rows, lanes], low), key_ref[rows, lanes]) + bias
            work.append((rows, lanes, scores))
        tops = [jnp.max(scores, axis=-1, keepdims=True) for _, _, scores in work]
        powers = [jnp.exp(scores - top) for (_, _, scores), top in zip(work, tops)]
        totals = [jnp.sum(power, axis=-1, keepdims=True) for power in powers]
        lows = [(power / total).astype(BF16) for power, total in zip(powers, totals)]
        for (item, pair), weights in zip(cells[start : start + together], lows):
            weight_ref[item, pair] = weights
        for (rows, lanes, _), weights in zip(work, lows):
            mixed = dot(weights, value_ref[rows, lanes])
            mixed_ref[rows, lanes] = jnp.where(low, mixed[:block], mixed[block:]).astype(BF16)
    weight_ref.flush()
    mixed_ref.flush()
    resid = inputs + dot(mixed_ref[...], out_w_ref[...])
    resid_ref[...] = resid
    resid_ref.flush()
    hat, _ = norm_rows(resid)
    second = (hat * gain_two_ref[...] + shift_two_ref[...]).astype(BF16)
    sent_ref[...] = dot(spread_ref[...], second).astype(BF16)


def dispatch_kernel(spread_ref, second_ref, sent_ref):
    sent_ref[...] = dot(spread_ref[...], second_ref[...]).astype(BF16)


def forward_kernel(experts, tile, me_ref, rows_ref, router_ref, up_bias_ref, *refs):
    ups = refs[:-5]
    hidden_ref, slope_ref, gate_ref, gates_ref, inner_s = refs[-5:]
    total = rows_ref.shape[0]
    chunk = 16
    root = math.sqrt(2.0 / math.pi)

    def project(step):
        inner_s[step % 2] = dot(rows_ref[...], ups[step][...])

    lane = lax.broadcasted_iota(jnp.int32, (total, LANES), 1)
    logits = dot_nt(rows_ref[...], router_ref[...])
    project(0)
    logits = jnp.where(lane < experts, logits, -1e30)
    powers = jnp.exp(logits - jnp.max(logits, axis=-1, keepdims=True))
    gates = powers / jnp.sum(powers, axis=-1, keepdims=True)
    gates_ref[...] = gates
    gates_ref.flush()
    gate = jnp.sum(jnp.where(lane == me_ref[0], gates, 0.0), axis=-1, keepdims=True)
    gate_ref[...] = jnp.broadcast_to(gate, (total, LANES))
    gate_ref.flush()
    for step in range(len(ups)):
        if step + 1 < len(ups):
            project(step + 1)
        lanes = slice(step * tile, (step + 1) * tile)
        bias = up_bias_ref[:, lanes]
        for start in range(0, total, chunk):
            at = slice(start, start + chunk)
            inner = inner_s[step % 2, at, :] + bias
            square = inner * inner
            half = 0.5 + 0.5 * jnp.tanh(inner * (root + (root * 0.044715) * square))
            hidden = inner * half
            slope = half + (hidden - hidden * half) * (2.0 * root + (6.0 * root * 0.044715) * square)
            hidden_ref[at, lanes] = hidden.astype(BF16)
            slope_ref[at, lanes] = slope.astype(BF16)
        hidden_ref.flush(slice(None), lanes)
        slope_ref.flush(slice(None), lanes)


def produce_kernel(hidden_ref, down_ref, down_bias_ref, gate_ref, out_ref, *refs):
    parts, total_s = refs[:-1], refs[-1]
    step = pl.program_id(0)
    made = dot(hidden_ref[...], down_ref[...])

    @pl.when(step == 0)
    def _():
        total_s[...] = made

    @pl.when(step > 0)
    def _():
        total_s[...] += made

    @pl.when(step == pl.num_programs(0) - 1)
    def _():
        produced = (total_s[...] + down_bias_ref[...]).astype(BF16)
        out_ref[...] = produced
        size = parts[0].shape[1]
        gate = jnp.concatenate([gate_ref[...]] * (size // LANES), axis=1)
        for at, ref in enumerate(parts):
            ref[...] = (produced[:, at * size : (at + 1) * size].astype(F32) * gate).astype(BF16)


def expert_kernel(experts, tile, me_ref, grad_ref, gate_ref, *refs):
    steps = (len(refs) - 6) // 3
    downs, slopes, ups = [refs[0], *refs[6 : 3 * steps + 3 : 3]], [refs[1], *refs[7 : 3 * steps + 3 : 3]], [refs[2], *refs[8 : 3 * steps + 3 : 3]]
    produced_ref, gates_ref, router_ref = refs[3:6]
    inner_grad_ref, rows_grad_ref, logit_grad_ref = refs[3 * steps + 3 :]
    total, width = grad_ref.shape
    gate = jnp.concatenate([gate_ref[...]] * (tile // LANES), axis=1)
    for step in range(steps):
        lanes = slice(step * tile, (step + 1) * tile)
        made = dot_nt(grad_ref[...], downs[step][...]) * gate * slopes[step][...].astype(F32)
        inner_grad_ref[:, lanes] = made.astype(BF16)
        inner_grad_ref.flush(slice(None), lanes)
        if step == 0:
            lane = lax.broadcasted_iota(jnp.int32, (total, LANES), 1)
            product = grad_ref[...].astype(F32) * produced_ref[...].astype(F32)
            pair_grad = jnp.sum(product, axis=-1, keepdims=True)
            own = jnp.where(lane == me_ref[0], 1.0, 0.0)
            logit_grad = (gates_ref[...] * (own - gate_ref[...]) * pair_grad).astype(BF16)
            logit_grad_ref[...] = logit_grad
            logit_grad_ref.flush()
    made = dot(logit_grad, router_ref[...])
    for step in range(steps):
        made = made + dot_nt(inner_grad_ref[:, step * tile : (step + 1) * tile], ups[step][...])
    rows_grad_ref[...] = made.astype(BF16)


def weight_kernel(sets, again, *refs):
    groups, refs = [refs[at * 5 : at * 5 + 5] for at in range(sets)], refs[5 * sets :]
    earlier, refs = refs[:again], refs[again:]
    extra_ref, out_ref, refs = refs[0], refs[1], refs[2:]
    router_refs, gated_s, inner_grad_s, back_s = refs[:-3], refs[-3], refs[-2], refs[-1]
    total, width = groups[0][0].shape
    chunk = 16

    @pl.when(pl.program_id(0) == 0)
    def _():
        for at, some in enumerate(groups):
            gate = jnp.concatenate([some[2][...]] * (width // LANES), axis=1)
            gated_s[at] = (gate * some[1][...].astype(F32)).astype(BF16)
        if router_refs:
            router_refs[0][...] = dot_tn(extra_ref[...], groups[0][0][...])[: router_refs[0].shape[0]]

    ones = jnp.ones((16, total), BF16)
    ups, downs, up_biases, down_biases = [], [], [], []
    for at, (rows_ref, grad_ref, gate_ref, hidden_ref, inner_grad_ref) in enumerate(groups):
        if again:
            slope_ref, inner_grad_ref = inner_grad_ref, inner_grad_s
            back_s[...] = dot_nt(grad_ref[...], extra_ref[...])
            for start in range(0, total, chunk):
                here = slice(start, start + chunk)
                gate = jnp.concatenate([gate_ref[here, :]] * (width // LANES), axis=1)
                made = back_s[here, :] * gate * slope_ref[here, :].astype(F32)
                inner_grad_s[here, :] = made.astype(BF16)
        inner_grad = inner_grad_ref[...]
        ups.append(dot_tn(rows_ref[...], inner_grad))
        downs.append(dot_tn(hidden_ref[...], gated_s[at]))
        up_biases.append(dot(ones, inner_grad))
        down_biases.append(dot(ones, gated_s[at]))

    def put(some, parts):
        made = sum(parts[1:], parts[0]).astype(BF16)
        if again:
            made = (made.astype(F32) + earlier[0][0, some, :].astype(F32)).astype(BF16)
        out_ref[0, some, :] = made

    put(slice(0, width), ups)
    put(slice(width, 2 * width), downs)
    row = lax.broadcasted_iota(jnp.int32, (16, width), 0)
    small = jnp.where(row == 0, sum(up_biases[1:], up_biases[0]), sum(down_biases[1:], down_biases[0]))
    put(slice(2 * width, None), [small])


def finish_experts_kernel(*refs):
    parts, (up_ref, up_bias_ref, down_ref, down_bias_ref) = refs[:2], refs[-4:]
    tall = up_ref.shape[0]

    def total(some):
        return sum_in_tree([ref[0, some, :].astype(F32) for ref in parts])

    up_ref[...] = total(slice(0, tall))
    down_ref[...] = total(slice(tall, 2 * tall))
    small = total(slice(2 * tall, None))
    up_bias_ref[...] = small[0:1]
    down_bias_ref[...] = small[1:2]


def one_hot_rows(target_ref, slots_all):
    count = target_ref.shape[0]
    lane = lax.broadcasted_iota(jnp.int32, (64, slots_all), 1).astype(F32)
    pieces = []
    for start in range(0, count, 64):
        one = target_ref[start : start + 64, 0:1]
        two = target_ref[start : start + 64, 1:2]
        pieces.append(jnp.where((lane == one) | (lane == two), 1.0, 0.0).astype(BF16))
    return jnp.concatenate(pieces, axis=0)


def combine_kernel(target_ref, resid_ref, *refs):
    parts, out_ref = refs[:-1], refs[-1]
    picked = one_hot_rows(target_ref, parts[0].shape[0])
    size = parts[0].shape[1]
    for at, ref in enumerate(parts):
        lanes = slice(at * size, (at + 1) * size)
        out_ref[:, lanes] = (resid_ref[:, lanes] + dot(picked, ref[...])).astype(BF16)


def backward_kernel(
    experts,
    core_ref,
    back_ref,
    target_ref,
    resid_ref,
    gain_two_ref,
    grad_ref,
    mixed_ref,
    out_w_ref,
    value_ref,
    query_ref,
    weight_ref,
    key_ref,
    normed_ref,
    query_w_ref,
    key_w_ref,
    value_w_ref,
    tokens_ref,
    gain_one_ref,
    count_ref,
    router_grad_ref,
    keep_ref,
    send_ref,
    tokens_grad_ref,
    queries_s,
    keys_s,
    values_s,
    mixed_grad_s,
    resid_grad_s,
):
    count, width = grad_ref.shape
    picked = one_hot_rows(target_ref, back_ref.shape[0])
    second_grad = dot(picked, back_ref[...])
    hat, rate = norm_rows(resid_ref[...])
    gain_two_grad = jnp.sum(second_grad * hat, axis=0, keepdims=True)
    shift_two_grad = jnp.sum(second_grad, axis=0, keepdims=True)
    resid_grad_s[...] = grad_ref[...].astype(F32) + norm_back(hat, rate, gain_two_ref[...], second_grad)
    branch = resid_grad_s[...].astype(BF16)
    half = width // 2
    first = core_ref[0] == 0

    def put(at, value):
        value = value.astype(BF16)
        keep_ref[at * half : (at + 1) * half, :] = jnp.where(first, value[:half], value[half:])
        send_ref[at * half : (at + 1) * half, :] = jnp.where(first, value[half:], value[:half])
        keep_ref.flush(slice(at * half, (at + 1) * half))

    put(3, dot_tn(mixed_ref[...], branch))
    mixed_grad_s[...] = dot_nt(branch, out_w_ref[...]).astype(BF16)
    pairs = HEADS // 2
    wide = width // pairs
    block = 2 * PATCHES
    scale = 1.0 / math.sqrt(width // HEADS)
    low = head_masks(wide)
    together = 8
    cells = [(item, pair) for item in range(count // block) for pair in range(pairs)]
    for start in range(0, len(cells), together):
        work = []
        for item, pair in cells[start : start + together]:
            rows = slice(item * block, (item + 1) * block)
            lanes = slice(pair * wide, (pair + 1) * wide)
            mixed_stack = stack_heads(mixed_grad_s[rows, lanes], low)
            weights = weight_ref[item, pair]
            work.append((rows, lanes, mixed_stack, weights, dot_nt(mixed_stack, value_ref[rows, lanes])))
        score_grads = []
        for rows, lanes, mixed_stack, weights, weight_grad in work:
            product = weights.astype(F32) * weight_grad
            score_grad = product - weights.astype(F32) * jnp.sum(product, axis=-1, keepdims=True)
            score_grads.append(score_grad.astype(BF16))
        for rows, lanes, mixed_stack, weights, _ in work:
            values_s[rows, lanes] = dot_tn(weights, mixed_stack).astype(BF16)
        for (rows, lanes, *_), score_grad in zip(work, score_grads):
            made = dot(score_grad, key_ref[rows, lanes]) * scale
            queries_s[rows, lanes] = jnp.where(low, made[:block], made[block:]).astype(BF16)
        for (rows, lanes, *_), score_grad in zip(work, score_grads):
            keys_s[rows, lanes] = dot_tn(score_grad, stack_heads(query_ref[rows, lanes], low)).astype(BF16)
    normed = normed_ref[...]
    put(0, dot_tn(normed, queries_s[...]))
    put(1, dot_tn(normed, keys_s[...]))
    put(2, dot_tn(normed, values_s[...]))
    normed_grad = (
        dot_nt(queries_s[...], query_w_ref[...])
        + dot_nt(keys_s[...], key_w_ref[...])
        + dot_nt(values_s[...], value_w_ref[...])
    )
    hat, rate = norm_rows(tokens_ref[...].astype(F32))
    gain_one_grad = jnp.sum(normed_grad * hat, axis=0, keepdims=True)
    shift_one_grad = jnp.sum(normed_grad, axis=0, keepdims=True)
    tokens_grad_ref[...] = (resid_grad_s[...] + norm_back(hat, rate, gain_one_ref[...], normed_grad)).astype(BF16)
    tokens_grad_ref.flush()
    digits = []
    for kind in range(2):
        value = count_ref[kind : kind + 1, :]
        high = jnp.floor(value * (1.0 / 128.0))
        digits.append(jnp.concatenate([value - 128.0 * high, high] + [jnp.zeros_like(value)] * (width // LANES - 2), axis=1))
    extra = keep_ref.shape[0] - 4 * half
    small = [gain_one_grad, shift_one_grad, gain_two_grad, shift_two_grad] + digits + [router_grad_ref[:experts, :]]
    small = jnp.concatenate(small + [jnp.zeros((extra - 6 - experts, width), F32)], axis=0).astype(BF16)
    keep_ref[4 * half :, :] = small
    send_ref[4 * half :, :] = small
    keep_ref.flush(slice(4 * half, None))


def carry_digits(total):
    row = lax.broadcasted_iota(jnp.int32, (total.shape[0], LANES), 0)
    one, two, three = (total[:, at * LANES : (at + 1) * LANES] for at in range(3))
    over = jnp.floor(one * (1.0 / 128.0))
    two_full = two + over
    over_two = jnp.floor(two_full * (1.0 / 128.0))
    parts = [one - 128.0 * over, two_full - 128.0 * over_two, three + over_two]
    is_count = (row == 4) | (row == 5)
    parts = [jnp.where(is_count, part, total[:, at * LANES : (at + 1) * LANES]) for at, part in enumerate(parts)]
    return jnp.concatenate(parts + [total[:, 3 * LANES :]], axis=1)


def sum_in_tree(values):
    while len(values) > 1:
        values = [values[at] + values[at + 1] for at in range(0, len(values), 2)]
    return values[0]


def share_kernel(given, pieces, *refs):
    index_ref, arrived, made = refs[0], refs[1 : 1 + given], refs[1 + given :]
    small_rows = (pieces * made[0].shape[0] - arrived[0].shape[0]) // (pieces - 1)
    size = made[0].shape[0] - small_rows
    top = pieces * size
    small = carry_digits(sum_in_tree([ref[top:, :].astype(F32) for ref in arrived])).astype(BF16)
    for away in range(pieces):
        at = pl.ds(pl.multiple_of((index_ref[0] ^ away) * size, size), size)
        made[away][:size, :] = sum_in_tree([ref[at, :].astype(F32) for ref in arrived]).astype(BF16)
        made[away][size:, :] = small


def copy_kernel(given_ref, made_ref, arrival):
    copy = pltpu.make_async_copy(given_ref, made_ref, arrival)
    copy.start()
    copy.wait()


def pass_kernel(given_ref, same_ref):
    pass


def gather_kernel(*refs):
    arrived, out_ref = refs[:-1], refs[-1]
    size = arrived[0].shape[0]
    for at, ref in enumerate(arrived):
        out_ref[at * size : (at + 1) * size, :] = ref[...]


def last_kernel(given, *refs):
    arrived, chunk_ref, small_ref = refs[:given], refs[given], refs[given + 1]
    size = chunk_ref.shape[0]
    chunk_ref[...] = sum_in_tree([ref[:size, :].astype(F32) for ref in arrived]).astype(BF16)
    small_ref[...] = carry_digits(sum_in_tree([ref[size:, :].astype(F32) for ref in arrived])).astype(BF16)


def finish_shared_kernel(experts, index_ref, *refs):
    own, others, small_ref, outs = refs[:4], refs[4:8], refs[8], refs[9:]
    vector_refs, router_ref, count_ref = outs[4:8], outs[8], outs[9]
    core, place, inner_place = index_ref[0], index_ref[1], index_ref[2]
    half = outs[0].shape[1] // 2
    size = half // 4
    for pieces, side in ((own, core), (others, 1 - core)):
        for away, piece in enumerate(pieces):
            for at in range(4):

                @pl.when((place ^ away) == at)
                def _(piece=piece, side=side, out=outs[at]):
                    for part in range(4):
                        start = pl.multiple_of((inner_place ^ part) * size, size)
                        row = pl.multiple_of(side * half + part * size, size)
                        out[pl.ds(row, size), :] = piece[pl.ds(start, size), :].astype(F32)

    small = small_ref[...].astype(F32)
    for at, ref in enumerate(vector_refs):
        ref[...] = small[at : at + 1, :]
    router_ref[...] = small[6 : 6 + experts, :]
    value = small[4:6, :LANES] + 128.0 * small[4:6, LANES : 2 * LANES] + 16384.0 * small[4:6, 2 * LANES : 3 * LANES]
    count_ref[...] = value[:, :experts].astype(jnp.int32)


def solution(mesh):
    narrow, wide = mesh.shape["narrow"], mesh.shape["wide"]

    def hop(value, narrow_bits, wide_bits):
        if wide_bits == 0:
            return lax.ppermute(value, "narrow", [(i, i ^ narrow_bits) for i in range(narrow)])
        if narrow_bits == 0:
            return lax.ppermute(value, "wide", [(i, i ^ wide_bits) for i in range(wide)])
        pairs = [
            (i * wide + j, (i ^ narrow_bits) * wide + (j ^ wide_bits)) for i in range(narrow) for j in range(wide)
        ]
        return lax.ppermute(value, ("narrow", "wide"), pairs)

    def body(
        tokens,
        gain_one,
        shift_one,
        query_w,
        key_w,
        value_w,
        out_w,
        gain_two,
        shift_two,
        router_w,
        up_w,
        up_bias,
        down_w,
        down_bias,
        picks,
        ranks,
        out_grad,
    ):
        count, width = tokens.shape
        experts = router_w.shape[1]
        capacity = ((21 * 2 * count + 20 * experts - 1) // (20 * experts) + 7) // 8 * 8
        slots_all = experts * capacity
        hidden_width = up_w.shape[2]
        half = width // 2
        pairs = HEADS // 2
        blocks = count // (2 * PATCHES)
        extra = (6 + experts + 15) // 16 * 16
        tile = width
        steps = hidden_width // tile
        narrow_at, wide_at = lax.axis_index("narrow"), lax.axis_index("wide")
        core = (narrow_at & 1)[None].astype(jnp.int32)
        place = (((narrow_at >> 1) & 1) * 2 + (wide_at & 1))[None].astype(jnp.int32)
        inner_place = ((wide_at >> 1) & 3)[None].astype(jnp.int32)
        gain_one, shift_one, gain_two, shift_two = (v[None, :] for v in (gain_one, shift_one, gain_two, shift_two))
        router_t = jnp.pad(router_w.T, ((0, LANES - experts), (0, 0)))
        up_w, down_w = up_w[0], down_w[0]

        def exchange(value):
            return lax.all_to_all(value, "wide", split_axis=0, concat_axis=0, tiled=True)

        token_rows = shape((count, width), BF16)
        rows_shape = shape((slots_all, width), BF16)
        lanes_shape = shape((slots_all, LANES), F32)
        narrow_far = far((count, width), BF16)
        spread, target, counts, resid, normed, queries, keys, values, weights, mixed, sent = fuse(
            functools.partial(attention_kernel, capacity, experts),
            (tokens, gain_one, shift_one, picks.T, ranks.T, query_w, key_w, value_w, out_w, gain_two, shift_two),
            (
                far((slots_all, count), BF16),
                far((count, 8), F32),
                far((8, LANES), F32),
                far((count, width), F32),
                narrow_far,
                narrow_far,
                narrow_far,
                narrow_far,
                far((blocks, pairs, 4 * PATCHES, 2 * PATCHES), BF16),
                narrow_far,
                held((slots_all, width), BF16),
            ),
            32,
            10,
            "attention",
        )
        rows = exchange(sent)
        (grad_sent,) = run(dispatch_kernel, (spread, out_grad), (rows_shape,), 16, 1, "dispatch", after=(Held(sent),))
        grad_rows = exchange(grad_sent)

        whole = pl.BlockSpec((slots_all, width), lambda f: (0, 0))
        lanes_whole = pl.BlockSpec((slots_all, LANES), lambda f: (0, 0))
        columns = pl.BlockSpec((slots_all, tile), lambda f: (0, f))
        down_spec = pl.BlockSpec((tile, width), lambda f: (f, 0))
        down_bias_spec = pl.BlockSpec((1, width), lambda f: (0, 0))
        payload = 2 * width + 16
        me = wide_at[None].astype(jnp.int32)
        rows = Held(rows)

        def forward(rows, us, after=()):
            return fuse(
                functools.partial(forward_kernel, experts, tile),
                (me, rows, router_t, up_bias) + tuple(Part(up_w, tile, at) for at in range(steps)),
                (far((slots_all, hidden_width), BF16),) * 2 + (far((slots_all, LANES), F32),) * 2,
                32,
                us,
                "forward",
                (pltpu.VMEM((2, slots_all, tile), F32),),
                after=after,
            )

        hidden, slope, gate, gates = forward(rows, 0.01)
        produced, gated = run(
            produce_kernel,
            (hidden, down_w, down_bias, gate),
            (rows_shape,) * 2,
            32,
            0.01,
            "produce",
            (pltpu.VMEM((slots_all, width), F32),),
            grid=(steps,),
            in_specs=(columns, down_spec, down_bias_spec, lanes_whole),
            out_specs=(whole,) * 2,
        )
        grad_rows = Held(grad_rows)

        def triple(at):
            return Part(down_w, tile, at, rows=True), Part(slope, tile, at), Part(up_w, tile, at)

        rows_others = [hop(rows.value, bits, 0) for bits in range(2, narrow, 2)]
        inner_grad, rows_grad, logit_grad = fuse(
            functools.partial(expert_kernel, experts, tile),
            (me, grad_rows, gate, *triple(0), produced, gates, router_t, *(part for at in range(1, steps) for part in triple(at))),
            (far((slots_all, hidden_width), BF16), held((slots_all, width), BF16), far((slots_all, LANES), BF16)),
            40,
            0.01,
            "experts",
            after=[Held(one) for one in rows_others],
        )
        back = exchange(rows_grad)

        def payload_of(number):
            return shape((number, payload, width), BF16)

        payload_spec = pl.BlockSpec((1, payload, width), lambda f: (f, 0, 0))
        router_spec = pl.BlockSpec((experts, width), lambda f: (0, 0))
        (grad_later,) = run(
            copy_kernel,
            (grad_rows,),
            (rows_shape,),
            4,
            0.01,
            "copy_rows",
            (pltpu.SemaphoreType.DMA,),
            in_specs=(pl.BlockSpec(memory_space=pl.ANY),),
            out_specs=(pl.BlockSpec(memory_space=pltpu.HBM),),
            after=(produced,),
        )

        def held_back(value, after, space=pltpu.HBM):
            return run(
                pass_kernel,
                (value if space == pltpu.HBM else Held(value),),
                (value,),
                1,
                0.01,
                "pass",
                in_specs=(pl.BlockSpec(memory_space=space),),
                out_specs=(pl.BlockSpec(memory_space=space),),
                after=after,
                free=space != pltpu.HBM,
                input_output_aliases={0: 0},
            )[0]

        sets = []
        for bits, rows_of in zip(range(2, narrow, 2), rows_others):
            grad_of = hop(grad_later, bits, 0)
            hidden_of, slope_of, gate_of, _ = forward(rows_of, 0.01, (logit_grad,))
            sets.append((rows_of, grad_of, gate_of, hidden_of, slope_of))

        def weight_part(again, sets, extra, extra_spec, earlier=(), after=()):
            return run(
                functools.partial(weight_kernel, len(sets), int(again)),
                (*(item for one in sets for item in one), *earlier, extra),
                (payload_of(steps),) + (shape((experts, width), F32),) * (not again),
                48,
                0.01,
                "expert_weights",
                (
                    pltpu.VMEM((len(sets), slots_all, width), BF16),
                    pltpu.VMEM((slots_all, tile), BF16),
                    pltpu.VMEM((slots_all, tile), F32),
                ),
                grid=(steps,),
                in_specs=(
                    *(spec for _ in sets for spec in (whole, whole, lanes_whole, columns, columns)),
                    *(payload_spec for _ in earlier),
                    extra_spec,
                ),
                out_specs=(payload_spec,) + (router_spec,) * (not again),
                after=after,
            )

        def finish_experts(start, number, parts, earlier, after=()):
            spec = lambda dims, index: pl.BlockSpec(dims, lambda f: index(start + f))
            return run(
                finish_experts_kernel,
                (*parts, *earlier),
                (
                    shape((width, hidden_width), F32),
                    shape((1, hidden_width), F32),
                    shape((hidden_width, width), F32),
                    shape((1, width), F32),
                ),
                32,
                0.01,
                "finish_experts",
                grid=(number,),
                in_specs=[pl.BlockSpec((1, payload, width), lambda f: (start + f, 0, 0))] * 2
                + [pl.BlockSpec(memory_space=pltpu.HBM)] * len(earlier),
                out_specs=(
                    spec((width, tile), lambda f: (0, f)),
                    spec((1, tile), lambda f: (0, f)),
                    spec((tile, width), lambda f: (f, 0)),
                    down_bias_spec,
                ),
                after=after,
                input_output_aliases={2 + at: at for at in range(len(earlier))},
            )

        own_sum, router_part = weight_part(
            False, [(rows, grad_rows, gate, hidden, inner_grad)], logit_grad, lanes_whole, (), [one[4] for one in sets]
        )
        produced_back = exchange(held_back(gated, (own_sum,)))
        tall = 4 * half + extra
        keep, send, tokens_grad = fuse(
            functools.partial(backward_kernel, experts),
            (
                core,
                Held(back),
                target,
                resid,
                gain_two,
                out_grad,
                mixed,
                out_w,
                values,
                queries,
                weights,
                keys,
                normed,
                query_w,
                key_w,
                value_w,
                tokens,
                gain_one,
                counts,
                router_part,
            ),
            (far((tall, width), BF16), held((tall, width), BF16), far((count, width), BF16)),
            32,
            0.01,
            "backward",
            [pltpu.VMEM((count, width), BF16)] * 4 + [pltpu.VMEM((count, width), F32)],
            after=[own_sum] + [Held(one[1]) for one in sets],
        )

        def share(index, arrived, after=()):
            size = (arrived[0].shape[0] - extra) // 4
            return run(
                functools.partial(share_kernel, len(arrived), 4),
                (index, arrived[0] if size == half else Held(arrived[0]), *map(Held, arrived[1:])),
                (shape((size + extra, width), BF16),) * 4,
                16,
                0.05,
                "share",
                after=after,
                free=True,
            )

        def last(arrived, after=()):
            return run(
                functools.partial(last_kernel, len(arrived)),
                tuple(map(Held, arrived)),
                (shape((half // 4, width), BF16), shape((extra, width), BF16)),
                16,
                0.05,
                "last",
                after=after,
                free=True,
            )

        def gather(arrived, after=()):
            rows_in = sum(value.shape[0] for value in arrived)
            return run(
                gather_kernel,
                tuple(map(Held, arrived)),
                (shape((rows_in, width), BF16),),
                16,
                0.05,
                "gather",
                after=after,
                free=True,
            )[0]

        def spread_out(parts, bits):
            return [parts[0]] + [hop(part, *bit) for part, bit in zip(parts[1:], bits[1:])]

        places = ((0, 0), (0, 1), (2, 0), (2, 1))
        inner_places = ((0, 0), (0, 2), (0, 4), (0, 6))
        parts = share(place, [keep, hop(send, 1, 0)])
        (far_sum,) = weight_part(True, sets, down_w, down_spec, (own_sum,), (Held(parts[0]),))
        parts = share(inner_place, spread_out(parts, places), (far_sum, Held(produced_back)))
        far_sum = held_back(far_sum, (Held(parts[0]),))
        parts = spread_out(parts, inner_places)
        (block_out,) = run(
            combine_kernel, (target, resid, Held(produced_back)), (token_rows,), 16, 0.01, "combine"
        )
        chunk, small = last(parts, (block_out,))
        others = [(bit, 0) for bit in (4, 8, 16, 32, 64) if bit < narrow]
        others += [(0, bit) for bit in (8, 16, 32, 64) if bit < wide]
        for bits in others:
            joined = jnp.concatenate([chunk, small], axis=0)
            chunk, small = last([joined, hop(joined, *bits)])
        sums = (far_sum, Held(hop(far_sum, 1, 0)))
        finished = finish_experts(0, steps // 2, sums, (), (Held(chunk),))
        chunk = gather(spread_out([chunk] * 4, inner_places), (finished[0],))
        pieces = spread_out([chunk] * 4, places)
        finished = finish_experts(steps // 2, steps - steps // 2, sums, finished, (Held(chunk),))
        pieces[3] = held_back(pieces[3], finished[:1], pl.ANY)
        up_grad, up_bias_grad, down_grad, down_bias_grad = finished
        outs = run(
            functools.partial(finish_shared_kernel, experts),
            (
                jnp.concatenate([core, place, inner_place]),
                *map(Held, pieces),
                *(Held(hop(piece, 1, 0)) for piece in pieces),
                Held(small),
            ),
            (shape((width, width), F32),) * 4
            + (shape((1, width), F32),) * 4
            + (shape((experts, width), F32), shape((2, experts), jnp.int32)),
            32,
            3,
            "finish_shared",
        )
        query_grad, key_grad, value_grad, out_w_grad, g_one, s_one, g_two, s_two, router_grad, tallies = outs
        return (
            block_out,
            tokens_grad,
            g_one[0],
            s_one[0],
            query_grad,
            key_grad,
            value_grad,
            out_w_grad,
            g_two[0],
            s_two[0],
            router_grad.T,
            up_grad[None],
            up_bias_grad,
            down_grad[None],
            down_bias_grad,
            tallies.T,
        )

    tokens_spec = P(("narrow", "wide"), None)
    in_specs = (
        (tokens_spec,)
        + (P(),) * 9
        + (P("wide", None, None), P("wide", None), P("wide", None, None), P("wide", None))
        + (tokens_spec,) * 3
    )
    out_specs = (
        (tokens_spec,) * 2
        + (P(),) * 9
        + (P("wide", None, None), P("wide", None), P("wide", None, None), P("wide", None))
        + (P(),)
    )
    return jax.shard_map(body, mesh=mesh, in_specs=in_specs, out_specs=out_specs, check_vma=False)
```

```python
import functools
import math

import jax
import jax.numpy as jnp
from jax import lax
from jax.experimental import pallas as pl
from jax.experimental.pallas import tpu as pltpu
from jax.sharding import PartitionSpec as P

HEADS = 8
PATCHES = 48
EPSILON = 1e-06
LANES = 128
MIB = 1 << 20
F32 = jnp.float32
BF16 = jnp.bfloat16

VMEM = functools.partial(pl.BlockSpec, memory_space=pltpu.VMEM)
SMEM = functools.partial(pl.BlockSpec, memory_space=pltpu.SMEM)


def shape(dims, dtype):
    return jax.ShapeDtypeStruct(dims, dtype)


def dot(a, b):
    return jnp.dot(a, b, preferred_element_type=F32)


def dot_nt(a, b):
    return lax.dot_general(a, b, (((1,), (1,)), ((), ())), preferred_element_type=F32)


def dot_tn(a, b):
    return lax.dot_general(a, b, (((0,), (0,)), ((), ())), preferred_element_type=F32)


def params(mib):
    return pltpu.CompilerParams(vmem_limit_bytes=mib * MIB)


def cost(us):
    return pl.CostEstimate(flops=int(us * 1.0e9), bytes_accessed=int(us * 1.0e5), transcendentals=0)


class Held:
    def __init__(self, value):
        self.value = value
        self.shape, self.dtype, self.ndim = value.shape, value.dtype, value.ndim


def placed(value):
    if isinstance(value, Held):
        return value.value
    if isinstance(value, Part):
        value = value.value
    return value if value.ndim == 1 else pltpu.with_memory_space_constraint(value, pltpu.HBM)


def whole_spec(dims):
    return pl.BlockSpec(tuple(dims), lambda *_: (0,) * len(dims))


def held(dims, dtype):
    return pltpu.VMEM(tuple(dims), dtype)


def far(dims, dtype):
    return pltpu.HBM(tuple(dims), dtype)


def loose(value):
    return pl.BlockSpec(memory_space=pl.ANY if isinstance(value, Held) else pltpu.HBM)


def run(kernel, args, outs, mib, us, name, scratch=(), after=(), grid=(1,), in_specs=None, out_specs=None, free=False, **more):
    given = len(args)
    if in_specs is None:
        in_specs = [SMEM() if a.ndim == 1 else whole_spec(a.shape) for a in args]
    if out_specs is None:
        out_specs = [whole_spec(o.shape) for o in outs]

    def body(*refs):
        kernel(*refs[:given], *refs[given + len(after) :])

    return pl.pallas_call(
        body,
        grid=grid,
        in_specs=list(in_specs) + [loose(value) for value in after],
        out_specs=tuple(out_specs),
        out_shape=tuple(shape(o.shape, o.dtype) if free else far(o.shape, o.dtype) for o in outs),
        scratch_shapes=list(scratch),
        compiler_params=params(mib),
        cost_estimate=cost(us),
        name=name,
        **more,
    )(*map(placed, args), *map(placed, after))


class Part:
    def __init__(self, value, tile, at, rows=False):
        some, all_of = slice(at * tile, (at + 1) * tile), slice(None)
        self.value, self.index = value, (some, all_of) if rows else (all_of, some)
        self.shape = (tile, value.shape[1]) if rows else (value.shape[0], tile)
        self.dtype, self.ndim = value.dtype, 2


class Arriving:
    def __init__(self, source, target, semaphore):
        self.target, self.shape = target, target.shape
        self.copy = pltpu.make_async_copy(source, target, semaphore)
        self.copy.start()
        self.here = False

    def wait(self):
        if not self.here:
            self.copy.wait()
            self.here = True

    def __getitem__(self, index):
        self.wait()
        return self.target[index]


class Leaving:
    def __init__(self, source, target, semaphores):
        self.source, self.target, self.semaphores = source, target, semaphores
        self.shape = source.shape
        self.copies = []

    def __getitem__(self, index):
        return self.source[index]

    def __setitem__(self, index, value):
        self.source[index] = value

    def flush(self, *index):
        one, two = (self.source.at[index], self.target.at[index]) if index else (self.source, self.target)
        self.copies.append(pltpu.make_async_copy(one, two, self.semaphores.at[len(self.copies)]))
        self.copies[-1].start()

    def wait(self):
        for copy in self.copies:
            copy.wait()


def fuse(kernel, args, outs, mib, us, name, scratch=(), after=()):
    is_far = [not isinstance(a, Held) and a.ndim > 1 for a in args]
    out_far = [o.memory_space == pltpu.HBM for o in outs]
    given, made = len(args), len(outs)

    def body(*refs):
        ins, refs = list(refs[:given]), refs[given + len(after) :]
        results, refs = list(refs[:made]), list(refs[made:])
        arrivals, departures = refs.pop(), refs.pop()
        coming, going = [], []
        for at in range(given):
            if is_far[at]:
                source = ins[at].at[args[at].index] if isinstance(args[at], Part) else ins[at]
                ins[at] = Arriving(source, refs.pop(0), arrivals.at[len(coming)])
                coming.append(ins[at])
        for at in range(made):
            if out_far[at]:
                results[at] = Leaving(refs.pop(0), results[at], departures.at[len(going)])
                going.append(results[at])
        kernel(*ins, *results, *refs)
        for item in coming + going:
            item.wait()

    def spec(value):
        if isinstance(value, Held):
            return VMEM()
        return SMEM() if value.ndim == 1 else pl.BlockSpec(memory_space=pltpu.HBM)

    return pl.pallas_call(
        body,
        in_specs=[spec(a) for a in args] + [loose(value) for value in after],
        out_specs=tuple(pl.BlockSpec(memory_space=o.memory_space) for o in outs),
        out_shape=tuple(outs),
        scratch_shapes=[pltpu.VMEM(a.shape, a.dtype) for a, there in zip(args, is_far) if there]
        + [pltpu.VMEM(o.shape, o.dtype) for o, there in zip(outs, out_far) if there]
        + list(scratch)
        + [pltpu.SemaphoreType.DMA((max(sum(out_far), 1), 8)), pltpu.SemaphoreType.DMA((max(sum(is_far), 1),))],
        compiler_params=params(mib),
        cost_estimate=cost(us),
        name=name,
    )(*map(placed, args), *map(placed, after))


def norm_rows(values):
    center = values - jnp.mean(values, axis=-1, keepdims=True)
    spread = jnp.mean(center * center, axis=-1, keepdims=True)
    rate = lax.rsqrt(spread + EPSILON)
    return center * rate, rate


def norm_back(hat, rate, gain, grad):
    scaled = grad * gain
    mean_one = jnp.mean(scaled, axis=-1, keepdims=True)
    mean_two = jnp.mean(scaled * hat, axis=-1, keepdims=True)
    return rate * (scaled - mean_one - hat * mean_two)


def route(capacity, experts, picks_ref, ranks_ref, spread_ref, target_ref, count_ref):
    count = picks_ref.shape[1]
    slots_all = experts * capacity
    span = 1 << (2 * count - 1).bit_length()
    picks = picks_ref[...].astype(F32)
    base = picks * span
    order = base + ranks_ref[...].astype(F32)
    padded = jnp.concatenate([picks, order, jnp.zeros((4, count), F32)], axis=0)
    turned = jnp.transpose(padded)
    targets = []
    for j in range(2):
        row = order[j : j + 1]
        floor = base[j : j + 1]
        slot = jnp.zeros((1, count), F32)
        for other in range(2):
            column = turned[:, 2 + other : 3 + other]
            ahead = (column < row) & (column >= floor)
            slot = slot + jnp.sum(jnp.where(ahead, 1.0, 0.0), axis=0, keepdims=True)
        kept = slot < capacity
        targets.append(jnp.where(kept, picks[j : j + 1] * capacity + slot, float(slots_all)))
    target_turned = jnp.transpose(jnp.concatenate(targets + [jnp.zeros((6, count), F32)], axis=0))
    target_ref[...] = target_turned
    lane = lax.broadcasted_iota(jnp.int32, (count, LANES), 1).astype(F32)
    kept_count = jnp.zeros((1, LANES), F32)
    all_count = jnp.zeros((1, LANES), F32)
    for j in range(2):
        named = jnp.where(turned[:, j : j + 1] == lane, 1.0, 0.0)
        live = jnp.where(target_turned[:, j : j + 1] < slots_all, 1.0, 0.0)
        all_count = all_count + jnp.sum(named, axis=0, keepdims=True)
        kept_count = kept_count + jnp.sum(named * live, axis=0, keepdims=True)
    count_ref[...] = jnp.concatenate([kept_count, all_count - kept_count, jnp.zeros((6, LANES), F32)], axis=0)
    step = 64
    for start in range(0, slots_all, step):
        index = lax.broadcasted_iota(jnp.int32, (step, count), 0).astype(F32) + float(start)
        hit = (index == targets[0]) | (index == targets[1])
        spread_ref[start : start + step, :] = jnp.where(hit, 1.0, 0.0).astype(BF16)


def head_masks(width):
    lane = lax.broadcasted_iota(jnp.int32, (1, width), 1)
    return lane < width // 2


def stack_heads(pair, low):
    zero = jnp.zeros_like(pair)
    return jnp.concatenate([jnp.where(low, pair, zero), jnp.where(low, zero, pair)], axis=0)


def attention_kernel(
    capacity,
    experts,
    tokens_ref,
    gain_one_ref,
    shift_one_ref,
    picks_ref,
    ranks_ref,
    query_w_ref,
    key_w_ref,
    value_w_ref,
    out_w_ref,
    gain_two_ref,
    shift_two_ref,
    spread_ref,
    target_ref,
    count_ref,
    resid_ref,
    normed_ref,
    query_ref,
    key_ref,
    value_ref,
    weight_ref,
    mixed_ref,
    sent_ref,
):
    count, width = tokens_ref.shape
    inputs = tokens_ref[...].astype(F32)
    hat, _ = norm_rows(inputs)
    normed_ref[...] = (hat * gain_one_ref[...] + shift_one_ref[...]).astype(BF16)
    normed_ref.flush()
    route(capacity, experts, picks_ref, ranks_ref, spread_ref, target_ref, count_ref)
    spread_ref.flush()
    target_ref.flush()
    count_ref.flush()
    normed = normed_ref[...]
    scale = 1.0 / math.sqrt(width // HEADS)
    query_ref[...] = (dot(normed, query_w_ref[...]).astype(BF16).astype(F32) * scale).astype(BF16)
    query_ref.flush()
    key_ref[...] = dot(normed, key_w_ref[...]).astype(BF16)
    key_ref.flush()
    value_ref[...] = dot(normed, value_w_ref[...]).astype(BF16)
    value_ref.flush()
    pairs = HEADS // 2
    wide = width // pairs
    block = 2 * PATCHES
    low = head_masks(wide)
    row_image = (lax.broadcasted_iota(jnp.int32, (2 * block, block), 0) % block) // PATCHES
    column_image = lax.broadcasted_iota(jnp.int32, (2 * block, block), 1) // PATCHES
    bias = jnp.where(row_image == column_image, 0.0, -1e30)
    together = 8
    cells = [(item, pair) for item in range(count // block) for pair in range(pairs)]
    for start in range(0, len(cells), together):
        work = []
        for item, pair in cells[start : start + together]:
            rows = slice(item * block, (item + 1) * block)
            lanes = slice(pair * wide, (pair + 1) * wide)
            scores = dot_nt(stack_heads(query_ref[rows, lanes], low), key_ref[rows, lanes]) + bias
            work.append((rows, lanes, scores))
        tops = [jnp.max(scores, axis=-1, keepdims=True) for _, _, scores in work]
        powers = [jnp.exp(scores - top) for (_, _, scores), top in zip(work, tops)]
        totals = [jnp.sum(power, axis=-1, keepdims=True) for power in powers]
        lows = [(power / total).astype(BF16) for power, total in zip(powers, totals)]
        for (item, pair), weights in zip(cells[start : start + together], lows):
            weight_ref[item, pair] = weights
        for (rows, lanes, _), weights in zip(work, lows):
            mixed = dot(weights, value_ref[rows, lanes])
            mixed_ref[rows, lanes] = jnp.where(low, mixed[:block], mixed[block:]).astype(BF16)
    weight_ref.flush()
    mixed_ref.flush()
    resid = inputs + dot(mixed_ref[...], out_w_ref[...])
    resid_ref[...] = resid
    resid_ref.flush()
    hat, _ = norm_rows(resid)
    second = (hat * gain_two_ref[...] + shift_two_ref[...]).astype(BF16)
    sent_ref[...] = dot(spread_ref[...], second).astype(BF16)


def dispatch_kernel(spread_ref, second_ref, sent_ref):
    sent_ref[...] = dot(spread_ref[...], second_ref[...]).astype(BF16)


def forward_kernel(experts, tile, me_ref, rows_ref, router_ref, up_bias_ref, *refs):
    ups = refs[:-4]
    hidden_ref, slope_ref, gate_ref, gates_ref = refs[-4:]
    total = rows_ref.shape[0]
    chunk = total // 4
    root = math.sqrt(2.0 / math.pi)
    rows = rows_ref[...]
    lane = lax.broadcasted_iota(jnp.int32, (total, LANES), 1)
    logits = jnp.where(lane < experts, dot_nt(rows, router_ref[...]), -1e30)
    powers = jnp.exp(logits - jnp.max(logits, axis=-1, keepdims=True))
    gates = powers / jnp.sum(powers, axis=-1, keepdims=True)
    gates_ref[...] = gates
    gates_ref.flush()
    gate = jnp.sum(jnp.where(lane == me_ref[0], gates, 0.0), axis=-1, keepdims=True)
    gate_ref[...] = jnp.broadcast_to(gate, (total, LANES))
    gate_ref.flush()
    for step, up_ref in enumerate(ups):
        lanes = slice(step * tile, (step + 1) * tile)
        for start in range(0, total, chunk):
            at = slice(start, start + chunk)
            inner = dot(rows[at], up_ref[...]) + up_bias_ref[:, lanes]
            square = inner * inner
            half = 0.5 + 0.5 * jnp.tanh(inner * (root + (root * 0.044715) * square))
            hidden = inner * half
            slope = half + (hidden - hidden * half) * (2.0 * root + (6.0 * root * 0.044715) * square)
            hidden_ref[at, lanes] = hidden.astype(BF16)
            slope_ref[at, lanes] = slope.astype(BF16)
        hidden_ref.flush(slice(None), lanes)
        slope_ref.flush(slice(None), lanes)


def produce_kernel(hidden_ref, down_ref, down_bias_ref, gate_ref, out_ref, *refs):
    parts, total_s = refs[:-1], refs[-1]
    step = pl.program_id(0)
    made = dot(hidden_ref[...], down_ref[...])

    @pl.when(step == 0)
    def _():
        total_s[...] = made

    @pl.when(step > 0)
    def _():
        total_s[...] += made

    @pl.when(step == pl.num_programs(0) - 1)
    def _():
        produced = (total_s[...] + down_bias_ref[...]).astype(BF16)
        out_ref[...] = produced
        size = parts[0].shape[1]
        gate = jnp.concatenate([gate_ref[...]] * (size // LANES), axis=1)
        for at, ref in enumerate(parts):
            ref[...] = (produced[:, at * size : (at + 1) * size].astype(F32) * gate).astype(BF16)


def expert_kernel(experts, tile, me_ref, grad_ref, gate_ref, *refs):
    steps = (len(refs) - 6) // 3
    downs, slopes, ups = [refs[0], *refs[6 : 3 * steps + 3 : 3]], [refs[1], *refs[7 : 3 * steps + 3 : 3]], [refs[2], *refs[8 : 3 * steps + 3 : 3]]
    produced_ref, gates_ref, router_ref = refs[3:6]
    inner_grad_ref, rows_grad_ref, logit_grad_ref = refs[3 * steps + 3 :]
    total, width = grad_ref.shape
    gate = jnp.concatenate([gate_ref[...]] * (tile // LANES), axis=1)
    for step in range(steps):
        lanes = slice(step * tile, (step + 1) * tile)
        made = dot_nt(grad_ref[...], downs[step][...]) * gate * slopes[step][...].astype(F32)
        inner_grad_ref[:, lanes] = made.astype(BF16)
        inner_grad_ref.flush(slice(None), lanes)
        if step == 0:
            lane = lax.broadcasted_iota(jnp.int32, (total, LANES), 1)
            product = grad_ref[...].astype(F32) * produced_ref[...].astype(F32)
            pair_grad = jnp.sum(product, axis=-1, keepdims=True)
            own = jnp.where(lane == me_ref[0], 1.0, 0.0)
            logit_grad = (gates_ref[...] * (own - gate_ref[...]) * pair_grad).astype(BF16)
            logit_grad_ref[...] = logit_grad
            logit_grad_ref.flush()
    made = dot(logit_grad, router_ref[...])
    for step in range(steps):
        made = made + dot_nt(inner_grad_ref[:, step * tile : (step + 1) * tile], ups[step][...])
    rows_grad_ref[...] = made.astype(BF16)


def weight_kernel(sets, again, *refs):
    groups, refs = [refs[at * 5 : at * 5 + 5] for at in range(sets)], refs[5 * sets :]
    earlier, refs = refs[:again], refs[again:]
    extra_ref, out_ref, refs = refs[0], refs[1], refs[2:]
    router_refs, gated_s, inner_grad_s = refs[:-2], refs[-2], refs[-1]
    total, width = groups[0][0].shape

    @pl.when(pl.program_id(0) == 0)
    def _():
        for at, some in enumerate(groups):
            gate = jnp.concatenate([some[2][...]] * (width // LANES), axis=1)
            gated_s[at] = (gate * some[1][...].astype(F32)).astype(BF16)
        if router_refs:
            router_refs[0][...] = dot_tn(extra_ref[...], groups[0][0][...])[: router_refs[0].shape[0]]

    ups, downs, up_biases, down_biases = [], [], [], []
    for at, (rows_ref, grad_ref, gate_ref, hidden_ref, inner_grad_ref) in enumerate(groups):
        if again:
            slope_ref, inner_grad_ref = inner_grad_ref, inner_grad_s
            gate = jnp.concatenate([gate_ref[...]] * (width // LANES), axis=1)
            made = dot_nt(grad_ref[...], extra_ref[...]) * gate * slope_ref[...].astype(F32)
            inner_grad_s[...] = made.astype(BF16)
        inner_grad = inner_grad_ref[...]
        ups.append(dot_tn(rows_ref[...], inner_grad))
        downs.append(dot_tn(hidden_ref[...], gated_s[at]))
        up_biases.append(jnp.sum(inner_grad.astype(F32), axis=0, keepdims=True))
        down_biases.append(jnp.sum(gated_s[at].astype(F32), axis=0, keepdims=True))

    def put(some, parts):
        made = sum(parts[1:], parts[0]).astype(BF16)
        if again:
            made = (made.astype(F32) + earlier[0][0, some, :].astype(F32)).astype(BF16)
        out_ref[0, some, :] = made

    put(slice(0, width), ups)
    put(slice(width, 2 * width), downs)
    row = lax.broadcasted_iota(jnp.int32, (16, width), 0)
    small = jnp.where(row == 0, sum(up_biases[1:], up_biases[0]), sum(down_biases[1:], down_biases[0]))
    put(slice(2 * width, None), [small])


def finish_experts_kernel(*refs):
    parts, (up_ref, up_bias_ref, down_ref, down_bias_ref) = refs[:2], refs[-4:]
    tall = up_ref.shape[0]

    def total(some):
        return sum_in_tree([ref[0, some, :].astype(F32) for ref in parts])

    up_ref[...] = total(slice(0, tall))
    down_ref[...] = total(slice(tall, 2 * tall))
    small = total(slice(2 * tall, None))
    up_bias_ref[...] = small[0:1]
    down_bias_ref[...] = small[1:2]


def one_hot_rows(target_ref, slots_all):
    count = target_ref.shape[0]
    lane = lax.broadcasted_iota(jnp.int32, (64, slots_all), 1).astype(F32)
    pieces = []
    for start in range(0, count, 64):
        one = target_ref[start : start + 64, 0:1]
        two = target_ref[start : start + 64, 1:2]
        pieces.append(jnp.where((lane == one) | (lane == two), 1.0, 0.0).astype(BF16))
    return jnp.concatenate(pieces, axis=0)


def combine_kernel(target_ref, resid_ref, *refs):
    parts, out_ref = refs[:-1], refs[-1]
    picked = one_hot_rows(target_ref, parts[0].shape[0])
    size = parts[0].shape[1]
    for at, ref in enumerate(parts):
        lanes = slice(at * size, (at + 1) * size)
        out_ref[:, lanes] = (resid_ref[:, lanes] + dot(picked, ref[...])).astype(BF16)


def backward_kernel(
    experts,
    core_ref,
    back_ref,
    target_ref,
    resid_ref,
    gain_two_ref,
    grad_ref,
    mixed_ref,
    out_w_ref,
    value_ref,
    query_ref,
    weight_ref,
    key_ref,
    normed_ref,
    query_w_ref,
    key_w_ref,
    value_w_ref,
    tokens_ref,
    gain_one_ref,
    count_ref,
    router_grad_ref,
    keep_ref,
    send_ref,
    tokens_grad_ref,
    queries_s,
    keys_s,
    values_s,
    mixed_grad_s,
    resid_grad_s,
):
    count, width = grad_ref.shape
    picked = one_hot_rows(target_ref, back_ref.shape[0])
    second_grad = dot(picked, back_ref[...])
    hat, rate = norm_rows(resid_ref[...])
    gain_two_grad = jnp.sum(second_grad * hat, axis=0, keepdims=True)
    shift_two_grad = jnp.sum(second_grad, axis=0, keepdims=True)
    resid_grad_s[...] = grad_ref[...].astype(F32) + norm_back(hat, rate, gain_two_ref[...], second_grad)
    branch = resid_grad_s[...].astype(BF16)
    half = width // 2
    first = core_ref[0] == 0

    def put(at, value):
        value = value.astype(BF16)
        keep_ref[at * half : (at + 1) * half, :] = jnp.where(first, value[:half], value[half:])
        send_ref[at * half : (at + 1) * half, :] = jnp.where(first, value[half:], value[:half])
        keep_ref.flush(slice(at * half, (at + 1) * half))

    put(3, dot_tn(mixed_ref[...], branch))
    mixed_grad_s[...] = dot_nt(branch, out_w_ref[...]).astype(BF16)
    pairs = HEADS // 2
    wide = width // pairs
    block = 2 * PATCHES
    scale = 1.0 / math.sqrt(width // HEADS)
    low = head_masks(wide)
    together = 8
    cells = [(item, pair) for item in range(count // block) for pair in range(pairs)]
    for start in range(0, len(cells), together):
        work = []
        for item, pair in cells[start : start + together]:
            rows = slice(item * block, (item + 1) * block)
            lanes = slice(pair * wide, (pair + 1) * wide)
            mixed_stack = stack_heads(mixed_grad_s[rows, lanes], low)
            weights = weight_ref[item, pair]
            work.append((rows, lanes, mixed_stack, weights, dot_nt(mixed_stack, value_ref[rows, lanes])))
        score_grads = []
        for rows, lanes, mixed_stack, weights, weight_grad in work:
            product = weights.astype(F32) * weight_grad
            score_grad = product - weights.astype(F32) * jnp.sum(product, axis=-1, keepdims=True)
            score_grads.append(score_grad.astype(BF16))
        for rows, lanes, mixed_stack, weights, _ in work:
            values_s[rows, lanes] = dot_tn(weights, mixed_stack).astype(BF16)
        for (rows, lanes, *_), score_grad in zip(work, score_grads):
            made = dot(score_grad, key_ref[rows, lanes]) * scale
            queries_s[rows, lanes] = jnp.where(low, made[:block], made[block:]).astype(BF16)
        for (rows, lanes, *_), score_grad in zip(work, score_grads):
            keys_s[rows, lanes] = dot_tn(score_grad, stack_heads(query_ref[rows, lanes], low)).astype(BF16)
    normed = normed_ref[...]
    put(0, dot_tn(normed, queries_s[...]))
    put(1, dot_tn(normed, keys_s[...]))
    put(2, dot_tn(normed, values_s[...]))
    normed_grad = (
        dot_nt(queries_s[...], query_w_ref[...])
        + dot_nt(keys_s[...], key_w_ref[...])
        + dot_nt(values_s[...], value_w_ref[...])
    )
    hat, rate = norm_rows(tokens_ref[...].astype(F32))
    gain_one_grad = jnp.sum(normed_grad * hat, axis=0, keepdims=True)
    shift_one_grad = jnp.sum(normed_grad, axis=0, keepdims=True)
    tokens_grad_ref[...] = (resid_grad_s[...] + norm_back(hat, rate, gain_one_ref[...], normed_grad)).astype(BF16)
    tokens_grad_ref.flush()
    digits = []
    for kind in range(2):
        value = count_ref[kind : kind + 1, :]
        high = jnp.floor(value * (1.0 / 128.0))
        digits.append(jnp.concatenate([value - 128.0 * high, high] + [jnp.zeros_like(value)] * (width // LANES - 2), axis=1))
    extra = keep_ref.shape[0] - 4 * half
    small = [gain_one_grad, shift_one_grad, gain_two_grad, shift_two_grad] + digits + [router_grad_ref[:experts, :]]
    small = jnp.concatenate(small + [jnp.zeros((extra - 6 - experts, width), F32)], axis=0).astype(BF16)
    keep_ref[4 * half :, :] = small
    send_ref[4 * half :, :] = small
    keep_ref.flush(slice(4 * half, None))


def carry_digits(total):
    row = lax.broadcasted_iota(jnp.int32, (total.shape[0], LANES), 0)
    one, two, three = (total[:, at * LANES : (at + 1) * LANES] for at in range(3))
    over = jnp.floor(one * (1.0 / 128.0))
    two_full = two + over
    over_two = jnp.floor(two_full * (1.0 / 128.0))
    parts = [one - 128.0 * over, two_full - 128.0 * over_two, three + over_two]
    is_count = (row == 4) | (row == 5)
    parts = [jnp.where(is_count, part, total[:, at * LANES : (at + 1) * LANES]) for at, part in enumerate(parts)]
    return jnp.concatenate(parts + [total[:, 3 * LANES :]], axis=1)


def sum_in_tree(values):
    while len(values) > 1:
        values = [values[at] + values[at + 1] for at in range(0, len(values), 2)]
    return values[0]


def share_kernel(given, pieces, *refs):
    index_ref, arrived, made = refs[0], refs[1 : 1 + given], refs[1 + given :]
    small_rows = (pieces * made[0].shape[0] - arrived[0].shape[0]) // (pieces - 1)
    size = made[0].shape[0] - small_rows
    top = pieces * size
    small = carry_digits(sum_in_tree([ref[top:, :].astype(F32) for ref in arrived])).astype(BF16)
    for away in range(pieces):
        at = pl.ds(pl.multiple_of((index_ref[0] ^ away) * size, size), size)
        made[away][:size, :] = sum_in_tree([ref[at, :].astype(F32) for ref in arrived]).astype(BF16)
        made[away][size:, :] = small


def copy_kernel(given_ref, made_ref, arrival):
    copy = pltpu.make_async_copy(given_ref, made_ref, arrival)
    copy.start()
    copy.wait()


def pass_kernel(given_ref, same_ref):
    pass


def gather_kernel(*refs):
    arrived, out_ref = refs[:-1], refs[-1]
    size = arrived[0].shape[0]
    for at, ref in enumerate(arrived):
        out_ref[at * size : (at + 1) * size, :] = ref[...]


def last_kernel(given, *refs):
    arrived, chunk_ref, small_ref = refs[:given], refs[given], refs[given + 1]
    size = chunk_ref.shape[0]
    chunk_ref[...] = sum_in_tree([ref[:size, :].astype(F32) for ref in arrived]).astype(BF16)
    small_ref[...] = carry_digits(sum_in_tree([ref[size:, :].astype(F32) for ref in arrived])).astype(BF16)


def finish_shared_kernel(experts, index_ref, *refs):
    own, others, small_ref, outs = refs[:4], refs[4:8], refs[8], refs[9:]
    vector_refs, router_ref, count_ref = outs[4:8], outs[8], outs[9]
    core, place, inner_place = index_ref[0], index_ref[1], index_ref[2]
    half = outs[0].shape[1] // 2
    size = half // 4
    for pieces, side in ((own, core), (others, 1 - core)):
        for away, piece in enumerate(pieces):
            for at in range(4):

                @pl.when((place ^ away) == at)
                def _(piece=piece, side=side, out=outs[at]):
                    for part in range(4):
                        start = pl.multiple_of((inner_place ^ part) * size, size)
                        row = pl.multiple_of(side * half + part * size, size)
                        out[pl.ds(row, size), :] = piece[pl.ds(start, size), :].astype(F32)

    small = small_ref[...].astype(F32)
    for at, ref in enumerate(vector_refs):
        ref[...] = small[at : at + 1, :]
    router_ref[...] = small[6 : 6 + experts, :]
    value = small[4:6, :LANES] + 128.0 * small[4:6, LANES : 2 * LANES] + 16384.0 * small[4:6, 2 * LANES : 3 * LANES]
    count_ref[...] = value[:, :experts].astype(jnp.int32)


def solution(mesh):
    narrow, wide = mesh.shape["narrow"], mesh.shape["wide"]

    def hop(value, narrow_bits, wide_bits):
        if wide_bits == 0:
            return lax.ppermute(value, "narrow", [(i, i ^ narrow_bits) for i in range(narrow)])
        if narrow_bits == 0:
            return lax.ppermute(value, "wide", [(i, i ^ wide_bits) for i in range(wide)])
        pairs = [
            (i * wide + j, (i ^ narrow_bits) * wide + (j ^ wide_bits)) for i in range(narrow) for j in range(wide)
        ]
        return lax.ppermute(value, ("narrow", "wide"), pairs)

    def body(
        tokens,
        gain_one,
        shift_one,
        query_w,
        key_w,
        value_w,
        out_w,
        gain_two,
        shift_two,
        router_w,
        up_w,
        up_bias,
        down_w,
        down_bias,
        picks,
        ranks,
        out_grad,
    ):
        count, width = tokens.shape
        experts = router_w.shape[1]
        capacity = ((21 * 2 * count + 20 * experts - 1) // (20 * experts) + 7) // 8 * 8
        slots_all = experts * capacity
        hidden_width = up_w.shape[2]
        half = width // 2
        pairs = HEADS // 2
        blocks = count // (2 * PATCHES)
        extra = (6 + experts + 15) // 16 * 16
        tile = width
        steps = hidden_width // tile
        narrow_at, wide_at = lax.axis_index("narrow"), lax.axis_index("wide")
        core = (narrow_at & 1)[None].astype(jnp.int32)
        place = (((narrow_at >> 1) & 1) * 2 + (wide_at & 1))[None].astype(jnp.int32)
        inner_place = ((wide_at >> 1) & 3)[None].astype(jnp.int32)
        gain_one, shift_one, gain_two, shift_two = (v[None, :] for v in (gain_one, shift_one, gain_two, shift_two))
        router_t = jnp.pad(router_w.T, ((0, LANES - experts), (0, 0)))
        up_w, down_w = up_w[0], down_w[0]

        def exchange(value):
            return lax.all_to_all(value, "wide", split_axis=0, concat_axis=0, tiled=True)

        token_rows = shape((count, width), BF16)
        rows_shape = shape((slots_all, width), BF16)
        lanes_shape = shape((slots_all, LANES), F32)
        narrow_far = far((count, width), BF16)
        spread, target, counts, resid, normed, queries, keys, values, weights, mixed, sent = fuse(
            functools.partial(attention_kernel, capacity, experts),
            (tokens, gain_one, shift_one, picks.T, ranks.T, query_w, key_w, value_w, out_w, gain_two, shift_two),
            (
                far((slots_all, count), BF16),
                far((count, 8), F32),
                far((8, LANES), F32),
                far((count, width), F32),
                narrow_far,
                narrow_far,
                narrow_far,
                narrow_far,
                far((blocks, pairs, 4 * PATCHES, 2 * PATCHES), BF16),
                narrow_far,
                held((slots_all, width), BF16),
            ),
            32,
            10,
            "attention",
        )
        rows = exchange(sent)
        (grad_sent,) = run(dispatch_kernel, (spread, out_grad), (rows_shape,), 16, 1, "dispatch", after=(Held(sent),))
        grad_rows = exchange(grad_sent)

        whole = pl.BlockSpec((slots_all, width), lambda f: (0, 0))
        lanes_whole = pl.BlockSpec((slots_all, LANES), lambda f: (0, 0))
        columns = pl.BlockSpec((slots_all, tile), lambda f: (0, f))
        down_spec = pl.BlockSpec((tile, width), lambda f: (f, 0))
        down_bias_spec = pl.BlockSpec((1, width), lambda f: (0, 0))
        payload = 2 * width + 16
        me = wide_at[None].astype(jnp.int32)
        rows = Held(rows)

        def forward(rows, us, after=()):
            return fuse(
                functools.partial(forward_kernel, experts, tile),
                (me, rows, router_t, up_bias) + tuple(Part(up_w, tile, at) for at in range(steps)),
                (far((slots_all, hidden_width), BF16),) * 2 + (far((slots_all, LANES), F32),) * 2,
                32,
                us,
                "forward",
                after=after,
            )

        hidden, slope, gate, gates = forward(rows, 0.01)
        produced, gated = run(
            produce_kernel,
            (hidden, down_w, down_bias, gate),
            (rows_shape,) * 2,
            32,
            0.01,
            "produce",
            (pltpu.VMEM((slots_all, width), F32),),
            grid=(steps,),
            in_specs=(columns, down_spec, down_bias_spec, lanes_whole),
            out_specs=(whole,) * 2,
        )
        grad_rows = Held(grad_rows)

        def triple(at):
            return Part(down_w, tile, at, rows=True), Part(slope, tile, at), Part(up_w, tile, at)

        rows_others = [hop(rows.value, bits, 0) for bits in range(2, narrow, 2)]
        inner_grad, rows_grad, logit_grad = fuse(
            functools.partial(expert_kernel, experts, tile),
            (me, grad_rows, gate, *triple(0), produced, gates, router_t, *(part for at in range(1, steps) for part in triple(at))),
            (far((slots_all, hidden_width), BF16), held((slots_all, width), BF16), far((slots_all, LANES), BF16)),
            40,
            0.01,
            "experts",
            after=[Held(one) for one in rows_others],
        )
        back = exchange(rows_grad)

        def payload_of(number):
            return shape((number, payload, width), BF16)

        payload_spec = pl.BlockSpec((1, payload, width), lambda f: (f, 0, 0))
        router_spec = pl.BlockSpec((experts, width), lambda f: (0, 0))
        (grad_later,) = run(
            copy_kernel,
            (grad_rows,),
            (rows_shape,),
            4,
            0.01,
            "copy_rows",
            (pltpu.SemaphoreType.DMA,),
            in_specs=(pl.BlockSpec(memory_space=pl.ANY),),
            out_specs=(pl.BlockSpec(memory_space=pltpu.HBM),),
            after=(produced,),
        )

        def held_back(value, after, space=pltpu.HBM):
            return run(
                pass_kernel,
                (value if space == pltpu.HBM else Held(value),),
                (value,),
                1,
                0.01,
                "pass",
                in_specs=(pl.BlockSpec(memory_space=space),),
                out_specs=(pl.BlockSpec(memory_space=space),),
                after=after,
                free=space != pltpu.HBM,
                input_output_aliases={0: 0},
            )[0]

        sets = []
        for bits, rows_of in zip(range(2, narrow, 2), rows_others):
            grad_of = hop(grad_later, bits, 0)
            hidden_of, slope_of, gate_of, _ = forward(rows_of, 0.01, (logit_grad,))
            sets.append((rows_of, grad_of, gate_of, hidden_of, slope_of))

        def weight_part(again, sets, extra, extra_spec, earlier=(), after=()):
            return run(
                functools.partial(weight_kernel, len(sets), int(again)),
                (*(item for one in sets for item in one), *earlier, extra),
                (payload_of(steps),) + (shape((experts, width), F32),) * (not again),
                48,
                0.01,
                "expert_weights",
                (
                    pltpu.VMEM((len(sets), slots_all, width), BF16),
                    pltpu.VMEM((slots_all, tile), BF16),
                ),
                grid=(steps,),
                in_specs=(
                    *(spec for _ in sets for spec in (whole, whole, lanes_whole, columns, columns)),
                    *(payload_spec for _ in earlier),
                    extra_spec,
                ),
                out_specs=(payload_spec,) + (router_spec,) * (not again),
                after=after,
            )

        def finish_experts(start, number, parts, earlier, after=()):
            spec = lambda dims, index: pl.BlockSpec(dims, lambda f: index(start + f))
            return run(
                finish_experts_kernel,
                (*parts, *earlier),
                (
                    shape((width, hidden_width), F32),
                    shape((1, hidden_width), F32),
                    shape((hidden_width, width), F32),
                    shape((1, width), F32),
                ),
                32,
                0.01,
                "finish_experts",
                grid=(number,),
                in_specs=[pl.BlockSpec((1, payload, width), lambda f: (start + f, 0, 0))] * 2
                + [pl.BlockSpec(memory_space=pltpu.HBM)] * len(earlier),
                out_specs=(
                    spec((width, tile), lambda f: (0, f)),
                    spec((1, tile), lambda f: (0, f)),
                    spec((tile, width), lambda f: (f, 0)),
                    down_bias_spec,
                ),
                after=after,
                input_output_aliases={2 + at: at for at in range(len(earlier))},
            )

        own_sum, router_part = weight_part(
            False, [(rows, grad_rows, gate, hidden, inner_grad)], logit_grad, lanes_whole, (), [one[4] for one in sets]
        )
        produced_back = exchange(held_back(gated, (own_sum,)))
        tall = 4 * half + extra
        keep, send, tokens_grad = fuse(
            functools.partial(backward_kernel, experts),
            (
                core,
                Held(back),
                target,
                resid,
                gain_two,
                out_grad,
                mixed,
                out_w,
                values,
                queries,
                weights,
                keys,
                normed,
                query_w,
                key_w,
                value_w,
                tokens,
                gain_one,
                counts,
                router_part,
            ),
            (far((tall, width), BF16), held((tall, width), BF16), far((count, width), BF16)),
            32,
            0.01,
            "backward",
            [pltpu.VMEM((count, width), BF16)] * 4 + [pltpu.VMEM((count, width), F32)],
            after=[own_sum] + [Held(one[1]) for one in sets],
        )

        def share(index, arrived, after=()):
            size = (arrived[0].shape[0] - extra) // 4
            return run(
                functools.partial(share_kernel, len(arrived), 4),
                (index, arrived[0] if size == half else Held(arrived[0]), *map(Held, arrived[1:])),
                (shape((size + extra, width), BF16),) * 4,
                16,
                0.05,
                "share",
                after=after,
                free=True,
            )

        def last(arrived, after=()):
            return run(
                functools.partial(last_kernel, len(arrived)),
                tuple(map(Held, arrived)),
                (shape((half // 4, width), BF16), shape((extra, width), BF16)),
                16,
                0.05,
                "last",
                after=after,
                free=True,
            )

        def gather(arrived, after=()):
            rows_in = sum(value.shape[0] for value in arrived)
            return run(
                gather_kernel,
                tuple(map(Held, arrived)),
                (shape((rows_in, width), BF16),),
                16,
                0.05,
                "gather",
                after=after,
                free=True,
            )[0]

        def spread_out(parts, bits):
            return [parts[0]] + [hop(part, *bit) for part, bit in zip(parts[1:], bits[1:])]

        places = ((0, 0), (0, 1), (2, 0), (2, 1))
        inner_places = ((0, 0), (0, 2), (0, 4), (0, 6))
        parts = share(place, [keep, hop(send, 1, 0)])
        (far_sum,) = weight_part(True, sets, down_w, down_spec, (own_sum,), (Held(parts[0]),))
        parts = share(inner_place, spread_out(parts, places), (far_sum, Held(produced_back)))
        far_sum = held_back(far_sum, (Held(parts[0]),))
        parts = spread_out(parts, inner_places)
        (block_out,) = run(
            combine_kernel, (target, resid, Held(produced_back)), (token_rows,), 16, 0.01, "combine"
        )
        chunk, small = last(parts, (block_out,))
        others = [(bit, 0) for bit in (4, 8, 16, 32, 64) if bit < narrow]
        others += [(0, bit) for bit in (8, 16, 32, 64) if bit < wide]
        for bits in others:
            joined = jnp.concatenate([chunk, small], axis=0)
            chunk, small = last([joined, hop(joined, *bits)])
        sums = (far_sum, Held(hop(far_sum, 1, 0)))
        finished = finish_experts(0, steps // 2, sums, (), (Held(chunk),))
        chunk = gather(spread_out([chunk] * 4, inner_places), (finished[0],))
        pieces = spread_out([chunk] * 4, places)
        finished = finish_experts(steps // 2, steps - steps // 2, sums, finished, (Held(chunk),))
        pieces[3] = held_back(pieces[3], finished[:1], pl.ANY)
        up_grad, up_bias_grad, down_grad, down_bias_grad = finished
        outs = run(
            functools.partial(finish_shared_kernel, experts),
            (
                jnp.concatenate([core, place, inner_place]),
                *map(Held, pieces),
                *(Held(hop(piece, 1, 0)) for piece in pieces),
                Held(small),
            ),
            (shape((width, width), F32),) * 4
            + (shape((1, width), F32),) * 4
            + (shape((experts, width), F32), shape((2, experts), jnp.int32)),
            32,
            3,
            "finish_shared",
        )
        query_grad, key_grad, value_grad, out_w_grad, g_one, s_one, g_two, s_two, router_grad, tallies = outs
        return (
            block_out,
            tokens_grad,
            g_one[0],
            s_one[0],
            query_grad,
            key_grad,
            value_grad,
            out_w_grad,
            g_two[0],
            s_two[0],
            router_grad.T,
            up_grad[None],
            up_bias_grad,
            down_grad[None],
            down_bias_grad,
            tallies.T,
        )

    tokens_spec = P(("narrow", "wide"), None)
    in_specs = (
        (tokens_spec,)
        + (P(),) * 9
        + (P("wide", None, None), P("wide", None), P("wide", None, None), P("wide", None))
        + (tokens_spec,) * 3
    )
    out_specs = (
        (tokens_spec,) * 2
        + (P(),) * 9
        + (P("wide", None, None), P("wide", None), P("wide", None, None), P("wide", None))
        + (P(),)
    )
    return jax.shard_map(body, mesh=mesh, in_specs=in_specs, out_specs=out_specs, check_vma=False)
```

```python
import functools
import math

import jax
import jax.numpy as jnp
from jax import lax
from jax.experimental import pallas as pl
from jax.experimental.pallas import tpu as pltpu
from jax.sharding import PartitionSpec as P

HEADS = 8
PATCHES = 48
EPSILON = 1e-06
LANES = 128
MIB = 1 << 20
F32 = jnp.float32
BF16 = jnp.bfloat16

VMEM = functools.partial(pl.BlockSpec, memory_space=pltpu.VMEM)
SMEM = functools.partial(pl.BlockSpec, memory_space=pltpu.SMEM)


def shape(dims, dtype):
    return jax.ShapeDtypeStruct(dims, dtype)


def dot(a, b):
    return jnp.dot(a, b, preferred_element_type=F32)


def dot_nt(a, b):
    return lax.dot_general(a, b, (((1,), (1,)), ((), ())), preferred_element_type=F32)


def dot_tn(a, b):
    return lax.dot_general(a, b, (((0,), (0,)), ((), ())), preferred_element_type=F32)


def params(mib):
    return pltpu.CompilerParams(vmem_limit_bytes=mib * MIB)


def cost(us):
    return pl.CostEstimate(flops=int(us * 1.0e9), bytes_accessed=int(us * 1.0e5), transcendentals=0)


class Held:
    def __init__(self, value):
        self.value = value
        self.shape, self.dtype, self.ndim = value.shape, value.dtype, value.ndim


def placed(value):
    if isinstance(value, Held):
        return value.value
    if isinstance(value, Part):
        value = value.value
    return value if value.ndim == 1 else pltpu.with_memory_space_constraint(value, pltpu.HBM)


def whole_spec(dims):
    return pl.BlockSpec(tuple(dims), lambda *_: (0,) * len(dims))


def held(dims, dtype):
    return pltpu.VMEM(tuple(dims), dtype)


def far(dims, dtype):
    return pltpu.HBM(tuple(dims), dtype)


def loose(value):
    return pl.BlockSpec(memory_space=pl.ANY if isinstance(value, Held) else pltpu.HBM)


def run(kernel, args, outs, mib, us, name, scratch=(), after=(), grid=(1,), in_specs=None, out_specs=None, free=False, **more):
    given = len(args)
    if in_specs is None:
        in_specs = [SMEM() if a.ndim == 1 else whole_spec(a.shape) for a in args]
    if out_specs is None:
        out_specs = [whole_spec(o.shape) for o in outs]

    def body(*refs):
        kernel(*refs[:given], *refs[given + len(after) :])

    return pl.pallas_call(
        body,
        grid=grid,
        in_specs=list(in_specs) + [loose(value) for value in after],
        out_specs=tuple(out_specs),
        out_shape=tuple(shape(o.shape, o.dtype) if free else far(o.shape, o.dtype) for o in outs),
        scratch_shapes=list(scratch),
        compiler_params=params(mib),
        cost_estimate=cost(us),
        name=name,
        **more,
    )(*map(placed, args), *map(placed, after))


class Part:
    def __init__(self, value, tile, at, rows=False):
        some, all_of = slice(at * tile, (at + 1) * tile), slice(None)
        self.value, self.index = value, (some, all_of) if rows else (all_of, some)
        self.shape = (tile, value.shape[1]) if rows else (value.shape[0], tile)
        self.dtype, self.ndim = value.dtype, 2


class Arriving:
    def __init__(self, source, target, semaphore):
        self.target, self.shape = target, target.shape
        self.copy = pltpu.make_async_copy(source, target, semaphore)
        self.copy.start()
        self.here = False

    def wait(self):
        if not self.here:
            self.copy.wait()
            self.here = True

    def __getitem__(self, index):
        self.wait()
        return self.target[index]


class Leaving:
    def __init__(self, source, target, semaphores):
        self.source, self.target, self.semaphores = source, target, semaphores
        self.shape = source.shape
        self.copies = []

    def __getitem__(self, index):
        return self.source[index]

    def __setitem__(self, index, value):
        self.source[index] = value

    def flush(self, *index):
        one, two = (self.source.at[index], self.target.at[index]) if index else (self.source, self.target)
        self.copies.append(pltpu.make_async_copy(one, two, self.semaphores.at[len(self.copies)]))
        self.copies[-1].start()

    def wait(self):
        for copy in self.copies:
            copy.wait()


def fuse(kernel, args, outs, mib, us, name, scratch=(), after=()):
    is_far = [not isinstance(a, Held) and a.ndim > 1 for a in args]
    out_far = [o.memory_space == pltpu.HBM for o in outs]
    given, made = len(args), len(outs)

    def body(*refs):
        ins, refs = list(refs[:given]), refs[given + len(after) :]
        results, refs = list(refs[:made]), list(refs[made:])
        arrivals, departures = refs.pop(), refs.pop()
        coming, going = [], []
        for at in range(given):
            if is_far[at]:
                source = ins[at].at[args[at].index] if isinstance(args[at], Part) else ins[at]
                ins[at] = Arriving(source, refs.pop(0), arrivals.at[len(coming)])
                coming.append(ins[at])
        for at in range(made):
            if out_far[at]:
                results[at] = Leaving(refs.pop(0), results[at], departures.at[len(going)])
                going.append(results[at])
        kernel(*ins, *results, *refs)
        for item in coming + going:
            item.wait()

    def spec(value):
        if isinstance(value, Held):
            return VMEM()
        return SMEM() if value.ndim == 1 else pl.BlockSpec(memory_space=pltpu.HBM)

    return pl.pallas_call(
        body,
        in_specs=[spec(a) for a in args] + [loose(value) for value in after],
        out_specs=tuple(pl.BlockSpec(memory_space=o.memory_space) for o in outs),
        out_shape=tuple(outs),
        scratch_shapes=[pltpu.VMEM(a.shape, a.dtype) for a, there in zip(args, is_far) if there]
        + [pltpu.VMEM(o.shape, o.dtype) for o, there in zip(outs, out_far) if there]
        + list(scratch)
        + [pltpu.SemaphoreType.DMA((max(sum(out_far), 1), 8)), pltpu.SemaphoreType.DMA((max(sum(is_far), 1),))],
        compiler_params=params(mib),
        cost_estimate=cost(us),
        name=name,
    )(*map(placed, args), *map(placed, after))


def norm_rows(values):
    center = values - jnp.mean(values, axis=-1, keepdims=True)
    spread = jnp.mean(center * center, axis=-1, keepdims=True)
    rate = lax.rsqrt(spread + EPSILON)
    return center * rate, rate


def norm_back(hat, rate, gain, grad):
    scaled = grad * gain
    mean_one = jnp.mean(scaled, axis=-1, keepdims=True)
    mean_two = jnp.mean(scaled * hat, axis=-1, keepdims=True)
    return rate * (scaled - mean_one - hat * mean_two)


def route(capacity, experts, picks_ref, ranks_ref, spread_ref, target_ref, count_ref):
    count = picks_ref.shape[1]
    slots_all = experts * capacity
    span = 1 << (2 * count - 1).bit_length()
    picks = picks_ref[...].astype(F32)
    base = picks * span
    order = base + ranks_ref[...].astype(F32)
    padded = jnp.concatenate([picks, order, jnp.zeros((4, count), F32)], axis=0)
    turned = jnp.transpose(padded)
    targets = []
    for j in range(2):
        row = order[j : j + 1]
        floor = base[j : j + 1]
        slot = jnp.zeros((1, count), F32)
        for other in range(2):
            column = turned[:, 2 + other : 3 + other]
            ahead = (column < row) & (column >= floor)
            slot = slot + jnp.sum(jnp.where(ahead, 1.0, 0.0), axis=0, keepdims=True)
        kept = slot < capacity
        targets.append(jnp.where(kept, picks[j : j + 1] * capacity + slot, float(slots_all)))
    target_turned = jnp.transpose(jnp.concatenate(targets + [jnp.zeros((6, count), F32)], axis=0))
    target_ref[...] = target_turned
    lane = lax.broadcasted_iota(jnp.int32, (count, LANES), 1).astype(F32)
    kept_count = jnp.zeros((1, LANES), F32)
    all_count = jnp.zeros((1, LANES), F32)
    for j in range(2):
        named = jnp.where(turned[:, j : j + 1] == lane, 1.0, 0.0)
        live = jnp.where(target_turned[:, j : j + 1] < slots_all, 1.0, 0.0)
        all_count = all_count + jnp.sum(named, axis=0, keepdims=True)
        kept_count = kept_count + jnp.sum(named * live, axis=0, keepdims=True)
    count_ref[...] = jnp.concatenate([kept_count, all_count - kept_count, jnp.zeros((6, LANES), F32)], axis=0)
    step = 64
    for start in range(0, slots_all, step):
        index = lax.broadcasted_iota(jnp.int32, (step, count), 0).astype(F32) + float(start)
        hit = (index == targets[0]) | (index == targets[1])
        spread_ref[start : start + step, :] = jnp.where(hit, 1.0, 0.0).astype(BF16)


def head_masks(width):
    lane = lax.broadcasted_iota(jnp.int32, (1, width), 1)
    return lane < width // 2


def stack_heads(pair, low):
    zero = jnp.zeros_like(pair)
    return jnp.concatenate([jnp.where(low, pair, zero), jnp.where(low, zero, pair)], axis=0)


def attention_kernel(
    capacity,
    experts,
    picks_ref,
    ranks_ref,
    tokens_ref,
    gain_one_ref,
    shift_one_ref,
    query_w_ref,
    key_w_ref,
    value_w_ref,
    out_w_ref,
    gain_two_ref,
    shift_two_ref,
    target_ref,
    count_ref,
    resid_ref,
    normed_ref,
    query_ref,
    key_ref,
    value_ref,
    weight_ref,
    mixed_ref,
    sent_ref,
    spread_ref,
):
    count, width = tokens_ref.shape
    route(capacity, experts, picks_ref, ranks_ref, spread_ref, target_ref, count_ref)
    target_ref.flush()
    count_ref.flush()
    inputs = tokens_ref[...].astype(F32)
    hat, _ = norm_rows(inputs)
    normed_ref[...] = (hat * gain_one_ref[...] + shift_one_ref[...]).astype(BF16)
    normed_ref.flush()
    normed = normed_ref[...]
    scale = 1.0 / math.sqrt(width // HEADS)
    query_ref[...] = (dot(normed, query_w_ref[...]).astype(BF16).astype(F32) * scale).astype(BF16)
    query_ref.flush()
    key_ref[...] = dot(normed, key_w_ref[...]).astype(BF16)
    key_ref.flush()
    value_ref[...] = dot(normed, value_w_ref[...]).astype(BF16)
    value_ref.flush()
    pairs = HEADS // 2
    wide = width // pairs
    block = 2 * PATCHES
    low = head_masks(wide)
    row_image = (lax.broadcasted_iota(jnp.int32, (2 * block, block), 0) % block) // PATCHES
    column_image = lax.broadcasted_iota(jnp.int32, (2 * block, block), 1) // PATCHES
    bias = jnp.where(row_image == column_image, 0.0, -1e30)
    together = 1
    cells = [(item, pair) for item in range(count // block) for pair in range(pairs)]
    for start in range(0, len(cells), together):
        work = []
        for item, pair in cells[start : start + together]:
            rows = slice(item * block, (item + 1) * block)
            lanes = slice(pair * wide, (pair + 1) * wide)
            scores = dot_nt(stack_heads(query_ref[rows, lanes], low), key_ref[rows, lanes]) + bias
            work.append((rows, lanes, scores))
        tops = [jnp.max(scores, axis=-1, keepdims=True) for _, _, scores in work]
        powers = [jnp.exp(scores - top) for (_, _, scores), top in zip(work, tops)]
        totals = [jnp.sum(power, axis=-1, keepdims=True) for power in powers]
        lows = [(power / total).astype(BF16) for power, total in zip(powers, totals)]
        for (item, pair), weights in zip(cells[start : start + together], lows):
            weight_ref[item, pair] = weights
        for (rows, lanes, _), weights in zip(work, lows):
            mixed = dot(weights, value_ref[rows, lanes])
            mixed_ref[rows, lanes] = jnp.where(low, mixed[:block], mixed[block:]).astype(BF16)
    weight_ref.flush()
    mixed_ref.flush()
    resid = inputs + dot(mixed_ref[...], out_w_ref[...])
    resid_ref[...] = resid
    resid_ref.flush()
    hat, _ = norm_rows(resid)
    second = (hat * gain_two_ref[...] + shift_two_ref[...]).astype(BF16)
    sent_ref[...] = dot(spread_ref[...], second).astype(BF16)


def dispatch_kernel(target_ref, given_ref, sent_ref):
    sent_ref[...] = dot_tn(one_hot_rows(target_ref, sent_ref.shape[0]), given_ref[...]).astype(BF16)


def forward_kernel(experts, tile, me_ref, rows_ref, router_ref, up_bias_ref, *refs):
    ups = refs[:-4]
    hidden_ref, slope_ref, gate_ref, gates_ref = refs[-4:]
    total = rows_ref.shape[0]
    chunk = total // 4
    root = math.sqrt(2.0 / math.pi)
    rows = rows_ref[...]
    lane = lax.broadcasted_iota(jnp.int32, (total, LANES), 1)
    logits = jnp.where(lane < experts, dot_nt(rows, router_ref[...]), -1e30)
    powers = jnp.exp(logits - jnp.max(logits, axis=-1, keepdims=True))
    gates = powers / jnp.sum(powers, axis=-1, keepdims=True)
    gates_ref[...] = gates
    gates_ref.flush()
    gate = jnp.sum(jnp.where(lane == me_ref[0], gates, 0.0), axis=-1, keepdims=True)
    gate_ref[...] = jnp.broadcast_to(gate, (total, LANES))
    gate_ref.flush()
    for step, up_ref in enumerate(ups):
        lanes = slice(step * tile, (step + 1) * tile)
        for start in range(0, total, chunk):
            at = slice(start, start + chunk)
            inner = dot(rows[at], up_ref[...]) + up_bias_ref[:, lanes]
            square = inner * inner
            half = 0.5 + 0.5 * jnp.tanh(inner * (root + (root * 0.044715) * square))
            hidden = inner * half
            slope = half + (hidden - hidden * half) * (2.0 * root + (6.0 * root * 0.044715) * square)
            hidden_ref[at, lanes] = hidden.astype(BF16)
            slope_ref[at, lanes] = slope.astype(BF16)
        hidden_ref.flush(slice(None), lanes)
        slope_ref.flush(slice(None), lanes)


def produce_kernel(hidden_ref, down_ref, down_bias_ref, gate_ref, out_ref, *refs):
    parts, total_s = refs[:-1], refs[-1]
    step = pl.program_id(0)
    made = dot(hidden_ref[...], down_ref[...])

    @pl.when(step == 0)
    def _():
        total_s[...] = made

    @pl.when(step > 0)
    def _():
        total_s[...] += made

    @pl.when(step == pl.num_programs(0) - 1)
    def _():
        produced = (total_s[...] + down_bias_ref[...]).astype(BF16)
        out_ref[...] = produced
        size = parts[0].shape[1]
        gate = jnp.concatenate([gate_ref[...]] * (size // LANES), axis=1)
        for at, ref in enumerate(parts):
            ref[...] = (produced[:, at * size : (at + 1) * size].astype(F32) * gate).astype(BF16)


def expert_kernel(experts, tile, me_ref, grad_ref, gate_ref, *refs):
    steps = (len(refs) - 6) // 3
    downs, slopes, ups = [refs[0], *refs[6 : 3 * steps + 3 : 3]], [refs[1], *refs[7 : 3 * steps + 3 : 3]], [refs[2], *refs[8 : 3 * steps + 3 : 3]]
    produced_ref, gates_ref, router_ref = refs[3:6]
    inner_grad_ref, rows_grad_ref, logit_grad_ref = refs[3 * steps + 3 :]
    total, width = grad_ref.shape
    gate = jnp.concatenate([gate_ref[...]] * (tile // LANES), axis=1)
    for step in range(steps):
        lanes = slice(step * tile, (step + 1) * tile)
        made = dot_nt(grad_ref[...], downs[step][...]) * gate * slopes[step][...].astype(F32)
        inner_grad_ref[:, lanes] = made.astype(BF16)
        inner_grad_ref.flush(slice(None), lanes)
        if step == 0:
            lane = lax.broadcasted_iota(jnp.int32, (total, LANES), 1)
            product = grad_ref[...].astype(F32) * produced_ref[...].astype(F32)
            pair_grad = jnp.sum(product, axis=-1, keepdims=True)
            own = jnp.where(lane == me_ref[0], 1.0, 0.0)
            logit_grad = (gates_ref[...] * (own - gate_ref[...]) * pair_grad).astype(BF16)
            logit_grad_ref[...] = logit_grad
            logit_grad_ref.flush()
    made = dot(logit_grad, router_ref[...])
    for step in range(steps):
        made = made + dot_nt(inner_grad_ref[:, step * tile : (step + 1) * tile], ups[step][...])
    rows_grad_ref[...] = made.astype(BF16)


def weight_kernel(sets, again, *refs):
    groups, refs = [refs[at * 5 : at * 5 + 5] for at in range(sets)], refs[5 * sets :]
    earlier, refs = refs[:again], refs[again:]
    extra_ref, out_ref, refs = refs[0], refs[1], refs[2:]
    router_refs, gated_s, inner_grad_s = refs[:-2], refs[-2], refs[-1]
    total, width = groups[0][0].shape

    @pl.when(pl.program_id(0) == 0)
    def _():
        for at, some in enumerate(groups):
            gate = jnp.concatenate([some[2][...]] * (width // LANES), axis=1)
            gated_s[at] = (gate * some[1][...].astype(F32)).astype(BF16)
        if router_refs:
            router_refs[0][...] = dot_tn(extra_ref[...], groups[0][0][...])[: router_refs[0].shape[0]]

    ups, downs, up_biases, down_biases = [], [], [], []
    for at, (rows_ref, grad_ref, gate_ref, hidden_ref, inner_grad_ref) in enumerate(groups):
        if again:
            slope_ref, inner_grad_ref = inner_grad_ref, inner_grad_s
            gate = jnp.concatenate([gate_ref[...]] * (width // LANES), axis=1)
            made = dot_nt(grad_ref[...], extra_ref[...]) * gate * slope_ref[...].astype(F32)
            inner_grad_s[...] = made.astype(BF16)
        inner_grad = inner_grad_ref[...]
        ups.append(dot_tn(rows_ref[...], inner_grad))
        downs.append(dot_tn(hidden_ref[...], gated_s[at]))
        up_biases.append(jnp.sum(inner_grad.astype(F32), axis=0, keepdims=True))
        down_biases.append(jnp.sum(gated_s[at].astype(F32), axis=0, keepdims=True))

    def put(some, parts):
        made = sum(parts[1:], parts[0]).astype(BF16)
        if again:
            made = (made.astype(F32) + earlier[0][0, some, :].astype(F32)).astype(BF16)
        out_ref[0, some, :] = made

    put(slice(0, width), ups)
    put(slice(width, 2 * width), downs)
    row = lax.broadcasted_iota(jnp.int32, (16, width), 0)
    small = jnp.where(row == 0, sum(up_biases[1:], up_biases[0]), sum(down_biases[1:], down_biases[0]))
    put(slice(2 * width, None), [small])


def finish_experts_kernel(*refs):
    parts, (up_ref, up_bias_ref, down_ref, down_bias_ref) = refs[:2], refs[-4:]
    tall = up_ref.shape[0]

    def total(some):
        return sum_in_tree([ref[0, some, :].astype(F32) for ref in parts])

    up_ref[...] = total(slice(0, tall))
    down_ref[...] = total(slice(tall, 2 * tall))
    small = total(slice(2 * tall, None))
    up_bias_ref[...] = small[0:1]
    down_bias_ref[...] = small[1:2]


def one_hot_rows(target_ref, slots_all):
    count = target_ref.shape[0]
    lane = lax.broadcasted_iota(jnp.int32, (64, slots_all), 1).astype(F32)
    pieces = []
    for start in range(0, count, 64):
        one = target_ref[start : start + 64, 0:1]
        two = target_ref[start : start + 64, 1:2]
        pieces.append(jnp.where((lane == one) | (lane == two), 1.0, 0.0).astype(BF16))
    return jnp.concatenate(pieces, axis=0)


def combine_kernel(target_ref, resid_ref, *refs):
    parts, out_ref = refs[:-1], refs[-1]
    picked = one_hot_rows(target_ref, parts[0].shape[0])
    size = parts[0].shape[1]
    for at, ref in enumerate(parts):
        lanes = slice(at * size, (at + 1) * size)
        out_ref[:, lanes] = (resid_ref[:, lanes] + dot(picked, ref[...])).astype(BF16)


def backward_kernel(
    experts,
    core_ref,
    back_ref,
    target_ref,
    resid_ref,
    gain_two_ref,
    grad_ref,
    mixed_ref,
    out_w_ref,
    value_ref,
    query_ref,
    weight_ref,
    key_ref,
    normed_ref,
    query_w_ref,
    key_w_ref,
    value_w_ref,
    tokens_ref,
    gain_one_ref,
    count_ref,
    router_grad_ref,
    keep_ref,
    send_ref,
    tokens_grad_ref,
    queries_s,
    keys_s,
    values_s,
    mixed_grad_s,
    resid_grad_s,
):
    count, width = grad_ref.shape
    picked = one_hot_rows(target_ref, back_ref.shape[0])
    second_grad = dot(picked, back_ref[...])
    hat, rate = norm_rows(resid_ref[...])
    gain_two_grad = jnp.sum(second_grad * hat, axis=0, keepdims=True)
    shift_two_grad = jnp.sum(second_grad, axis=0, keepdims=True)
    resid_grad_s[...] = grad_ref[...].astype(F32) + norm_back(hat, rate, gain_two_ref[...], second_grad)
    branch = resid_grad_s[...].astype(BF16)
    half = width // 2
    first = core_ref[0] == 0

    def put(at, value):
        value = value.astype(BF16)
        keep_ref[at * half : (at + 1) * half, :] = jnp.where(first, value[:half], value[half:])
        send_ref[at * half : (at + 1) * half, :] = jnp.where(first, value[half:], value[:half])
        keep_ref.flush(slice(at * half, (at + 1) * half))

    put(3, dot_tn(mixed_ref[...], branch))
    mixed_grad_s[...] = dot_nt(branch, out_w_ref[...]).astype(BF16)
    pairs = HEADS // 2
    wide = width // pairs
    block = 2 * PATCHES
    scale = 1.0 / math.sqrt(width // HEADS)
    low = head_masks(wide)
    together = 8
    cells = [(item, pair) for item in range(count // block) for pair in range(pairs)]
    for start in range(0, len(cells), together):
        work = []
        for item, pair in cells[start : start + together]:
            rows = slice(item * block, (item + 1) * block)
            lanes = slice(pair * wide, (pair + 1) * wide)
            mixed_stack = stack_heads(mixed_grad_s[rows, lanes], low)
            weights = weight_ref[item, pair]
            work.append((rows, lanes, mixed_stack, weights, dot_nt(mixed_stack, value_ref[rows, lanes])))
        score_grads = []
        for rows, lanes, mixed_stack, weights, weight_grad in work:
            product = weights.astype(F32) * weight_grad
            score_grad = product - weights.astype(F32) * jnp.sum(product, axis=-1, keepdims=True)
            score_grads.append(score_grad.astype(BF16))
        for rows, lanes, mixed_stack, weights, _ in work:
            values_s[rows, lanes] = dot_tn(weights, mixed_stack).astype(BF16)
        for (rows, lanes, *_), score_grad in zip(work, score_grads):
            made = dot(score_grad, key_ref[rows, lanes]) * scale
            queries_s[rows, lanes] = jnp.where(low, made[:block], made[block:]).astype(BF16)
        for (rows, lanes, *_), score_grad in zip(work, score_grads):
            keys_s[rows, lanes] = dot_tn(score_grad, stack_heads(query_ref[rows, lanes], low)).astype(BF16)
    normed = normed_ref[...]
    put(0, dot_tn(normed, queries_s[...]))
    put(1, dot_tn(normed, keys_s[...]))
    put(2, dot_tn(normed, values_s[...]))
    normed_grad = (
        dot_nt(queries_s[...], query_w_ref[...])
        + dot_nt(keys_s[...], key_w_ref[...])
        + dot_nt(values_s[...], value_w_ref[...])
    )
    hat, rate = norm_rows(tokens_ref[...].astype(F32))
    gain_one_grad = jnp.sum(normed_grad * hat, axis=0, keepdims=True)
    shift_one_grad = jnp.sum(normed_grad, axis=0, keepdims=True)
    tokens_grad_ref[...] = (resid_grad_s[...] + norm_back(hat, rate, gain_one_ref[...], normed_grad)).astype(BF16)
    tokens_grad_ref.flush()
    digits = []
    for kind in range(2):
        value = count_ref[kind : kind + 1, :]
        high = jnp.floor(value * (1.0 / 128.0))
        digits.append(jnp.concatenate([value - 128.0 * high, high] + [jnp.zeros_like(value)] * (width // LANES - 2), axis=1))
    extra = keep_ref.shape[0] - 4 * half
    small = [gain_one_grad, shift_one_grad, gain_two_grad, shift_two_grad] + digits + [router_grad_ref[:experts, :]]
    small = jnp.concatenate(small + [jnp.zeros((extra - 6 - experts, width), F32)], axis=0).astype(BF16)
    keep_ref[4 * half :, :] = small
    send_ref[4 * half :, :] = small
    keep_ref.flush(slice(4 * half, None))


def carry_digits(total):
    row = lax.broadcasted_iota(jnp.int32, (total.shape[0], LANES), 0)
    one, two, three = (total[:, at * LANES : (at + 1) * LANES] for at in range(3))
    over = jnp.floor(one * (1.0 / 128.0))
    two_full = two + over
    over_two = jnp.floor(two_full * (1.0 / 128.0))
    parts = [one - 128.0 * over, two_full - 128.0 * over_two, three + over_two]
    is_count = (row == 4) | (row == 5)
    parts = [jnp.where(is_count, part, total[:, at * LANES : (at + 1) * LANES]) for at, part in enumerate(parts)]
    return jnp.concatenate(parts + [total[:, 3 * LANES :]], axis=1)


def sum_in_tree(values):
    while len(values) > 1:
        values = [values[at] + values[at + 1] for at in range(0, len(values), 2)]
    return values[0]


def share_kernel(given, pieces, *refs):
    index_ref, arrived, made = refs[0], refs[1 : 1 + given], refs[1 + given :]
    small_rows = (pieces * made[0].shape[0] - arrived[0].shape[0]) // (pieces - 1)
    size = made[0].shape[0] - small_rows
    top = pieces * size
    small = carry_digits(sum_in_tree([ref[top:, :].astype(F32) for ref in arrived])).astype(BF16)
    for away in range(pieces):
        at = pl.ds(pl.multiple_of((index_ref[0] ^ away) * size, size), size)
        made[away][:size, :] = sum_in_tree([ref[at, :].astype(F32) for ref in arrived]).astype(BF16)
        made[away][size:, :] = small


def copy_kernel(given_ref, made_ref, arrival):
    copy = pltpu.make_async_copy(given_ref, made_ref, arrival)
    copy.start()
    copy.wait()


def pass_kernel(given_ref, same_ref):
    pass


def gather_kernel(*refs):
    arrived, out_ref = refs[:-1], refs[-1]
    size = arrived[0].shape[0]
    for at, ref in enumerate(arrived):
        out_ref[at * size : (at + 1) * size, :] = ref[...]


def last_kernel(given, *refs):
    arrived, chunk_ref, small_ref = refs[:given], refs[given], refs[given + 1]
    size = chunk_ref.shape[0]
    chunk_ref[...] = sum_in_tree([ref[:size, :].astype(F32) for ref in arrived]).astype(BF16)
    small_ref[...] = carry_digits(sum_in_tree([ref[size:, :].astype(F32) for ref in arrived])).astype(BF16)


def finish_shared_kernel(experts, index_ref, *refs):
    own, others, small_ref, outs = refs[:4], refs[4:8], refs[8], refs[9:]
    vector_refs, router_ref, count_ref = outs[4:8], outs[8], outs[9]
    core, place, inner_place = index_ref[0], index_ref[1], index_ref[2]
    half = outs[0].shape[1] // 2
    size = half // 4
    for pieces, side in ((own, core), (others, 1 - core)):
        for away, piece in enumerate(pieces):
            for at in range(4):

                @pl.when((place ^ away) == at)
                def _(piece=piece, side=side, out=outs[at]):
                    for part in range(4):
                        start = pl.multiple_of((inner_place ^ part) * size, size)
                        row = pl.multiple_of(side * half + part * size, size)
                        out[pl.ds(row, size), :] = piece[pl.ds(start, size), :].astype(F32)

    small = small_ref[...].astype(F32)
    for at, ref in enumerate(vector_refs):
        ref[...] = small[at : at + 1, :]
    router_ref[...] = small[6 : 6 + experts, :]
    value = small[4:6, :LANES] + 128.0 * small[4:6, LANES : 2 * LANES] + 16384.0 * small[4:6, 2 * LANES : 3 * LANES]
    count_ref[...] = value[:, :experts].astype(jnp.int32)


def solution(mesh):
    narrow, wide = mesh.shape["narrow"], mesh.shape["wide"]

    def hop(value, narrow_bits, wide_bits):
        if wide_bits == 0:
            return lax.ppermute(value, "narrow", [(i, i ^ narrow_bits) for i in range(narrow)])
        if narrow_bits == 0:
            return lax.ppermute(value, "wide", [(i, i ^ wide_bits) for i in range(wide)])
        pairs = [
            (i * wide + j, (i ^ narrow_bits) * wide + (j ^ wide_bits)) for i in range(narrow) for j in range(wide)
        ]
        return lax.ppermute(value, ("narrow", "wide"), pairs)

    def body(
        tokens,
        gain_one,
        shift_one,
        query_w,
        key_w,
        value_w,
        out_w,
        gain_two,
        shift_two,
        router_w,
        up_w,
        up_bias,
        down_w,
        down_bias,
        picks,
        ranks,
        out_grad,
    ):
        count, width = tokens.shape
        experts = router_w.shape[1]
        capacity = ((21 * 2 * count + 20 * experts - 1) // (20 * experts) + 7) // 8 * 8
        slots_all = experts * capacity
        hidden_width = up_w.shape[2]
        half = width // 2
        pairs = HEADS // 2
        blocks = count // (2 * PATCHES)
        extra = (6 + experts + 15) // 16 * 16
        tile = width
        steps = hidden_width // tile
        narrow_at, wide_at = lax.axis_index("narrow"), lax.axis_index("wide")
        core = (narrow_at & 1)[None].astype(jnp.int32)
        place = (((narrow_at >> 1) & 1) * 2 + (wide_at & 1))[None].astype(jnp.int32)
        inner_place = ((wide_at >> 1) & 3)[None].astype(jnp.int32)
        gain_one, shift_one, gain_two, shift_two = (v[None, :] for v in (gain_one, shift_one, gain_two, shift_two))
        router_t = jnp.pad(router_w.T, ((0, LANES - experts), (0, 0)))
        up_w, down_w = up_w[0], down_w[0]

        def exchange(value):
            return lax.all_to_all(value, "wide", split_axis=0, concat_axis=0, tiled=True)

        token_rows = shape((count, width), BF16)
        rows_shape = shape((slots_all, width), BF16)
        lanes_shape = shape((slots_all, LANES), F32)
        narrow_far = far((count, width), BF16)
        target, counts, resid, normed, queries, keys, values, weights, mixed, sent = fuse(
            functools.partial(attention_kernel, capacity, experts),
            (picks.T, ranks.T, tokens, gain_one, shift_one, query_w, key_w, value_w, out_w, gain_two, shift_two),
            (
                far((count, 8), F32),
                far((8, LANES), F32),
                far((count, width), F32),
                narrow_far,
                narrow_far,
                narrow_far,
                narrow_far,
                far((blocks, pairs, 4 * PATCHES, 2 * PATCHES), BF16),
                narrow_far,
                held((slots_all, width), BF16),
            ),
            32,
            10,
            "attention",
            (pltpu.VMEM((slots_all, count), BF16),),
        )
        rows = exchange(sent)
        (grad_sent,) = run(dispatch_kernel, (target, out_grad), (rows_shape,), 16, 1, "dispatch", after=(Held(sent),))
        grad_rows = exchange(grad_sent)

        whole = pl.BlockSpec((slots_all, width), lambda f: (0, 0))
        lanes_whole = pl.BlockSpec((slots_all, LANES), lambda f: (0, 0))
        columns = pl.BlockSpec((slots_all, tile), lambda f: (0, f))
        down_spec = pl.BlockSpec((tile, width), lambda f: (f, 0))
        down_bias_spec = pl.BlockSpec((1, width), lambda f: (0, 0))
        payload = 2 * width + 16
        me = wide_at[None].astype(jnp.int32)
        rows = Held(rows)

        def forward(rows, us, after=()):
            return fuse(
                functools.partial(forward_kernel, experts, tile),
                (me, rows, router_t, up_bias) + tuple(Part(up_w, tile, at) for at in range(steps)),
                (far((slots_all, hidden_width), BF16),) * 2 + (far((slots_all, LANES), F32),) * 2,
                32,
                us,
                "forward",
                after=after,
            )

        hidden, slope, gate, gates = forward(rows, 0.01)
        produced, gated = run(
            produce_kernel,
            (hidden, down_w, down_bias, gate),
            (rows_shape,) * 2,
            32,
            0.01,
            "produce",
            (pltpu.VMEM((slots_all, width), F32),),
            grid=(steps,),
            in_specs=(columns, down_spec, down_bias_spec, lanes_whole),
            out_specs=(whole,) * 2,
        )
        grad_rows = Held(grad_rows)

        def triple(at):
            return Part(down_w, tile, at, rows=True), Part(slope, tile, at), Part(up_w, tile, at)

        rows_others = [hop(rows.value, bits, 0) for bits in range(2, narrow, 2)]
        inner_grad, rows_grad, logit_grad = fuse(
            functools.partial(expert_kernel, experts, tile),
            (me, grad_rows, gate, *triple(0), produced, gates, router_t, *(part for at in range(1, steps) for part in triple(at))),
            (far((slots_all, hidden_width), BF16), held((slots_all, width), BF16), far((slots_all, LANES), BF16)),
            40,
            0.01,
            "experts",
            after=[Held(one) for one in rows_others],
        )
        back = exchange(rows_grad)

        def payload_of(number):
            return shape((number, payload, width), BF16)

        payload_spec = pl.BlockSpec((1, payload, width), lambda f: (f, 0, 0))
        router_spec = pl.BlockSpec((experts, width), lambda f: (0, 0))
        (grad_later,) = run(
            copy_kernel,
            (grad_rows,),
            (rows_shape,),
            4,
            0.01,
            "copy_rows",
            (pltpu.SemaphoreType.DMA,),
            in_specs=(pl.BlockSpec(memory_space=pl.ANY),),
            out_specs=(pl.BlockSpec(memory_space=pltpu.HBM),),
            after=(produced,),
        )

        def held_back(value, after, space=pltpu.HBM):
            return run(
                pass_kernel,
                (value if space == pltpu.HBM else Held(value),),
                (value,),
                1,
                0.01,
                "pass",
                in_specs=(pl.BlockSpec(memory_space=space),),
                out_specs=(pl.BlockSpec(memory_space=space),),
                after=after,
                free=space != pltpu.HBM,
                input_output_aliases={0: 0},
            )[0]

        sets = []
        for bits, rows_of in zip(range(2, narrow, 2), rows_others):
            grad_of = hop(grad_later, bits, 0)
            hidden_of, slope_of, gate_of, _ = forward(rows_of, 0.01, (logit_grad,))
            sets.append((rows_of, grad_of, gate_of, hidden_of, slope_of))

        def weight_part(again, sets, extra, extra_spec, earlier=(), after=()):
            return run(
                functools.partial(weight_kernel, len(sets), int(again)),
                (*(item for one in sets for item in one), *earlier, extra),
                (payload_of(steps),) + (shape((experts, width), F32),) * (not again),
                48,
                0.01,
                "expert_weights",
                (
                    pltpu.VMEM((len(sets), slots_all, width), BF16),
                    pltpu.VMEM((slots_all, tile), BF16),
                ),
                grid=(steps,),
                in_specs=(
                    *(spec for _ in sets for spec in (whole, whole, lanes_whole, columns, columns)),
                    *(payload_spec for _ in earlier),
                    extra_spec,
                ),
                out_specs=(payload_spec,) + (router_spec,) * (not again),
                after=after,
            )

        def finish_experts(start, number, parts, earlier, after=()):
            spec = lambda dims, index: pl.BlockSpec(dims, lambda f: index(start + f))
            return run(
                finish_experts_kernel,
                (*parts, *earlier),
                (
                    shape((width, hidden_width), F32),
                    shape((1, hidden_width), F32),
                    shape((hidden_width, width), F32),
                    shape((1, width), F32),
                ),
                32,
                0.01,
                "finish_experts",
                grid=(number,),
                in_specs=[pl.BlockSpec((1, payload, width), lambda f: (start + f, 0, 0))] * 2
                + [pl.BlockSpec(memory_space=pltpu.HBM)] * len(earlier),
                out_specs=(
                    spec((width, tile), lambda f: (0, f)),
                    spec((1, tile), lambda f: (0, f)),
                    spec((tile, width), lambda f: (f, 0)),
                    down_bias_spec,
                ),
                after=after,
                input_output_aliases={2 + at: at for at in range(len(earlier))},
            )

        own_sum, router_part = weight_part(
            False, [(rows, grad_rows, gate, hidden, inner_grad)], logit_grad, lanes_whole, (), [one[4] for one in sets]
        )
        produced_back = exchange(held_back(gated, (own_sum,)))
        tall = 4 * half + extra
        keep, send, tokens_grad = fuse(
            functools.partial(backward_kernel, experts),
            (
                core,
                Held(back),
                target,
                resid,
                gain_two,
                out_grad,
                mixed,
                out_w,
                values,
                queries,
                weights,
                keys,
                normed,
                query_w,
                key_w,
                value_w,
                tokens,
                gain_one,
                counts,
                router_part,
            ),
            (far((tall, width), BF16), held((tall, width), BF16), far((count, width), BF16)),
            32,
            0.01,
            "backward",
            [pltpu.VMEM((count, width), BF16)] * 4 + [pltpu.VMEM((count, width), F32)],
            after=[own_sum] + [Held(one[1]) for one in sets],
        )

        def share(index, arrived, after=()):
            size = (arrived[0].shape[0] - extra) // 4
            return run(
                functools.partial(share_kernel, len(arrived), 4),
                (index, arrived[0] if size == half else Held(arrived[0]), *map(Held, arrived[1:])),
                (shape((size + extra, width), BF16),) * 4,
                16,
                0.05,
                "share",
                after=after,
                free=True,
            )

        def last(arrived, after=()):
            return run(
                functools.partial(last_kernel, len(arrived)),
                tuple(map(Held, arrived)),
                (shape((half // 4, width), BF16), shape((extra, width), BF16)),
                16,
                0.05,
                "last",
                after=after,
                free=True,
            )

        def gather(arrived, after=()):
            rows_in = sum(value.shape[0] for value in arrived)
            return run(
                gather_kernel,
                tuple(map(Held, arrived)),
                (shape((rows_in, width), BF16),),
                16,
                0.05,
                "gather",
                after=after,
                free=True,
            )[0]

        def spread_out(parts, bits):
            return [parts[0]] + [hop(part, *bit) for part, bit in zip(parts[1:], bits[1:])]

        places = ((0, 0), (0, 1), (2, 0), (2, 1))
        inner_places = ((0, 0), (0, 2), (0, 4), (0, 6))
        parts = share(place, [keep, hop(send, 1, 0)])
        (far_sum,) = weight_part(True, sets, down_w, down_spec, (own_sum,), (Held(parts[0]),))
        parts = share(inner_place, spread_out(parts, places), (far_sum, Held(produced_back)))
        far_sum = held_back(far_sum, (Held(parts[0]),))
        parts = spread_out(parts, inner_places)
        (block_out,) = run(
            combine_kernel, (target, resid, Held(produced_back)), (token_rows,), 16, 0.01, "combine"
        )
        chunk, small = last(parts, (block_out,))
        others = [(bit, 0) for bit in (4, 8, 16, 32, 64) if bit < narrow]
        others += [(0, bit) for bit in (8, 16, 32, 64) if bit < wide]
        for bits in others:
            joined = jnp.concatenate([chunk, small], axis=0)
            chunk, small = last([joined, hop(joined, *bits)])
        sums = (far_sum, Held(hop(far_sum, 1, 0)))
        finished = finish_experts(0, steps // 2, sums, (), (Held(chunk),))
        chunk = gather(spread_out([chunk] * 4, inner_places), (finished[0],))
        pieces = spread_out([chunk] * 4, places)
        finished = finish_experts(steps // 2, steps - steps // 2, sums, finished, (Held(chunk),))
        pieces[3] = held_back(pieces[3], finished[:1], pl.ANY)
        up_grad, up_bias_grad, down_grad, down_bias_grad = finished
        outs = run(
            functools.partial(finish_shared_kernel, experts),
            (
                jnp.concatenate([core, place, inner_place]),
                *map(Held, pieces),
                *(Held(hop(piece, 1, 0)) for piece in pieces),
                Held(small),
            ),
            (shape((width, width), F32),) * 4
            + (shape((1, width), F32),) * 4
            + (shape((experts, width), F32), shape((2, experts), jnp.int32)),
            32,
            3,
            "finish_shared",
        )
        query_grad, key_grad, value_grad, out_w_grad, g_one, s_one, g_two, s_two, router_grad, tallies = outs
        return (
            block_out,
            tokens_grad,
            g_one[0],
            s_one[0],
            query_grad,
            key_grad,
            value_grad,
            out_w_grad,
            g_two[0],
            s_two[0],
            router_grad.T,
            up_grad[None],
            up_bias_grad,
            down_grad[None],
            down_bias_grad,
            tallies.T,
        )

    tokens_spec = P(("narrow", "wide"), None)
    in_specs = (
        (tokens_spec,)
        + (P(),) * 9
        + (P("wide", None, None), P("wide", None), P("wide", None, None), P("wide", None))
        + (tokens_spec,) * 3
    )
    out_specs = (
        (tokens_spec,) * 2
        + (P(),) * 9
        + (P("wide", None, None), P("wide", None), P("wide", None, None), P("wide", None))
        + (P(),)
    )
    return jax.shard_map(body, mesh=mesh, in_specs=in_specs, out_specs=out_specs, check_vma=False)
```

```python
import functools
import math

import jax
import jax.numpy as jnp
from jax import lax
from jax.experimental import pallas as pl
from jax.experimental.pallas import tpu as pltpu
from jax.sharding import PartitionSpec as P

HEADS = 8
PATCHES = 48
EPSILON = 1e-06
LANES = 128
MIB = 1 << 20
F32 = jnp.float32
BF16 = jnp.bfloat16

VMEM = functools.partial(pl.BlockSpec, memory_space=pltpu.VMEM)
SMEM = functools.partial(pl.BlockSpec, memory_space=pltpu.SMEM)


def shape(dims, dtype):
    return jax.ShapeDtypeStruct(dims, dtype)


def dot(a, b):
    return jnp.dot(a, b, preferred_element_type=F32)


def dot_nt(a, b):
    return lax.dot_general(a, b, (((1,), (1,)), ((), ())), preferred_element_type=F32)


def dot_tn(a, b):
    return lax.dot_general(a, b, (((0,), (0,)), ((), ())), preferred_element_type=F32)


def params(mib):
    return pltpu.CompilerParams(vmem_limit_bytes=mib * MIB)


def cost(us):
    return pl.CostEstimate(flops=int(us * 1.0e9), bytes_accessed=int(us * 1.0e5), transcendentals=0)


class Held:
    def __init__(self, value):
        self.value = value
        self.shape, self.dtype, self.ndim = value.shape, value.dtype, value.ndim


def placed(value):
    if isinstance(value, Held):
        return value.value
    if isinstance(value, Part):
        value = value.value
    return value if value.ndim == 1 else pltpu.with_memory_space_constraint(value, pltpu.HBM)


def whole_spec(dims):
    return pl.BlockSpec(tuple(dims), lambda *_: (0,) * len(dims))


def held(dims, dtype):
    return pltpu.VMEM(tuple(dims), dtype)


def far(dims, dtype):
    return pltpu.HBM(tuple(dims), dtype)


def loose(value):
    return pl.BlockSpec(memory_space=pl.ANY if isinstance(value, Held) else pltpu.HBM)


def run(kernel, args, outs, mib, us, name, scratch=(), after=(), grid=(1,), in_specs=None, out_specs=None, free=False, **more):
    given = len(args)
    if in_specs is None:
        in_specs = [SMEM() if a.ndim == 1 else whole_spec(a.shape) for a in args]
    if out_specs is None:
        out_specs = [whole_spec(o.shape) for o in outs]

    def body(*refs):
        kernel(*refs[:given], *refs[given + len(after) :])

    return pl.pallas_call(
        body,
        grid=grid,
        in_specs=list(in_specs) + [loose(value) for value in after],
        out_specs=tuple(out_specs),
        out_shape=tuple(shape(o.shape, o.dtype) if free else far(o.shape, o.dtype) for o in outs),
        scratch_shapes=list(scratch),
        compiler_params=params(mib),
        cost_estimate=cost(us),
        name=name,
        **more,
    )(*map(placed, args), *map(placed, after))


class Part:
    def __init__(self, value, tile, at, rows=False):
        some, all_of = slice(at * tile, (at + 1) * tile), slice(None)
        self.value, self.index = value, (some, all_of) if rows else (all_of, some)
        self.shape = (tile, value.shape[1]) if rows else (value.shape[0], tile)
        self.dtype, self.ndim = value.dtype, 2


class Arriving:
    def __init__(self, source, target, semaphore):
        self.target, self.shape = target, target.shape
        self.copy = pltpu.make_async_copy(source, target, semaphore)
        self.copy.start()
        self.here = False

    def wait(self):
        if not self.here:
            self.copy.wait()
            self.here = True

    def __getitem__(self, index):
        self.wait()
        return self.target[index]


class Leaving:
    def __init__(self, source, target, semaphores):
        self.source, self.target, self.semaphores = source, target, semaphores
        self.shape = source.shape
        self.copies = []

    def __getitem__(self, index):
        return self.source[index]

    def __setitem__(self, index, value):
        self.source[index] = value

    def flush(self, *index):
        one, two = (self.source.at[index], self.target.at[index]) if index else (self.source, self.target)
        self.copies.append(pltpu.make_async_copy(one, two, self.semaphores.at[len(self.copies)]))
        self.copies[-1].start()

    def wait(self):
        for copy in self.copies:
            copy.wait()


def fuse(kernel, args, outs, mib, us, name, scratch=(), after=()):
    is_far = [not isinstance(a, Held) and a.ndim > 1 for a in args]
    out_far = [o.memory_space == pltpu.HBM for o in outs]
    given, made = len(args), len(outs)

    def body(*refs):
        ins, refs = list(refs[:given]), refs[given + len(after) :]
        results, refs = list(refs[:made]), list(refs[made:])
        arrivals, departures = refs.pop(), refs.pop()
        coming, going = [], []
        for at in range(given):
            if is_far[at]:
                source = ins[at].at[args[at].index] if isinstance(args[at], Part) else ins[at]
                ins[at] = Arriving(source, refs.pop(0), arrivals.at[len(coming)])
                coming.append(ins[at])
        for at in range(made):
            if out_far[at]:
                results[at] = Leaving(refs.pop(0), results[at], departures.at[len(going)])
                going.append(results[at])
        kernel(*ins, *results, *refs)
        for item in coming + going:
            item.wait()

    def spec(value):
        if isinstance(value, Held):
            return VMEM()
        return SMEM() if value.ndim == 1 else pl.BlockSpec(memory_space=pltpu.HBM)

    return pl.pallas_call(
        body,
        in_specs=[spec(a) for a in args] + [loose(value) for value in after],
        out_specs=tuple(pl.BlockSpec(memory_space=o.memory_space) for o in outs),
        out_shape=tuple(outs),
        scratch_shapes=[pltpu.VMEM(a.shape, a.dtype) for a, there in zip(args, is_far) if there]
        + [pltpu.VMEM(o.shape, o.dtype) for o, there in zip(outs, out_far) if there]
        + list(scratch)
        + [pltpu.SemaphoreType.DMA((max(sum(out_far), 1), 8)), pltpu.SemaphoreType.DMA((max(sum(is_far), 1),))],
        compiler_params=params(mib),
        cost_estimate=cost(us),
        name=name,
    )(*map(placed, args), *map(placed, after))


def norm_rows(values):
    center = values - jnp.mean(values, axis=-1, keepdims=True)
    spread = jnp.mean(center * center, axis=-1, keepdims=True)
    rate = lax.rsqrt(spread + EPSILON)
    return center * rate, rate


def norm_back(hat, rate, gain, grad):
    scaled = grad * gain
    mean_one = jnp.mean(scaled, axis=-1, keepdims=True)
    mean_two = jnp.mean(scaled * hat, axis=-1, keepdims=True)
    return rate * (scaled - mean_one - hat * mean_two)


def route(capacity, experts, picks_ref, ranks_ref, spread_ref, target_ref, count_ref):
    count = picks_ref.shape[1]
    slots_all = experts * capacity
    span = 1 << (2 * count - 1).bit_length()
    picks = picks_ref[...].astype(F32)
    base = picks * span
    order = base + ranks_ref[...].astype(F32)
    padded = jnp.concatenate([picks, order, jnp.zeros((4, count), F32)], axis=0)
    turned = jnp.transpose(padded)
    targets = []
    for j in range(2):
        row = order[j : j + 1]
        floor = base[j : j + 1]
        slot = jnp.zeros((1, count), F32)
        for other in range(2):
            column = turned[:, 2 + other : 3 + other]
            ahead = (column < row) & (column >= floor)
            slot = slot + jnp.sum(jnp.where(ahead, 1.0, 0.0), axis=0, keepdims=True)
        kept = slot < capacity
        targets.append(jnp.where(kept, picks[j : j + 1] * capacity + slot, float(slots_all)))
    target_turned = jnp.transpose(jnp.concatenate(targets + [jnp.zeros((6, count), F32)], axis=0))
    target_ref[...] = target_turned
    lane = lax.broadcasted_iota(jnp.int32, (count, LANES), 1).astype(F32)
    kept_count = jnp.zeros((1, LANES), F32)
    all_count = jnp.zeros((1, LANES), F32)
    for j in range(2):
        named = jnp.where(turned[:, j : j + 1] == lane, 1.0, 0.0)
        live = jnp.where(target_turned[:, j : j + 1] < slots_all, 1.0, 0.0)
        all_count = all_count + jnp.sum(named, axis=0, keepdims=True)
        kept_count = kept_count + jnp.sum(named * live, axis=0, keepdims=True)
    count_ref[...] = jnp.concatenate([kept_count, all_count - kept_count, jnp.zeros((6, LANES), F32)], axis=0)
    step = 64
    for start in range(0, slots_all, step):
        index = lax.broadcasted_iota(jnp.int32, (step, count), 0).astype(F32) + float(start)
        hit = (index == targets[0]) | (index == targets[1])
        spread_ref[start : start + step, :] = jnp.where(hit, 1.0, 0.0).astype(BF16)


def head_masks(width):
    lane = lax.broadcasted_iota(jnp.int32, (1, width), 1)
    return lane < width // 2


def stack_heads(pair, low):
    zero = jnp.zeros_like(pair)
    return jnp.concatenate([jnp.where(low, pair, zero), jnp.where(low, zero, pair)], axis=0)


def attention_kernel(
    capacity,
    experts,
    picks_ref,
    ranks_ref,
    tokens_ref,
    gain_one_ref,
    shift_one_ref,
    query_w_ref,
    key_w_ref,
    value_w_ref,
    out_w_ref,
    gain_two_ref,
    shift_two_ref,
    target_ref,
    count_ref,
    resid_ref,
    normed_ref,
    query_ref,
    key_ref,
    value_ref,
    weight_ref,
    mixed_ref,
    sent_ref,
    spread_ref,
):
    count, width = tokens_ref.shape
    route(capacity, experts, picks_ref, ranks_ref, spread_ref, target_ref, count_ref)
    target_ref.flush()
    count_ref.flush()
    inputs = tokens_ref[...].astype(F32)
    hat, _ = norm_rows(inputs)
    normed_ref[...] = (hat * gain_one_ref[...] + shift_one_ref[...]).astype(BF16)
    normed_ref.flush()
    normed = normed_ref[...]
    scale = 1.0 / math.sqrt(width // HEADS)
    query_ref[...] = (dot(normed, query_w_ref[...]).astype(BF16).astype(F32) * scale).astype(BF16)
    query_ref.flush()
    key_ref[...] = dot(normed, key_w_ref[...]).astype(BF16)
    key_ref.flush()
    value_ref[...] = dot(normed, value_w_ref[...]).astype(BF16)
    value_ref.flush()
    pairs = HEADS // 2
    wide = width // pairs
    block = 2 * PATCHES
    low = head_masks(wide)
    row_image = (lax.broadcasted_iota(jnp.int32, (2 * block, block), 0) % block) // PATCHES
    column_image = lax.broadcasted_iota(jnp.int32, (2 * block, block), 1) // PATCHES
    bias = jnp.where(row_image == column_image, 0.0, -1e30)
    together = 1
    cells = [(item, pair) for item in range(count // block) for pair in range(pairs)]
    for start in range(0, len(cells), together):
        work = []
        for item, pair in cells[start : start + together]:
            rows = slice(item * block, (item + 1) * block)
            lanes = slice(pair * wide, (pair + 1) * wide)
            scores = dot_nt(stack_heads(query_ref[rows, lanes], low), key_ref[rows, lanes]) + bias
            work.append((rows, lanes, scores))
        tops = [jnp.max(scores, axis=-1, keepdims=True) for _, _, scores in work]
        powers = [jnp.exp(scores - top) for (_, _, scores), top in zip(work, tops)]
        totals = [jnp.sum(power, axis=-1, keepdims=True) for power in powers]
        lows = [(power / total).astype(BF16) for power, total in zip(powers, totals)]
        for (item, pair), weights in zip(cells[start : start + together], lows):
            weight_ref[item, pair] = weights
        for (rows, lanes, _), weights in zip(work, lows):
            mixed = dot(weights, value_ref[rows, lanes])
            mixed_ref[rows, lanes] = jnp.where(low, mixed[:block], mixed[block:]).astype(BF16)
    weight_ref.flush()
    mixed_ref.flush()
    resid = inputs + dot(mixed_ref[...], out_w_ref[...])
    resid_ref[...] = resid
    resid_ref.flush()
    hat, _ = norm_rows(resid)
    second = (hat * gain_two_ref[...] + shift_two_ref[...]).astype(BF16)
    sent_ref[...] = dot(spread_ref[...], second).astype(BF16)


def dispatch_kernel(target_ref, given_ref, sent_ref):
    sent_ref[...] = dot_tn(one_hot_rows(target_ref, sent_ref.shape[0]), given_ref[...]).astype(BF16)


def forward_kernel(experts, tile, me_ref, rows_ref, router_ref, up_bias_ref, *refs):
    ups = refs[:-4]
    hidden_ref, slope_ref, gate_ref, gates_ref = refs[-4:]
    total = rows_ref.shape[0]
    chunk = total // 4
    root = math.sqrt(2.0 / math.pi)
    rows = rows_ref[...]
    lane = lax.broadcasted_iota(jnp.int32, (total, LANES), 1)
    logits = jnp.where(lane < experts, dot_nt(rows, router_ref[...]), -1e30)
    powers = jnp.exp(logits - jnp.max(logits, axis=-1, keepdims=True))
    gates = powers / jnp.sum(powers, axis=-1, keepdims=True)
    gates_ref[...] = gates
    gates_ref.flush()
    gate = jnp.sum(jnp.where(lane == me_ref[0], gates, 0.0), axis=-1, keepdims=True)
    gate_ref[...] = jnp.broadcast_to(gate, (total, LANES))
    gate_ref.flush()
    for step, up_ref in enumerate(ups):
        lanes = slice(step * tile, (step + 1) * tile)
        for start in range(0, total, chunk):
            at = slice(start, start + chunk)
            inner = dot(rows[at], up_ref[...]) + up_bias_ref[:, lanes]
            square = inner * inner
            half = 0.5 + 0.5 * jnp.tanh(inner * (root + (root * 0.044715) * square))
            hidden = inner * half
            slope = half + (hidden - hidden * half) * (2.0 * root + (6.0 * root * 0.044715) * square)
            hidden_ref[at, lanes] = hidden.astype(BF16)
            slope_ref[at, lanes] = slope.astype(BF16)
        hidden_ref.flush(slice(None), lanes)
        slope_ref.flush(slice(None), lanes)


def produce_kernel(hidden_ref, down_ref, down_bias_ref, gate_ref, out_ref, *refs):
    parts, total_s = refs[:-1], refs[-1]
    step = pl.program_id(0)
    made = dot(hidden_ref[...], down_ref[...])

    @pl.when(step == 0)
    def _():
        total_s[...] = made

    @pl.when(step > 0)
    def _():
        total_s[...] += made

    @pl.when(step == pl.num_programs(0) - 1)
    def _():
        produced = (total_s[...] + down_bias_ref[...]).astype(BF16)
        out_ref[...] = produced
        size = parts[0].shape[1]
        gate = jnp.concatenate([gate_ref[...]] * (size // LANES), axis=1)
        for at, ref in enumerate(parts):
            ref[...] = (produced[:, at * size : (at + 1) * size].astype(F32) * gate).astype(BF16)


def expert_kernel(experts, tile, me_ref, grad_ref, *refs):
    steps = (len(refs) - 7) // 3
    gate_ref, produced_ref, gates_ref, router_ref = refs[1], *refs[3:6]
    pairs = [(refs[0], refs[2])] + [refs[at : at + 2] for at in range(6, 2 * steps + 4, 2)]
    downs, slopes = zip(*pairs)
    ups = refs[2 * steps + 4 : 3 * steps + 4]
    inner_grad_ref, rows_grad_ref, logit_grad_ref = refs[3 * steps + 4 :]
    total, width = grad_ref.shape
    for step in range(steps):
        lanes = slice(step * tile, (step + 1) * tile)
        made = dot_nt(grad_ref[...], downs[step][...])
        gate = jnp.concatenate([gate_ref[...]] * (tile // LANES), axis=1)
        made = made * gate * slopes[step][...].astype(F32)
        inner_grad_ref[:, lanes] = made.astype(BF16)
        inner_grad_ref.flush(slice(None), lanes)
        if step == 0:
            lane = lax.broadcasted_iota(jnp.int32, (total, LANES), 1)
            product = grad_ref[...].astype(F32) * produced_ref[...].astype(F32)
            pair_grad = jnp.sum(product, axis=-1, keepdims=True)
            own = jnp.where(lane == me_ref[0], 1.0, 0.0)
            logit_grad = (gates_ref[...] * (own - gate_ref[...]) * pair_grad).astype(BF16)
            logit_grad_ref[...] = logit_grad
            logit_grad_ref.flush()
    made = dot(logit_grad, router_ref[...])
    for step in range(steps):
        made = made + dot_nt(inner_grad_ref[:, step * tile : (step + 1) * tile], ups[step][...])
    rows_grad_ref[...] = made.astype(BF16)


def weight_kernel(sets, again, *refs):
    groups, refs = [refs[at * 5 : at * 5 + 5] for at in range(sets)], refs[5 * sets :]
    earlier, refs = refs[:again], refs[again:]
    extra_ref, out_ref, refs = refs[0], refs[1], refs[2:]
    router_refs, gated_s, inner_grad_s = refs[:-2], refs[-2], refs[-1]
    total, width = groups[0][0].shape

    @pl.when(pl.program_id(0) == 0)
    def _():
        for at, some in enumerate(groups):
            gate = jnp.concatenate([some[2][...]] * (width // LANES), axis=1)
            gated_s[at] = (gate * some[1][...].astype(F32)).astype(BF16)
        if router_refs:
            router_refs[0][...] = dot_tn(extra_ref[...], groups[0][0][...])[: router_refs[0].shape[0]]

    ups, downs, up_biases, down_biases = [], [], [], []
    for at, (rows_ref, grad_ref, gate_ref, hidden_ref, inner_grad_ref) in enumerate(groups):
        if again:
            slope_ref, inner_grad_ref = inner_grad_ref, inner_grad_s
            gate = jnp.concatenate([gate_ref[...]] * (width // LANES), axis=1)
            made = dot_nt(grad_ref[...], extra_ref[...]) * gate * slope_ref[...].astype(F32)
            inner_grad_s[...] = made.astype(BF16)
        inner_grad = inner_grad_ref[...]
        ups.append(dot_tn(rows_ref[...], inner_grad))
        downs.append(dot_tn(hidden_ref[...], gated_s[at]))
        up_biases.append(jnp.sum(inner_grad.astype(F32), axis=0, keepdims=True))
        down_biases.append(jnp.sum(gated_s[at].astype(F32), axis=0, keepdims=True))

    def put(some, parts):
        made = sum(parts[1:], parts[0]).astype(BF16)
        if again:
            made = (made.astype(F32) + earlier[0][0, some, :].astype(F32)).astype(BF16)
        out_ref[0, some, :] = made

    put(slice(0, width), ups)
    put(slice(width, 2 * width), downs)
    row = lax.broadcasted_iota(jnp.int32, (16, width), 0)
    small = jnp.where(row == 0, sum(up_biases[1:], up_biases[0]), sum(down_biases[1:], down_biases[0]))
    put(slice(2 * width, None), [small])


def finish_experts_kernel(*refs):
    parts, (up_ref, up_bias_ref, down_ref, down_bias_ref) = refs[:2], refs[-4:]
    tall = up_ref.shape[0]

    def total(some):
        return sum_in_tree([ref[0, some, :].astype(F32) for ref in parts])

    up_ref[...] = total(slice(0, tall))
    down_ref[...] = total(slice(tall, 2 * tall))
    small = total(slice(2 * tall, None))
    up_bias_ref[...] = small[0:1]
    down_bias_ref[...] = small[1:2]


def one_hot_rows(target_ref, slots_all):
    count = target_ref.shape[0]
    lane = lax.broadcasted_iota(jnp.int32, (64, slots_all), 1).astype(F32)
    pieces = []
    for start in range(0, count, 64):
        one = target_ref[start : start + 64, 0:1]
        two = target_ref[start : start + 64, 1:2]
        pieces.append(jnp.where((lane == one) | (lane == two), 1.0, 0.0).astype(BF16))
    return jnp.concatenate(pieces, axis=0)


def combine_kernel(target_ref, resid_ref, *refs):
    parts, out_ref = refs[:-1], refs[-1]
    picked = one_hot_rows(target_ref, parts[0].shape[0])
    size = parts[0].shape[1]
    for at, ref in enumerate(parts):
        lanes = slice(at * size, (at + 1) * size)
        out_ref[:, lanes] = (resid_ref[:, lanes] + dot(picked, ref[...])).astype(BF16)


def backward_kernel(
    experts,
    core_ref,
    back_ref,
    target_ref,
    resid_ref,
    gain_two_ref,
    grad_ref,
    mixed_ref,
    out_w_ref,
    value_ref,
    query_ref,
    weight_ref,
    key_ref,
    normed_ref,
    query_w_ref,
    key_w_ref,
    value_w_ref,
    tokens_ref,
    gain_one_ref,
    count_ref,
    router_grad_ref,
    keep_ref,
    send_ref,
    tokens_grad_ref,
    queries_s,
    keys_s,
    values_s,
    mixed_grad_s,
    resid_grad_s,
):
    count, width = grad_ref.shape
    picked = one_hot_rows(target_ref, back_ref.shape[0])
    second_grad = dot(picked, back_ref[...])
    hat, rate = norm_rows(resid_ref[...])
    gain_two_grad = jnp.sum(second_grad * hat, axis=0, keepdims=True)
    shift_two_grad = jnp.sum(second_grad, axis=0, keepdims=True)
    resid_grad_s[...] = grad_ref[...].astype(F32) + norm_back(hat, rate, gain_two_ref[...], second_grad)
    branch = resid_grad_s[...].astype(BF16)
    half = width // 2
    first = core_ref[0] == 0

    def put(at, value):
        value = value.astype(BF16)
        keep_ref[at * half : (at + 1) * half, :] = jnp.where(first, value[:half], value[half:])
        send_ref[at * half : (at + 1) * half, :] = jnp.where(first, value[half:], value[:half])
        keep_ref.flush(slice(at * half, (at + 1) * half))

    put(3, dot_tn(mixed_ref[...], branch))
    mixed_grad_s[...] = dot_nt(branch, out_w_ref[...]).astype(BF16)
    pairs = HEADS // 2
    wide = width // pairs
    block = 2 * PATCHES
    scale = 1.0 / math.sqrt(width // HEADS)
    low = head_masks(wide)
    together = 8
    cells = [(item, pair) for item in range(count // block) for pair in range(pairs)]
    for start in range(0, len(cells), together):
        work = []
        for item, pair in cells[start : start + together]:
            rows = slice(item * block, (item + 1) * block)
            lanes = slice(pair * wide, (pair + 1) * wide)
            mixed_stack = stack_heads(mixed_grad_s[rows, lanes], low)
            weights = weight_ref[item, pair]
            work.append((rows, lanes, mixed_stack, weights, dot_nt(mixed_stack, value_ref[rows, lanes])))
        score_grads = []
        for rows, lanes, mixed_stack, weights, weight_grad in work:
            product = weights.astype(F32) * weight_grad
            score_grad = product - weights.astype(F32) * jnp.sum(product, axis=-1, keepdims=True)
            score_grads.append(score_grad.astype(BF16))
        for rows, lanes, mixed_stack, weights, _ in work:
            values_s[rows, lanes] = dot_tn(weights, mixed_stack).astype(BF16)
        for (rows, lanes, *_), score_grad in zip(work, score_grads):
            made = dot(score_grad, key_ref[rows, lanes]) * scale
            queries_s[rows, lanes] = jnp.where(low, made[:block], made[block:]).astype(BF16)
        for (rows, lanes, *_), score_grad in zip(work, score_grads):
            keys_s[rows, lanes] = dot_tn(score_grad, stack_heads(query_ref[rows, lanes], low)).astype(BF16)
    normed = normed_ref[...]
    put(0, dot_tn(normed, queries_s[...]))
    put(1, dot_tn(normed, keys_s[...]))
    put(2, dot_tn(normed, values_s[...]))
    normed_grad = (
        dot_nt(queries_s[...], query_w_ref[...])
        + dot_nt(keys_s[...], key_w_ref[...])
        + dot_nt(values_s[...], value_w_ref[...])
    )
    hat, rate = norm_rows(tokens_ref[...].astype(F32))
    gain_one_grad = jnp.sum(normed_grad * hat, axis=0, keepdims=True)
    shift_one_grad = jnp.sum(normed_grad, axis=0, keepdims=True)
    tokens_grad_ref[...] = (resid_grad_s[...] + norm_back(hat, rate, gain_one_ref[...], normed_grad)).astype(BF16)
    tokens_grad_ref.flush()
    digits = []
    for kind in range(2):
        value = count_ref[kind : kind + 1, :]
        high = jnp.floor(value * (1.0 / 128.0))
        digits.append(jnp.concatenate([value - 128.0 * high, high] + [jnp.zeros_like(value)] * (width // LANES - 2), axis=1))
    extra = keep_ref.shape[0] - 4 * half
    small = [gain_one_grad, shift_one_grad, gain_two_grad, shift_two_grad] + digits + [router_grad_ref[:experts, :]]
    small = jnp.concatenate(small + [jnp.zeros((extra - 6 - experts, width), F32)], axis=0).astype(BF16)
    keep_ref[4 * half :, :] = small
    send_ref[4 * half :, :] = small
    keep_ref.flush(slice(4 * half, None))


def carry_digits(total):
    row = lax.broadcasted_iota(jnp.int32, (total.shape[0], LANES), 0)
    one, two, three = (total[:, at * LANES : (at + 1) * LANES] for at in range(3))
    over = jnp.floor(one * (1.0 / 128.0))
    two_full = two + over
    over_two = jnp.floor(two_full * (1.0 / 128.0))
    parts = [one - 128.0 * over, two_full - 128.0 * over_two, three + over_two]
    is_count = (row == 4) | (row == 5)
    parts = [jnp.where(is_count, part, total[:, at * LANES : (at + 1) * LANES]) for at, part in enumerate(parts)]
    return jnp.concatenate(parts + [total[:, 3 * LANES :]], axis=1)


def sum_in_tree(values):
    while len(values) > 1:
        values = [values[at] + values[at + 1] for at in range(0, len(values), 2)]
    return values[0]


def share_kernel(given, pieces, *refs):
    index_ref, arrived, made = refs[0], refs[1 : 1 + given], refs[1 + given :]
    small_rows = (pieces * made[0].shape[0] - arrived[0].shape[0]) // (pieces - 1)
    size = made[0].shape[0] - small_rows
    top = pieces * size
    small = carry_digits(sum_in_tree([ref[top:, :].astype(F32) for ref in arrived])).astype(BF16)
    for away in range(pieces):
        at = pl.ds(pl.multiple_of((index_ref[0] ^ away) * size, size), size)
        made[away][:size, :] = sum_in_tree([ref[at, :].astype(F32) for ref in arrived]).astype(BF16)
        made[away][size:, :] = small


def copy_kernel(given_ref, made_ref, arrival):
    copy = pltpu.make_async_copy(given_ref, made_ref, arrival)
    copy.start()
    copy.wait()


def pass_kernel(given_ref, same_ref):
    pass


def gather_kernel(*refs):
    arrived, out_ref = refs[:-1], refs[-1]
    size = arrived[0].shape[0]
    for at, ref in enumerate(arrived):
        out_ref[at * size : (at + 1) * size, :] = ref[...]


def last_kernel(given, *refs):
    arrived, chunk_ref, small_ref = refs[:given], refs[given], refs[given + 1]
    size = chunk_ref.shape[0]
    chunk_ref[...] = sum_in_tree([ref[:size, :].astype(F32) for ref in arrived]).astype(BF16)
    small_ref[...] = carry_digits(sum_in_tree([ref[size:, :].astype(F32) for ref in arrived])).astype(BF16)


def finish_shared_kernel(experts, index_ref, *refs):
    own, others, small_ref, outs = refs[:4], refs[4:8], refs[8], refs[9:]
    vector_refs, router_ref, count_ref = outs[4:8], outs[8], outs[9]
    core, place, inner_place = index_ref[0], index_ref[1], index_ref[2]
    half = outs[0].shape[1] // 2
    size = half // 4
    for pieces, side in ((own, core), (others, 1 - core)):
        for away, piece in enumerate(pieces):
            for at in range(4):

                @pl.when((place ^ away) == at)
                def _(piece=piece, side=side, out=outs[at]):
                    for part in range(4):
                        start = pl.multiple_of((inner_place ^ part) * size, size)
                        row = pl.multiple_of(side * half + part * size, size)
                        out[pl.ds(row, size), :] = piece[pl.ds(start, size), :].astype(F32)

    small = small_ref[...].astype(F32)
    for at, ref in enumerate(vector_refs):
        ref[...] = small[at : at + 1, :]
    router_ref[...] = small[6 : 6 + experts, :]
    value = small[4:6, :LANES] + 128.0 * small[4:6, LANES : 2 * LANES] + 16384.0 * small[4:6, 2 * LANES : 3 * LANES]
    count_ref[...] = value[:, :experts].astype(jnp.int32)


def solution(mesh):
    narrow, wide = mesh.shape["narrow"], mesh.shape["wide"]

    def hop(value, narrow_bits, wide_bits):
        if wide_bits == 0:
            return lax.ppermute(value, "narrow", [(i, i ^ narrow_bits) for i in range(narrow)])
        if narrow_bits == 0:
            return lax.ppermute(value, "wide", [(i, i ^ wide_bits) for i in range(wide)])
        pairs = [
            (i * wide + j, (i ^ narrow_bits) * wide + (j ^ wide_bits)) for i in range(narrow) for j in range(wide)
        ]
        return lax.ppermute(value, ("narrow", "wide"), pairs)

    def body(
        tokens,
        gain_one,
        shift_one,
        query_w,
        key_w,
        value_w,
        out_w,
        gain_two,
        shift_two,
        router_w,
        up_w,
        up_bias,
        down_w,
        down_bias,
        picks,
        ranks,
        out_grad,
    ):
        count, width = tokens.shape
        experts = router_w.shape[1]
        capacity = ((21 * 2 * count + 20 * experts - 1) // (20 * experts) + 7) // 8 * 8
        slots_all = experts * capacity
        hidden_width = up_w.shape[2]
        half = width // 2
        pairs = HEADS // 2
        blocks = count // (2 * PATCHES)
        extra = (6 + experts + 15) // 16 * 16
        tile = width
        steps = hidden_width // tile
        narrow_at, wide_at = lax.axis_index("narrow"), lax.axis_index("wide")
        core = (narrow_at & 1)[None].astype(jnp.int32)
        place = (((narrow_at >> 1) & 1) * 2 + (wide_at & 1))[None].astype(jnp.int32)
        inner_place = ((wide_at >> 1) & 3)[None].astype(jnp.int32)
        gain_one, shift_one, gain_two, shift_two = (v[None, :] for v in (gain_one, shift_one, gain_two, shift_two))
        router_t = jnp.pad(router_w.T, ((0, LANES - experts), (0, 0)))
        up_w, down_w = up_w[0], down_w[0]

        def exchange(value):
            return lax.all_to_all(value, "wide", split_axis=0, concat_axis=0, tiled=True)

        token_rows = shape((count, width), BF16)
        rows_shape = shape((slots_all, width), BF16)
        lanes_shape = shape((slots_all, LANES), F32)
        narrow_far = far((count, width), BF16)
        target, counts, resid, normed, queries, keys, values, weights, mixed, sent = fuse(
            functools.partial(attention_kernel, capacity, experts),
            (picks.T, ranks.T, tokens, gain_one, shift_one, query_w, key_w, value_w, out_w, gain_two, shift_two),
            (
                far((count, 8), F32),
                far((8, LANES), F32),
                far((count, width), F32),
                narrow_far,
                narrow_far,
                narrow_far,
                narrow_far,
                far((blocks, pairs, 4 * PATCHES, 2 * PATCHES), BF16),
                narrow_far,
                held((slots_all, width), BF16),
            ),
            32,
            10,
            "attention",
            (pltpu.VMEM((slots_all, count), BF16),),
        )
        rows = exchange(sent)
        (grad_sent,) = run(dispatch_kernel, (target, out_grad), (rows_shape,), 16, 1, "dispatch", after=(Held(sent),))
        grad_rows = exchange(grad_sent)

        whole = pl.BlockSpec((slots_all, width), lambda f: (0, 0))
        lanes_whole = pl.BlockSpec((slots_all, LANES), lambda f: (0, 0))
        columns = pl.BlockSpec((slots_all, tile), lambda f: (0, f))
        down_spec = pl.BlockSpec((tile, width), lambda f: (f, 0))
        down_bias_spec = pl.BlockSpec((1, width), lambda f: (0, 0))
        payload = 2 * width + 16
        me = wide_at[None].astype(jnp.int32)
        rows = Held(rows)

        def forward(rows, us, after=()):
            return fuse(
                functools.partial(forward_kernel, experts, tile),
                (me, rows, router_t, up_bias) + tuple(Part(up_w, tile, at) for at in range(steps)),
                (far((slots_all, hidden_width), BF16),) * 2 + (far((slots_all, LANES), F32),) * 2,
                32,
                us,
                "forward",
                after=after,
            )

        hidden, slope, gate, gates = forward(rows, 0.01)
        produced, gated = run(
            produce_kernel,
            (hidden, down_w, down_bias, gate),
            (rows_shape,) * 2,
            32,
            0.01,
            "produce",
            (pltpu.VMEM((slots_all, width), F32),),
            grid=(steps,),
            in_specs=(columns, down_spec, down_bias_spec, lanes_whole),
            out_specs=(whole,) * 2,
        )
        grad_rows = Held(grad_rows)

        def pair_of(at):
            return Part(down_w, tile, at, rows=True), Part(slope, tile, at)

        down_first, slope_first = pair_of(0)
        later = [part for at in range(1, steps) for part in pair_of(at)] + [Part(up_w, tile, at) for at in range(steps)]
        rows_others = [hop(rows.value, bits, 0) for bits in range(2, narrow, 2)]
        inner_grad, rows_grad, logit_grad = fuse(
            functools.partial(expert_kernel, experts, tile),
            (me, grad_rows, down_first, gate, slope_first, produced, gates, router_t, *later),
            (far((slots_all, hidden_width), BF16), held((slots_all, width), BF16), far((slots_all, LANES), BF16)),
            40,
            0.01,
            "experts",
            after=[Held(one) for one in rows_others],
        )
        back = exchange(rows_grad)

        def payload_of(number):
            return shape((number, payload, width), BF16)

        payload_spec = pl.BlockSpec((1, payload, width), lambda f: (f, 0, 0))
        router_spec = pl.BlockSpec((experts, width), lambda f: (0, 0))
        (grad_later,) = run(
            copy_kernel,
            (grad_rows,),
            (rows_shape,),
            4,
            0.01,
            "copy_rows",
            (pltpu.SemaphoreType.DMA,),
            in_specs=(pl.BlockSpec(memory_space=pl.ANY),),
            out_specs=(pl.BlockSpec(memory_space=pltpu.HBM),),
            after=(produced,),
        )

        def held_back(value, after, space=pltpu.HBM):
            return run(
                pass_kernel,
                (value if space == pltpu.HBM else Held(value),),
                (value,),
                1,
                0.01,
                "pass",
                in_specs=(pl.BlockSpec(memory_space=space),),
                out_specs=(pl.BlockSpec(memory_space=space),),
                after=after,
                free=space != pltpu.HBM,
                input_output_aliases={0: 0},
            )[0]

        sets = []
        for bits, rows_of in zip(range(2, narrow, 2), rows_others):
            grad_of = hop(grad_later, bits, 0)
            hidden_of, slope_of, gate_of, _ = forward(rows_of, 0.01, (logit_grad,))
            sets.append((rows_of, grad_of, gate_of, hidden_of, slope_of))

        def weight_part(again, sets, extra, extra_spec, earlier=(), after=()):
            return run(
                functools.partial(weight_kernel, len(sets), int(again)),
                (*(item for one in sets for item in one), *earlier, extra),
                (payload_of(steps),) + (shape((experts, width), F32),) * (not again),
                48,
                0.01,
                "expert_weights",
                (
                    pltpu.VMEM((len(sets), slots_all, width), BF16),
                    pltpu.VMEM((slots_all, tile), BF16),
                ),
                grid=(steps,),
                in_specs=(
                    *(spec for _ in sets for spec in (whole, whole, lanes_whole, columns, columns)),
                    *(payload_spec for _ in earlier),
                    extra_spec,
                ),
                out_specs=(payload_spec,) + (router_spec,) * (not again),
                after=after,
            )

        def finish_experts(start, number, parts, earlier, after=()):
            spec = lambda dims, index: pl.BlockSpec(dims, lambda f: index(start + f))
            return run(
                finish_experts_kernel,
                (*parts, *earlier),
                (
                    shape((width, hidden_width), F32),
                    shape((1, hidden_width), F32),
                    shape((hidden_width, width), F32),
                    shape((1, width), F32),
                ),
                32,
                0.01,
                "finish_experts",
                grid=(number,),
                in_specs=[pl.BlockSpec((1, payload, width), lambda f: (start + f, 0, 0))] * 2
                + [pl.BlockSpec(memory_space=pltpu.HBM)] * len(earlier),
                out_specs=(
                    spec((width, tile), lambda f: (0, f)),
                    spec((1, tile), lambda f: (0, f)),
                    spec((tile, width), lambda f: (f, 0)),
                    down_bias_spec,
                ),
                after=after,
                input_output_aliases={2 + at: at for at in range(len(earlier))},
            )

        own_sum, router_part = weight_part(
            False, [(rows, grad_rows, gate, hidden, inner_grad)], logit_grad, lanes_whole, (), [one[4] for one in sets]
        )
        produced_back = exchange(held_back(gated, (own_sum,)))
        tall = 4 * half + extra
        keep, send, tokens_grad = fuse(
            functools.partial(backward_kernel, experts),
            (
                core,
                Held(back),
                target,
                resid,
                gain_two,
                out_grad,
                mixed,
                out_w,
                values,
                queries,
                weights,
                keys,
                normed,
                query_w,
                key_w,
                value_w,
                tokens,
                gain_one,
                counts,
                router_part,
            ),
            (far((tall, width), BF16), held((tall, width), BF16), far((count, width), BF16)),
            32,
            0.01,
            "backward",
            [pltpu.VMEM((count, width), BF16)] * 4 + [pltpu.VMEM((count, width), F32)],
            after=[own_sum] + [Held(one[1]) for one in sets],
        )

        def share(index, arrived, after=()):
            size = (arrived[0].shape[0] - extra) // 4
            return run(
                functools.partial(share_kernel, len(arrived), 4),
                (index, arrived[0] if size == half else Held(arrived[0]), *map(Held, arrived[1:])),
                (shape((size + extra, width), BF16),) * 4,
                16,
                0.05,
                "share",
                after=after,
                free=True,
            )

        def last(arrived, after=()):
            return run(
                functools.partial(last_kernel, len(arrived)),
                tuple(map(Held, arrived)),
                (shape((half // 4, width), BF16), shape((extra, width), BF16)),
                16,
                0.05,
                "last",
                after=after,
                free=True,
            )

        def gather(arrived, after=()):
            rows_in = sum(value.shape[0] for value in arrived)
            return run(
                gather_kernel,
                tuple(map(Held, arrived)),
                (shape((rows_in, width), BF16),),
                16,
                0.05,
                "gather",
                after=after,
                free=True,
            )[0]

        def spread_out(parts, bits):
            return [parts[0]] + [hop(part, *bit) for part, bit in zip(parts[1:], bits[1:])]

        places = ((0, 0), (0, 1), (2, 0), (2, 1))
        inner_places = ((0, 0), (0, 2), (0, 4), (0, 6))
        parts = share(place, [keep, hop(send, 1, 0)])
        (far_sum,) = weight_part(True, sets, down_w, down_spec, (own_sum,), (Held(parts[0]),))
        parts = share(inner_place, spread_out(parts, places), (far_sum, Held(produced_back)))
        far_sum = held_back(far_sum, (Held(parts[0]),))
        parts = spread_out(parts, inner_places)
        (block_out,) = run(
            combine_kernel, (target, resid, Held(produced_back)), (token_rows,), 16, 0.01, "combine"
        )
        chunk, small = last(parts, (block_out,))
        others = [(bit, 0) for bit in (4, 8, 16, 32, 64) if bit < narrow]
        others += [(0, bit) for bit in (8, 16, 32, 64) if bit < wide]
        for bits in others:
            joined = jnp.concatenate([chunk, small], axis=0)
            chunk, small = last([joined, hop(joined, *bits)])
        sums = (far_sum, Held(hop(far_sum, 1, 0)))
        finished = finish_experts(0, steps // 2, sums, (), (Held(chunk),))
        chunk = gather(spread_out([chunk] * 4, inner_places), (finished[0],))
        pieces = spread_out([chunk] * 4, places)
        finished = finish_experts(steps // 2, steps - steps // 2, sums, finished, (Held(chunk),))
        pieces[3] = held_back(pieces[3], finished[:1], pl.ANY)
        up_grad, up_bias_grad, down_grad, down_bias_grad = finished
        outs = run(
            functools.partial(finish_shared_kernel, experts),
            (
                jnp.concatenate([core, place, inner_place]),
                *map(Held, pieces),
                *(Held(hop(piece, 1, 0)) for piece in pieces),
                Held(small),
            ),
            (shape((width, width), F32),) * 4
            + (shape((1, width), F32),) * 4
            + (shape((experts, width), F32), shape((2, experts), jnp.int32)),
            32,
            3,
            "finish_shared",
        )
        query_grad, key_grad, value_grad, out_w_grad, g_one, s_one, g_two, s_two, router_grad, tallies = outs
        return (
            block_out,
            tokens_grad,
            g_one[0],
            s_one[0],
            query_grad,
            key_grad,
            value_grad,
            out_w_grad,
            g_two[0],
            s_two[0],
            router_grad.T,
            up_grad[None],
            up_bias_grad,
            down_grad[None],
            down_bias_grad,
            tallies.T,
        )

    tokens_spec = P(("narrow", "wide"), None)
    in_specs = (
        (tokens_spec,)
        + (P(),) * 9
        + (P("wide", None, None), P("wide", None), P("wide", None, None), P("wide", None))
        + (tokens_spec,) * 3
    )
    out_specs = (
        (tokens_spec,) * 2
        + (P(),) * 9
        + (P("wide", None, None), P("wide", None), P("wide", None, None), P("wide", None))
        + (P(),)
    )
    return jax.shard_map(body, mesh=mesh, in_specs=in_specs, out_specs=out_specs, check_vma=False)
```
